512 devices in a mesh: grp: 4 (over z_hi, core), gx: 32 (over x, y), gy: 4 (over z_lo).
Axes of the slice: x: 4, y: 8, z: 8 (z_hi: 2, z_lo: 4; z = z_hi * 4 + z_lo), core: 2. Of those that a mesh axis runs over, the one named last changes fastest.
Arguments:
- slot_field: float32 [4, 2, 1536, 512], P('grp', None, 'gx', 'gy'), may hold values from -6 to 6
- solid: int32 [2, 1536, 512], P(None, 'gx', 'gy'), may hold values 0 or 1
- lift_weight: bfloat16 [3, 64], replicated, may hold values from -3.5 to 3.5
- spectral_weight: bfloat16 [2048, 128], replicated, may hold values from -1.5 to 1.5
- mix_weight: bfloat16 [64, 64], replicated, may hold values from -0.75 to 0.75
- project_weight: bfloat16 [64, 3], replicated, may hold values from -0.75 to 0.75
- mode_index: int32 [32], replicated, may hold values from 0 to 47, as said below
Outputs:
- new_velocity: float32 [3, 2, 1536, 512], P(None, None, 'gx', 'gy')
- spectral_grad: float32 [2048, 128], P(('grp', 'gx', 'gy'))
- mix_grad: float32 [64, 64], replicated
The draws below stay inside these ranges and needn't reach their ends.
Inputs may be any that keep to these rules, and one draw needn't show every extreme that they name: `mode_index`: 32 distinct values in ascending order; 0 and 47 are always among them.
All inputs are finite; a program needn't handle non-finite values. No bound on the sum of `solid` on one device may be relied on, other than what follows from the above.
Results may differ from the reference program's by a relative error of at most 0.0013.
Values may be sent and summed in bfloat16 or wider, within the bound.
No kernel may reach another device: no remote copies, remote signals or barrier semaphores. Data moves between devices by JAX's collectives and lax.ppermute only.
A program may use at most 64 MiB of HBM per device.

```python
import math
import jax
import jax.numpy as jnp
from jax import lax

WIDTH = 64
MODES = 32
MODE_RANGE = 48
NX = 1536
NY = 512
NZ = 2
N_GRP = 4


def draw_mode_index(key, part):
    key = jax.random.fold_in(key, 7)
    inner = (jax.random.permutation(key, MODE_RANGE - 2) + 1).astype(jnp.int32)
    chosen = jnp.concatenate([jnp.zeros((1,), jnp.int32), inner[:MODES - 2], jnp.full((1,), MODE_RANGE - 1, jnp.int32)])
    return jnp.sort(chosen)


def set_ends(array, key, least, top_value):
    place = [jax.random.randint(jax.random.fold_in(key, axis), (), 0, length) for axis, length in enumerate(array.shape)]
    main_axis = array.shape.index(max(array.shape))
    next_to = place[:main_axis] + [(place[main_axis] + 1) % array.shape[main_axis]] + place[main_axis + 1:]
    return array.at[tuple(place)].set(least).at[tuple(next_to)].set(top_value)


def shard_levels(stream_key, extent, shards, low, high):
    loudness, own = 1.0, jax.random.fold_in(stream_key, 6)
    for dim, shards_of in shards:
        steps = jnp.exp(jax.random.uniform(jax.random.fold_in(own, dim), (shards_of,), jnp.float32, low / len(shards), high / len(shards)))
        loudness = loudness * jnp.repeat(steps, extent[dim] // shards_of).reshape([-1 if axis == dim else 1 for axis in range(len(extent))])
    return loudness


def centred(stream_key, extent, spread, most, shards=(), kind=jnp.bfloat16):
    factor_of = shard_levels(stream_key, extent, shards, -0.22, 0.18) if shards else 1.0
    drawn = jax.random.normal(stream_key, extent, jnp.float32) * spread * factor_of
    return jnp.minimum(jnp.maximum(drawn, -most), most).astype(kind)


def setup_inputs(seed: int = 0) -> dict:
    key_list = jax.random.split(jax.random.key(seed), 8)
    slot_field = centred(key_list[0], (N_GRP, NZ, NX, NY), 1.0, 6.0, ((0, 4), (2, 32), (3, 4)), jnp.float32)
    solid = set_ends((jax.random.randint(key_list[1], (NZ, NX, NY), 0, 8) < 1).astype(jnp.int32), jax.random.fold_in(key_list[1], 1), 0, 1)
    lift_weight = centred(key_list[2], (3, WIDTH), 3 ** -0.5, 3.5)
    spectral_weight = centred(key_list[3], (MODES * WIDTH, 2 * WIDTH), 0.25, 1.5)
    mix_weight = centred(key_list[4], (WIDTH, WIDTH), WIDTH ** -0.5, 0.75)
    project_weight = centred(key_list[5], (WIDTH, 3), WIDTH ** -0.5, 0.75)
    mode_index = draw_mode_index(jax.random.fold_in(key_list[7], 71), 0)
    return {"slot_field": slot_field, "solid": solid, "lift_weight": lift_weight, "spectral_weight": spectral_weight, "mix_weight": mix_weight, "project_weight": project_weight, "mode_index": mode_index}


VISCOSITY = 0.05
TIME_STEP = 0.1

def interior(source):
    return source[1:-1, 1:-1, 1:-1]

def along_x(source):
    return 0.5 * (source[1:-1, 2:, 1:-1] - source[1:-1, :-2, 1:-1])

def along_y(source):
    return 0.5 * (source[1:-1, 1:-1, 2:] - source[1:-1, 1:-1, :-2])

def along_z(source):
    return 0.5 * (source[2:, 1:-1, 1:-1] - source[:-2, 1:-1, 1:-1])

def laplace(source):
    total = source[2:, 1:-1, 1:-1] + source[:-2, 1:-1, 1:-1]
    total = total + source[1:-1, 2:, 1:-1] + source[1:-1, :-2, 1:-1]
    total = total + source[1:-1, 1:-1, 2:] + source[1:-1, 1:-1, :-2]
    return total - 6.0 * interior(source)

def section_component(padded, component, solid):
    source = padded[component]
    velocity = [interior(padded[index]) for index in range(3)]
    advect = velocity[0] * along_x(source) + velocity[1] * along_y(source) + velocity[2] * along_z(source)
    pressure = padded[3]
    press_grad = jnp.stack([along_x(pressure), along_y(pressure), along_z(pressure)])[component]
    update = interior(source) + TIME_STEP * (VISCOSITY * laplace(source) - advect - press_grad)
    return update * (1.0 - solid.astype(jnp.float32))

def spectral_table(mode_index, x_length):
    places = jnp.arange(x_length, dtype=jnp.int32)
    phases = mode_index[:, None] * places[None, :] % x_length
    angles = 2.0 * jnp.pi / x_length * phases.astype(jnp.float32)
    return jnp.concatenate([jnp.cos(angles), -jnp.sin(angles)], axis=0).astype(jnp.bfloat16)

def contract(form, left, right):
    return jnp.einsum(form, left.astype(jnp.float32), right.astype(jnp.float32))

def student_terms(line_data, dft_table, lift_weight, spectral_weight, mix_weight, project_weight, loss_scale, x_length):
    mode_count = dft_table.shape[0] // 2
    chan_count = mix_weight.shape[0]
    scale_dft = 1.0 / math.sqrt(x_length)
    old_part = line_data[:3]
    target = line_data[3:].astype(jnp.float32)
    lifted = contract('iln,ic->cln', old_part, lift_weight).astype(jnp.bfloat16)
    coeffs = (contract('cln,mn->clm', lifted, dft_table) * scale_dft).astype(jnp.bfloat16)
    real_in = coeffs[..., :mode_count]
    imag_in = coeffs[..., mode_count:]
    weights = spectral_weight.reshape(mode_count, chan_count, 2 * chan_count)
    real_w = weights[..., :chan_count]
    imag_w = weights[..., chan_count:]
    real_out = contract('clm,mco->olm', real_in, real_w) - contract('clm,mco->olm', imag_in, imag_w)
    imag_out = contract('clm,mco->olm', real_in, imag_w) + contract('clm,mco->olm', imag_in, real_w)
    mixed = jnp.concatenate([real_out, imag_out], axis=2).astype(jnp.bfloat16)
    spectral = contract('olm,mn->oln', mixed, dft_table) * (2.0 * scale_dft)
    local_term = contract('cln,co->oln', lifted, mix_weight)
    hidden = spectral + local_term
    active, gelu_back = jax.vjp(jax.nn.gelu, hidden)
    active = active.astype(jnp.bfloat16)
    predicted = contract('oln,oi->iln', active, project_weight)
    misfit = (predicted - target) * loss_scale
    back_active = jnp.einsum('iln,oi->oln', misfit, project_weight.astype(jnp.float32), precision=lax.Precision.HIGHEST)
    back_hidden = gelu_back(back_active)[0].astype(jnp.bfloat16)
    mix_part = contract('cln,oln->co', lifted, back_hidden)
    back_mixed = (contract('oln,mn->olm', back_hidden, dft_table) * (2.0 * scale_dft)).astype(jnp.bfloat16)
    back_real = back_mixed[..., :mode_count]
    back_imag = back_mixed[..., mode_count:]
    grad_real = contract('clm,olm->mco', real_in, back_real) + contract('clm,olm->mco', imag_in, back_imag)
    grad_imag = contract('clm,olm->mco', real_in, back_imag) - contract('clm,olm->mco', imag_in, back_real)
    spectral_part = jnp.concatenate([grad_real, grad_imag], axis=2).reshape(mode_count * chan_count, 2 * chan_count)
    return (spectral_part, mix_part)

def reference(slot_field, solid, lift_weight, spectral_weight, mix_weight, project_weight, mode_index):
    padded = jnp.pad(slot_field, ((0, 0), (1, 1), (1, 1), (1, 1)))
    new_velocity = jnp.stack([section_component(padded, component, solid) for component in range(3)])
    fields = jnp.concatenate([slot_field[:3], new_velocity], axis=0).astype(jnp.bfloat16)
    line_count = NZ * NY
    line_data = jnp.transpose(fields, (0, 1, 3, 2)).reshape(6, line_count, NX)
    block_rows = math.gcd(line_count, 128)
    blocks = jnp.transpose(line_data.reshape(6, line_count // block_rows, block_rows, NX), (1, 0, 2, 3))
    dft_table = spectral_table(mode_index, NX)
    loss_scale = 16.0 / math.sqrt(NX * NY * NZ)

    def scan_step(totals, line_block):
        spec_part, mix_part = student_terms(line_block, dft_table, lift_weight, spectral_weight, mix_weight, project_weight, loss_scale, NX)
        return ((totals[0] + spec_part, totals[1] + mix_part), None)
    starting = (jnp.zeros(spectral_weight.shape, jnp.float32), jnp.zeros(mix_weight.shape, jnp.float32))
    (spec_total, mix_total), _ = lax.scan(scan_step, starting, blocks)
    return (new_velocity, spec_total, mix_total)
```

```python
import math

import jax
import jax.numpy as jnp
from jax import lax
from jax.experimental import pallas as pl
from jax.experimental.pallas import tpu as pltpu
from jax.sharding import PartitionSpec as P

VISCOSITY = 0.05
TIME_STEP = 0.1
F32 = jnp.float32
BF16 = jnp.bfloat16
GELU_A = math.sqrt(2.0 / math.pi)
GELU_B = 0.044715
VMEM = pl.BlockSpec(memory_space=pltpu.VMEM)
NT = (((1,), (1,)), ((), ()))
NN = (((1,), (0,)), ((), ()))
TN = (((0,), (0,)), ((), ()))


def dot(a, b, dims):
    return lax.dot_general(a, b, dims, preferred_element_type=F32)


def iota(shape, axis):
    return lax.broadcasted_iota(jnp.int32, shape, axis)


def call(kernel, out_shape, *args, scratch=()):
    count = len(out_shape) if isinstance(out_shape, (tuple, list)) else 1
    return pl.pallas_call(
        kernel,
        out_shape=out_shape,
        in_specs=[VMEM] * len(args),
        out_specs=[VMEM] * count if isinstance(out_shape, (tuple, list)) else VMEM,
        scratch_shapes=list(scratch),
        compiler_params=pltpu.CompilerParams(vmem_limit_bytes=40 * 1024 * 1024),
    )(*args)


def edge_kernel(tile_ref, up_ref, down_ref, right_ref, left_ref):
    rows, lanes = tile_ref.shape[1:]
    same = iota((rows, lanes), 0) == iota((rows, lanes), 1)
    for z in range(2):
        tile = tile_ref[z]
        up_ref[z : z + 1, :] = tile[rows - 1 : rows, :]
        down_ref[z : z + 1, :] = tile[0:1, :]
        for ref, lane in ((right_ref, lanes - 1), (left_ref, 0)):
            column = jnp.broadcast_to(tile[:, lane : lane + 1], (rows, lanes))
            ref[z : z + 1, :] = jnp.sum(jnp.where(same, column, 0.0), axis=0, keepdims=True)


def stencil_kernel(rows, fields_ref, solid_ref, new_ref, send_ref):
    lanes = fields_ref.shape[3]
    role = lax.axis_index("grp")
    row = iota((rows, lanes), 0)
    lane = iota((rows, lanes), 1)
    same = row == lane
    centre = [[fields_ref[f, z, 0:rows, :] for z in range(2)] for f in range(4)]

    def near(f, z):
        tile = centre[f][z]
        x_up = fields_ref[f, z, 1 : rows + 1, :]
        below = fields_ref[f, z, rows + 1 : rows + 2, :]
        x_down = jnp.where(row == 0, below, pltpu.roll(tile, 1, 0))
        rims = []
        for k in (2, 3):
            line = jnp.broadcast_to(fields_ref[f, z, rows + k : rows + k + 1, :], (rows, lanes))
            rims.append(jnp.sum(jnp.where(same, line, 0.0), axis=1, keepdims=True))
        y_down = jnp.where(lane == 0, rims[0], pltpu.roll(tile, 1, 1))
        y_up = jnp.where(lane == lanes - 1, rims[1], pltpu.roll(tile, lanes - 1, 1))
        return x_up, x_down, y_up, y_down

    values = []
    for z in range(2):
        fluid = 1.0 - solid_ref[z].astype(F32)
        velocity = [centre[f][z] for f in range(3)]
        sign = 0.5 if z == 0 else -0.5
        px_up, px_down, py_up, py_down = near(3, z)
        press = (0.5 * (px_up - px_down), 0.5 * (py_up - py_down), sign * centre[3][1 - z])
        new = []
        for f in range(3):
            x_up, x_down, y_up, y_down = near(f, z)
            other = centre[f][1 - z]
            advect = (
                velocity[0] * (0.5 * (x_up - x_down))
                + velocity[1] * (0.5 * (y_up - y_down))
                + velocity[2] * (sign * other)
            )
            lap = other + x_up + x_down + y_up + y_down - 6.0 * velocity[f]
            update = velocity[f] + TIME_STEP * (VISCOSITY * lap - advect - press[f])
            new.append(update * fluid)
            new_ref[f, z] = new[f]
        parts = [part.astype(BF16) for part in velocity + new]
        values.append(jnp.concatenate(parts, axis=1))
    pad = jnp.zeros((128 - 2 * rows, 6 * lanes), BF16)
    stacked = jnp.concatenate(values + [pad], axis=0)
    count = send_ref.shape[0]
    out_row = iota((count, 6 * lanes), 0)
    column = iota((count, 6 * lanes), 1)
    wanted = (out_row & 7) * lanes + (out_row >> 3) + role * (count // 8)
    pick = jnp.where(((out_row & 7) < 6) & (column == wanted), 1.0, 0.0).astype(BF16)
    send_ref[...] = dot(pick, stacked, NT).astype(BF16)


def line_kernel(
    scale_dft, loss_scale, recv_ref, table_ref, lift_ref, mix_ref, weight_ref, proj_ref, projt_ref,
    send_ref, back_ref, coef_ref,
):
    blocks = recv_ref.shape[0]
    cells = blocks * 128
    rows = 48
    lines = jnp.concatenate([recv_ref[b] for b in range(blocks)], axis=1)
    plane = iota((64, cells), 1) & 127
    table = table_ref[...]
    zero = jnp.zeros_like(table)
    first = jnp.where(plane < rows, table, zero)
    second = jnp.where((plane >= rows) & (plane < 2 * rows), table, zero)
    both = jnp.concatenate([first, second], axis=0)
    lifted = dot(lift_ref[...], lines, NN).astype(BF16)
    coeffs = dot(both, lifted, NT) * scale_dft
    coeffs16 = coeffs.astype(BF16)
    wide = jnp.concatenate([coeffs16] * 32, axis=1)
    mode_row = iota(wide.shape, 0) & 31
    mode_col = iota(wide.shape, 1) >> 6
    wide = jnp.where(mode_row == mode_col, wide, jnp.zeros_like(wide))
    product = dot(wide, weight_ref[...], NN)
    turned = pltpu.roll(product, 64, 1)
    parts = []
    for line in range(2):
        real = slice(64 * line, 64 * line + 32)
        imag = slice(64 * line + 32, 64 * line + 64)
        parts.append(product[real] - turned[imag])
        parts.append(turned[real] + product[imag])
    mixed = jnp.concatenate(parts, axis=0)
    mixed_t = jnp.transpose(mixed)[0:64].astype(BF16)
    hidden = dot(mixed_t, both, NN) * (2.0 * scale_dft) + dot(mix_ref[...], lifted, NN)
    square = hidden * hidden
    inner = GELU_A * (hidden + GELU_B * (square * hidden))
    tanh = jnp.tanh(inner)
    half = 0.5 * (1.0 + tanh)
    active = (hidden * half).astype(BF16)
    slope = half + (0.5 * GELU_A) * hidden * (1.0 - tanh * tanh) * (1.0 + (3.0 * GELU_B) * square)
    predicted = dot(projt_ref[...], active, NN)
    target = pltpu.roll(lines.astype(F32), 5, 0)
    misfit = (predicted - target) * loss_scale
    misfit = jnp.where(iota(misfit.shape, 0) < 3, misfit, 0.0)
    high = misfit.astype(BF16)
    low = (misfit - high.astype(F32)).astype(BF16)
    proj = proj_ref[...]
    back = slope * (dot(proj, high, NN) + dot(proj, low, NN))
    back16 = back.astype(BF16)
    mix_terms = dot(lines, back16, NT)
    back_mixed = dot(both, back16, NT) * (2.0 * scale_dft)
    back_ref[...] = jnp.concatenate([back_mixed[0:64], back_mixed[64:128]], axis=1)
    coef_ref[...] = jnp.concatenate([coeffs[0:64], coeffs[64:128]], axis=1)
    mix_high = mix_terms.astype(BF16)
    mix_low = (mix_terms - mix_high.astype(F32)).astype(BF16)
    tail = jnp.concatenate([mix_high, mix_low], axis=1)
    for j in range(8):
        chunk = jnp.concatenate(
            [
                back_ref[pl.ds(j, 8, stride=8), :],
                coef_ref[pl.ds(j, 8, stride=8), :],
                tail.astype(F32),
            ],
            axis=0,
        ).astype(BF16)
        for q in range(4):
            send_ref[4 * j + q] = chunk


def grad_kernel(recv_ref, send_ref, wide_ref, grad_ref):
    quarter = lax.rem(lax.axis_index("gx"), 4)
    blocks, height = recv_ref.shape[:2]
    for b in range(blocks):
        wide_ref[b * height : (b + 1) * height, :] = recv_ref[b].astype(F32)

    def rows(k):
        return wide_ref[pl.ds(k, blocks, stride=height), :]

    for g in range(4):
        back_re, back_im, coef_re, coef_im = rows(g), rows(4 + g), rows(8 + g), rows(12 + g)
        outs = []
        for left, right in (
            ([coef_re, coef_im], [back_re, back_im]),
            ([coef_re, -coef_im], [back_im, back_re]),
        ):
            left = jnp.concatenate(left, axis=0).astype(BF16)
            right = jnp.concatenate(right, axis=0).astype(BF16)
            outs.append(dot(left, right, TN))
        real, imag = outs
        lane = iota(real.shape, 1)
        low = jnp.where(lane < 64, real, pltpu.roll(imag, 64, 1))
        high = jnp.where(lane < 64, pltpu.roll(real, 64, 1), imag)
        grad_ref[g] = low[0:64] + high[64:128]
    mix = []
    for i in range(3):
        total = jnp.sum(rows(16 + i), axis=0, keepdims=True)
        mix.append(total + pltpu.roll(total, 64, 1))
    for g in range(4):
        own = grad_ref[g, pl.ds(quarter * 16, 16), :]
        for c in range(4):
            k = 4 * g + c
            send_ref[k, 0:4, :] = own[4 * c : 4 * c + 4]
            for i in range(3):
                send_ref[k, 4 + i : 5 + i, :] = mix[i]
            send_ref[k, 7:8, :] = mix[0]


def final_kernel(recv_ref, lift_ref, grad_ref, mix_ref):
    total = recv_ref[0]
    for k in range(1, recv_ref.shape[0]):
        total = total + recv_ref[k]
    grad_ref[...] = total[0:4]
    lift = lift_ref[...].astype(F32)
    mix = lift[:, 0:1] * total[4:5, 0:64]
    mix = mix + lift[:, 1:2] * total[5:6, 0:64]
    mix_ref[...] = mix + lift[:, 2:3] * total[6:7, 0:64]


def spectral_table(mode_index, blocks, rows):
    place = jnp.arange(blocks * 128, dtype=jnp.int32)
    within = place & 127
    cell = (place >> 7) * rows + jnp.where(within >= rows, within - rows, within)
    x_length = blocks * rows
    phases = mode_index[:, None] * cell[None, :] % x_length
    angles = 2.0 * jnp.pi / x_length * phases.astype(F32)
    return jnp.concatenate([jnp.cos(angles), -jnp.sin(angles)], axis=0).astype(BF16)


def local(slot_field, solid, lift_weight, spectral_weight, mix_weight, project_weight, mode_index):
    tile = slot_field[0]
    planes, rows, lanes = tile.shape
    blocks = lax.axis_size("gx")
    x_length = rows * blocks
    cell_total = x_length * lanes * lax.axis_size("gy") * planes
    loss_scale = 16.0 / math.sqrt(cell_total)
    scale_dft = 1.0 / math.sqrt(x_length)
    table = spectral_table(mode_index, blocks, rows)
    lift_t = jnp.pad(lift_weight.T, ((0, 0), (0, 5)))
    mix_t = mix_weight.T
    proj = jnp.pad(project_weight, ((0, 0), (0, 5)))
    proj_t = proj.T

    edge = jax.ShapeDtypeStruct((planes, lanes), F32)
    up, down, right, left = call(edge_kernel, [edge] * 4, tile)

    def shift(array, axis, step):
        count = lax.axis_size(axis)
        pairs = [(i, i + step) for i in range(count) if 0 <= i + step < count]
        return lax.ppermute(array, axis, pairs)

    rims = [shift(down, "gx", -1), shift(up, "gx", 1), shift(right, "gy", 1), shift(left, "gy", -1)]
    rims = jnp.stack(rims + [jnp.zeros_like(up)] * 4, axis=1)
    payload = jnp.concatenate([tile, rims], axis=1)
    fields = lax.all_gather(payload, "grp", axis=0)

    new_velocity, send = call(
        lambda *refs: stencil_kernel(rows, *refs),
        [
            jax.ShapeDtypeStruct((3, planes, rows, lanes), F32),
            jax.ShapeDtypeStruct((blocks * 8, 128), BF16),
        ],
        fields,
        solid,
    )
    recv = lax.all_to_all(
        send.reshape(blocks, 8, 128), "gx", split_axis=0, concat_axis=0, tiled=True
    )
    send = call(
        lambda *refs: line_kernel(scale_dft, loss_scale, *refs),
        jax.ShapeDtypeStruct((blocks, 24, 128), BF16),
        recv,
        table,
        lift_t,
        mix_t,
        spectral_weight,
        proj,
        proj_t,
        scratch=[pltpu.VMEM((64, 128), F32), pltpu.VMEM((64, 128), F32)],
    )
    recv = lax.all_to_all(send, "gx", split_axis=0, concat_axis=0, tiled=True)
    send = call(
        grad_kernel,
        jax.ShapeDtypeStruct((16, 8, 128), F32),
        recv,
        scratch=[pltpu.VMEM((blocks * 24, 128), F32), pltpu.VMEM((4, 64, 128), F32)],
    )
    recv = lax.all_to_all(send, ("grp", "gy"), split_axis=0, concat_axis=0, tiled=True)
    spectral_grad, mix_grad = call(
        final_kernel,
        [jax.ShapeDtypeStruct((4, 128), F32), jax.ShapeDtypeStruct((64, 64), F32)],
        recv,
        lift_t,
    )
    return new_velocity, spectral_grad, mix_grad


def solution(mesh):
    in_specs = (P("grp", None, "gx", "gy"), P(None, "gx", "gy"), P(), P(), P(), P(), P())
    out_specs = (P(None, None, "gx", "gy"), P(("grp", "gx", "gy"), None), P())
    return jax.shard_map(local, mesh=mesh, in_specs=in_specs, out_specs=out_specs, check_vma=False)
```

```python
import math

import jax
import jax.numpy as jnp
from jax import lax
from jax.experimental import pallas as pl
from jax.experimental.pallas import tpu as pltpu
from jax.sharding import PartitionSpec as P

VISCOSITY = 0.05
TIME_STEP = 0.1
F32 = jnp.float32
BF16 = jnp.bfloat16
GELU_A = math.sqrt(2.0 / math.pi)
GELU_B = 0.044715
VMEM = pl.BlockSpec(memory_space=pltpu.VMEM)
NT = (((1,), (1,)), ((), ()))
NN = (((1,), (0,)), ((), ()))
TN = (((0,), (0,)), ((), ()))


def dot(a, b, dims):
    return lax.dot_general(a, b, dims, preferred_element_type=F32)


def iota(shape, axis):
    return lax.broadcasted_iota(jnp.int32, shape, axis)


def call(kernel, out_shape, *args, scratch=()):
    count = len(out_shape) if isinstance(out_shape, (tuple, list)) else 1
    return pl.pallas_call(
        kernel,
        out_shape=out_shape,
        in_specs=[VMEM] * len(args),
        out_specs=[VMEM] * count if isinstance(out_shape, (tuple, list)) else VMEM,
        scratch_shapes=list(scratch),
        compiler_params=pltpu.CompilerParams(vmem_limit_bytes=40 * 1024 * 1024),
    )(*args)


def edge_kernel(tile_ref, right_ref, left_ref):
    rows, lanes = tile_ref.shape[1:]
    same = iota((rows, lanes), 0) == iota((rows, lanes), 1)
    for z in range(2):
        tile = tile_ref[z]
        for ref, lane in ((right_ref, lanes - 1), (left_ref, 0)):
            column = jnp.broadcast_to(tile[:, lane : lane + 1], (rows, lanes))
            ref[z : z + 1, :] = jnp.sum(jnp.where(same, column, 0.0), axis=0, keepdims=True)


def section(rows, fields_ref, solid_ref, rims):
    lanes = fields_ref.shape[3]
    row = iota((rows, lanes), 0)
    lane = iota((rows, lanes), 1)
    same = row == lane
    centre = [[fields_ref[f, z, 0:rows, :] for z in range(2)] for f in range(4)]

    def near(f, z):
        tile = centre[f][z]
        below = above = 0.0
        if rims is not None:
            below, above = (ref[2 * f + z : 2 * f + z + 1, :] for ref in rims)
        x_down = jnp.where(row == 0, below, pltpu.roll(tile, 1, 0))
        x_up = jnp.where(row == rows - 1, above, pltpu.roll(tile, rows - 1, 0))
        sides = []
        for k in (0, 1):
            line = jnp.broadcast_to(fields_ref[f, z, rows + k : rows + k + 1, :], (rows, lanes))
            sides.append(jnp.sum(jnp.where(same, line, 0.0), axis=1, keepdims=True))
        y_down = jnp.where(lane == 0, sides[0], pltpu.roll(tile, 1, 1))
        y_up = jnp.where(lane == lanes - 1, sides[1], pltpu.roll(tile, lanes - 1, 1))
        return x_up, x_down, y_up, y_down

    results = []
    for z in range(2):
        fluid = 1.0 - solid_ref[z].astype(F32)
        velocity = [centre[f][z] for f in range(3)]
        sign = 0.5 if z == 0 else -0.5
        px_up, px_down, py_up, py_down = near(3, z)
        press = (0.5 * (px_up - px_down), 0.5 * (py_up - py_down), sign * centre[3][1 - z])
        new = []
        for f in range(3):
            x_up, x_down, y_up, y_down = near(f, z)
            other = centre[f][1 - z]
            advect = (
                velocity[0] * (0.5 * (x_up - x_down))
                + velocity[1] * (0.5 * (y_up - y_down))
                + velocity[2] * (sign * other)
            )
            lap = other + x_up + x_down + y_up + y_down - 6.0 * velocity[f]
            update = velocity[f] + TIME_STEP * (VISCOSITY * lap - advect - press[f])
            new.append(update * fluid)
        results.append(velocity + new + [centre[3][z], fluid])
    return results


def source_kernel(rows, fields_ref, solid_ref, send_ref, low_ref, high_ref):
    lanes = fields_ref.shape[3]
    role = lax.axis_index("grp")
    results = section(rows, fields_ref, solid_ref, None)
    for f in range(4):
        for z in range(2):
            low_ref[2 * f + z : 2 * f + z + 1, :] = fields_ref[f, z, 0:1, :]
            high_ref[2 * f + z : 2 * f + z + 1, :] = fields_ref[f, z, rows - 1 : rows, :]
    values = [jnp.concatenate([p.astype(BF16) for p in parts], axis=1) for parts in results]
    pad = jnp.zeros((128 - 2 * rows, 8 * lanes), BF16)
    stacked = jnp.concatenate(values + [pad], axis=0)
    count = send_ref.shape[0]
    out_row = iota((count, 8 * lanes), 0)
    column = iota((count, 8 * lanes), 1)
    wanted = (out_row & 7) * lanes + (out_row >> 3) + role * (count // 8)
    pick = jnp.where(column == wanted, 1.0, 0.0).astype(BF16)
    send_ref[...] = dot(pick, stacked, NT).astype(BF16)


def velocity_kernel(rows, fields_ref, solid_ref, below_ref, above_ref, new_ref):
    results = section(rows, fields_ref, solid_ref, (below_ref, above_ref))
    for z in range(2):
        for f in range(3):
            new_ref[f, z] = results[z][3 + f]


def neighbour_terms(lines, rows):
    cells = lines.shape[1]
    lane = iota((8, cells), 1)
    place = lane & 127
    starts = ((place == 0) | (place == rows)) & (lane >= 128)
    stops = ((place == rows - 1) | (place == 2 * rows - 1)) & (lane < cells - 128)
    hop = 128 - rows + 1
    below = jnp.where(starts, pltpu.roll(lines, hop, 1), 0.0)
    above = jnp.where(stops, pltpu.roll(lines, cells - hop, 1), 0.0)
    slope = 0.5 * (above - below)
    first = jnp.where(iota((8, cells), 0) == 0, slope[6:7, :], 0.0)
    terms = VISCOSITY * (above + below) - lines[0:1, :] * slope - first
    return lines[7:8, :] * (TIME_STEP * terms)


def line_kernel(
    scale_dft, loss_scale, recv_ref, table_ref, lift_ref, mix_ref, weight_ref, proj_ref, projt_ref,
    send_ref, back_ref, coef_ref,
):
    blocks = recv_ref.shape[0]
    cells = blocks * 128
    rows = 48
    lines = jnp.concatenate([recv_ref[b] for b in range(blocks)], axis=1)
    plane = iota((64, cells), 1) & 127
    table = table_ref[...]
    zero = jnp.zeros_like(table)
    first = jnp.where(plane < rows, table, zero)
    second = jnp.where((plane >= rows) & (plane < 2 * rows), table, zero)
    both = jnp.concatenate([first, second], axis=0)
    lifted = dot(lift_ref[...], lines, NN).astype(BF16)
    coeffs = dot(both, lifted, NT) * scale_dft
    coeffs16 = coeffs.astype(BF16)
    wide = jnp.concatenate([coeffs16] * 32, axis=1)
    mode_row = iota(wide.shape, 0) & 31
    mode_col = iota(wide.shape, 1) >> 6
    wide = jnp.where(mode_row == mode_col, wide, jnp.zeros_like(wide))
    product = dot(wide, weight_ref[...], NN)
    turned = pltpu.roll(product, 64, 1)
    parts = []
    for line in range(2):
        real = slice(64 * line, 64 * line + 32)
        imag = slice(64 * line + 32, 64 * line + 64)
        parts.append(product[real] - turned[imag])
        parts.append(turned[real] + product[imag])
    mixed = jnp.concatenate(parts, axis=0)
    mixed_t = jnp.transpose(mixed)[0:64].astype(BF16)
    hidden = dot(mixed_t, both, NN) * (2.0 * scale_dft) + dot(mix_ref[...], lifted, NN)
    square = hidden * hidden
    inner = GELU_A * (hidden + GELU_B * (square * hidden))
    tanh = jnp.tanh(inner)
    half = 0.5 * (1.0 + tanh)
    active = (hidden * half).astype(BF16)
    slope = half + (0.5 * GELU_A) * hidden * (1.0 - tanh * tanh) * (1.0 + (3.0 * GELU_B) * square)
    predicted = dot(projt_ref[...], active, NN)
    wide_lines = lines.astype(F32)
    target = pltpu.roll(wide_lines, 5, 0) + neighbour_terms(wide_lines, rows)
    misfit = (predicted - target) * loss_scale
    misfit = jnp.where(iota(misfit.shape, 0) < 3, misfit, 0.0)
    high = misfit.astype(BF16)
    low = (misfit - high.astype(F32)).astype(BF16)
    proj = proj_ref[...]
    back = slope * (dot(proj, high, NN) + dot(proj, low, NN))
    back16 = back.astype(BF16)
    mix_terms = dot(lines, back16, NT)
    back_mixed = dot(both, back16, NT) * (2.0 * scale_dft)
    back_ref[...] = jnp.concatenate([back_mixed[0:64], back_mixed[64:128]], axis=1)
    coef_ref[...] = jnp.concatenate([coeffs[0:64], coeffs[64:128]], axis=1)
    mix_high = mix_terms.astype(BF16)
    mix_low = (mix_terms - mix_high.astype(F32)).astype(BF16)
    tail = jnp.concatenate([mix_high, mix_low], axis=1)
    for j in range(8):
        chunk = jnp.concatenate(
            [
                back_ref[pl.ds(j, 8, stride=8), :],
                coef_ref[pl.ds(j, 8, stride=8), :],
                tail.astype(F32),
            ],
            axis=0,
        ).astype(BF16)
        for q in range(4):
            send_ref[4 * j + q] = chunk


def grad_kernel(recv_ref, send_ref, wide_ref, grad_ref):
    quarter = lax.rem(lax.axis_index("gx"), 4)
    blocks, height = recv_ref.shape[:2]
    for b in range(blocks):
        wide_ref[b * height : (b + 1) * height, :] = recv_ref[b].astype(F32)

    def rows(k):
        return wide_ref[pl.ds(k, blocks, stride=height), :]

    for g in range(4):
        back_re, back_im, coef_re, coef_im = rows(g), rows(4 + g), rows(8 + g), rows(12 + g)
        outs = []
        for left, right in (
            ([coef_re, coef_im], [back_re, back_im]),
            ([coef_re, -coef_im], [back_im, back_re]),
        ):
            left = jnp.concatenate(left, axis=0).astype(BF16)
            right = jnp.concatenate(right, axis=0).astype(BF16)
            outs.append(dot(left, right, TN))
        real, imag = outs
        lane = iota(real.shape, 1)
        low = jnp.where(lane < 64, real, pltpu.roll(imag, 64, 1))
        high = jnp.where(lane < 64, pltpu.roll(real, 64, 1), imag)
        grad_ref[g] = low[0:64] + high[64:128]
    mix = []
    for i in range(3):
        total = jnp.sum(rows(16 + i), axis=0, keepdims=True)
        mix.append(total + pltpu.roll(total, 64, 1))
    for g in range(4):
        own = grad_ref[g, pl.ds(quarter * 16, 16), :]
        for c in range(4):
            k = 4 * g + c
            send_ref[k, 0:4, :] = own[4 * c : 4 * c + 4]
            for i in range(3):
                send_ref[k, 4 + i : 5 + i, :] = mix[i]
            send_ref[k, 7:8, :] = mix[0]


def final_kernel(recv_ref, lift_ref, grad_ref, mix_ref):
    total = recv_ref[0]
    for k in range(1, recv_ref.shape[0]):
        total = total + recv_ref[k]
    grad_ref[...] = total[0:4]
    lift = lift_ref[...].astype(F32)
    mix = lift[:, 0:1] * total[4:5, 0:64]
    mix = mix + lift[:, 1:2] * total[5:6, 0:64]
    mix_ref[...] = mix + lift[:, 2:3] * total[6:7, 0:64]


def spectral_table(mode_index, blocks, rows):
    place = jnp.arange(blocks * 128, dtype=jnp.int32)
    within = place & 127
    cell = (place >> 7) * rows + jnp.where(within >= rows, within - rows, within)
    x_length = blocks * rows
    phases = mode_index[:, None] * cell[None, :] % x_length
    angles = 2.0 * jnp.pi / x_length * phases.astype(F32)
    return jnp.concatenate([jnp.cos(angles), -jnp.sin(angles)], axis=0).astype(BF16)


def local(slot_field, solid, lift_weight, spectral_weight, mix_weight, project_weight, mode_index):
    tile = slot_field[0]
    planes, rows, lanes = tile.shape
    blocks = lax.axis_size("gx")
    x_length = rows * blocks
    cell_total = x_length * lanes * lax.axis_size("gy") * planes
    loss_scale = 16.0 / math.sqrt(cell_total)
    scale_dft = 1.0 / math.sqrt(x_length)
    lift_t = jnp.pad(lift_weight.T, ((0, 0), (0, 5)))
    mix_t = mix_weight.T
    proj = jnp.pad(project_weight, ((0, 0), (0, 5)))
    proj_t = proj.T

    def shift(array, axis, step):
        count = lax.axis_size(axis)
        pairs = [(i, i + step) for i in range(count) if 0 <= i + step < count]
        return lax.ppermute(array, axis, pairs)

    edge = jax.ShapeDtypeStruct((planes, lanes), F32)
    right, left = call(edge_kernel, [edge] * 2, tile)
    rims = [shift(right, "gy", 1), shift(left, "gy", -1)]
    rims = jnp.stack(rims + [jnp.zeros_like(right)] * 6, axis=1)
    payload = jnp.concatenate([tile, rims], axis=1)
    fields = lax.all_gather(payload, "grp", axis=0)

    rim = jax.ShapeDtypeStruct((8, lanes), F32)
    send, low, high = call(
        lambda *refs: source_kernel(rows, *refs),
        [jax.ShapeDtypeStruct((blocks * 8, 128), BF16), rim, rim],
        fields,
        solid,
    )
    mode_index, low, high, send = lax.optimization_barrier((mode_index, low, high, send))
    recv = lax.all_to_all(
        send.reshape(blocks, 8, 128), "gx", split_axis=0, concat_axis=0, tiled=True
    )
    table = spectral_table(mode_index, blocks, rows)
    new_velocity = call(
        lambda *refs: velocity_kernel(rows, *refs),
        jax.ShapeDtypeStruct((3, planes, rows, lanes), F32),
        fields,
        solid,
        shift(high, "gx", 1),
        shift(low, "gx", -1),
    )
    send = call(
        lambda *refs: line_kernel(scale_dft, loss_scale, *refs),
        jax.ShapeDtypeStruct((blocks, 24, 128), BF16),
        recv,
        table,
        lift_t,
        mix_t,
        spectral_weight,
        proj,
        proj_t,
        scratch=[pltpu.VMEM((64, 128), F32), pltpu.VMEM((64, 128), F32)],
    )
    recv = lax.all_to_all(send, "gx", split_axis=0, concat_axis=0, tiled=True)
    send = call(
        grad_kernel,
        jax.ShapeDtypeStruct((16, 8, 128), F32),
        recv,
        scratch=[pltpu.VMEM((blocks * 24, 128), F32), pltpu.VMEM((4, 64, 128), F32)],
    )
    recv = lax.all_to_all(send, ("grp", "gy"), split_axis=0, concat_axis=0, tiled=True)
    spectral_grad, mix_grad = call(
        final_kernel,
        [jax.ShapeDtypeStruct((4, 128), F32), jax.ShapeDtypeStruct((64, 64), F32)],
        recv,
        lift_t,
    )
    return new_velocity, spectral_grad, mix_grad


def solution(mesh):
    in_specs = (P("grp", None, "gx", "gy"), P(None, "gx", "gy"), P(), P(), P(), P(), P())
    out_specs = (P(None, None, "gx", "gy"), P(("grp", "gx", "gy"), None), P())
    return jax.shard_map(local, mesh=mesh, in_specs=in_specs, out_specs=out_specs, check_vma=False)
```

```python
import math

import jax
import jax.numpy as jnp
from jax import lax
from jax.experimental import pallas as pl
from jax.experimental.pallas import tpu as pltpu
from jax.sharding import PartitionSpec as P

VISCOSITY = 0.05
TIME_STEP = 0.1
F32 = jnp.float32
BF16 = jnp.bfloat16
GELU_A = math.sqrt(2.0 / math.pi)
GELU_B = 0.044715
VMEM = pl.BlockSpec(memory_space=pltpu.VMEM)
NT = (((1,), (1,)), ((), ()))
NN = (((1,), (0,)), ((), ()))
TN = (((0,), (0,)), ((), ()))


def dot(a, b, dims):
    return lax.dot_general(a, b, dims, preferred_element_type=F32)


def iota(shape, axis):
    return lax.broadcasted_iota(jnp.int32, shape, axis)


def call(kernel, out_shape, *args, scratch=()):
    count = len(out_shape) if isinstance(out_shape, (tuple, list)) else 1
    return pl.pallas_call(
        kernel,
        out_shape=out_shape,
        in_specs=[VMEM] * len(args),
        out_specs=[VMEM] * count if isinstance(out_shape, (tuple, list)) else VMEM,
        scratch_shapes=list(scratch),
        compiler_params=pltpu.CompilerParams(vmem_limit_bytes=40 * 1024 * 1024),
    )(*args)


def edge_kernel(tile_ref, right_ref, left_ref):
    rows, lanes = tile_ref.shape[1:]
    same = iota((rows, lanes), 0) == iota((rows, lanes), 1)
    for z in range(2):
        tile = tile_ref[z]
        for ref, lane in ((right_ref, lanes - 1), (left_ref, 0)):
            column = jnp.broadcast_to(tile[:, lane : lane + 1], (rows, lanes))
            ref[z : z + 1, :] = jnp.sum(jnp.where(same, column, 0.0), axis=0, keepdims=True)


def section(rows, fields_ref, solid_ref, rims):
    lanes = fields_ref.shape[3]
    row = iota((rows, lanes), 0)
    lane = iota((rows, lanes), 1)
    same = row == lane
    centre = [[fields_ref[f, z, 0:rows, :] for z in range(2)] for f in range(4)]

    def near(f, z):
        tile = centre[f][z]
        below = above = 0.0
        if rims is not None:
            below, above = (ref[2 * f + z : 2 * f + z + 1, :] for ref in rims)
        x_down = jnp.where(row == 0, below, pltpu.roll(tile, 1, 0))
        x_up = jnp.where(row == rows - 1, above, pltpu.roll(tile, rows - 1, 0))
        sides = []
        for k in (0, 1):
            line = jnp.broadcast_to(fields_ref[f, z, rows + k : rows + k + 1, :], (rows, lanes))
            sides.append(jnp.sum(jnp.where(same, line, 0.0), axis=1, keepdims=True))
        y_down = jnp.where(lane == 0, sides[0], pltpu.roll(tile, 1, 1))
        y_up = jnp.where(lane == lanes - 1, sides[1], pltpu.roll(tile, lanes - 1, 1))
        return x_up, x_down, y_up, y_down

    results = []
    for z in range(2):
        fluid = 1.0 - solid_ref[z].astype(F32)
        velocity = [centre[f][z] for f in range(3)]
        sign = 0.5 if z == 0 else -0.5
        px_up, px_down, py_up, py_down = near(3, z)
        press = (0.5 * (px_up - px_down), 0.5 * (py_up - py_down), sign * centre[3][1 - z])
        new = []
        for f in range(3):
            x_up, x_down, y_up, y_down = near(f, z)
            other = centre[f][1 - z]
            advect = (
                velocity[0] * (0.5 * (x_up - x_down))
                + velocity[1] * (0.5 * (y_up - y_down))
                + velocity[2] * (sign * other)
            )
            lap = other + x_up + x_down + y_up + y_down - 6.0 * velocity[f]
            update = velocity[f] + TIME_STEP * (VISCOSITY * lap - advect - press[f])
            new.append(update * fluid)
        results.append(velocity + new + [centre[3][z], fluid])
    return results


def source_kernel(rows, fields_ref, solid_ref, send_ref, low_ref, high_ref):
    lanes = fields_ref.shape[3]
    role = lax.axis_index("grp")
    results = section(rows, fields_ref, solid_ref, None)
    for f in range(4):
        for z in range(2):
            low_ref[2 * f + z : 2 * f + z + 1, :] = fields_ref[f, z, 0:1, :]
            high_ref[2 * f + z : 2 * f + z + 1, :] = fields_ref[f, z, rows - 1 : rows, :]
    values = [jnp.concatenate([p.astype(BF16) for p in parts], axis=1) for parts in results]
    pad = jnp.zeros((128 - 2 * rows, 8 * lanes), BF16)
    stacked = jnp.concatenate(values + [pad], axis=0)
    count = send_ref.shape[0]
    out_row = iota((count, 8 * lanes), 0)
    column = iota((count, 8 * lanes), 1)
    wanted = (out_row & 7) * lanes + (out_row >> 3) + role * (count // 8)
    pick = jnp.where(column == wanted, 1.0, 0.0).astype(BF16)
    send_ref[...] = dot(pick, stacked, NT).astype(BF16)


def velocity_kernel(rows, fields_ref, solid_ref, below_ref, above_ref, new_ref):
    results = section(rows, fields_ref, solid_ref, (below_ref, above_ref))
    for z in range(2):
        for f in range(3):
            new_ref[f, z] = results[z][3 + f]


def neighbour_terms(lines, rows):
    cells = lines.shape[1]
    lane = iota((8, cells), 1)
    place = lane & 127
    starts = ((place == 0) | (place == rows)) & (lane >= 128)
    stops = ((place == rows - 1) | (place == 2 * rows - 1)) & (lane < cells - 128)
    hop = 128 - rows + 1
    below = jnp.where(starts, pltpu.roll(lines, hop, 1), 0.0)
    above = jnp.where(stops, pltpu.roll(lines, cells - hop, 1), 0.0)
    slope = 0.5 * (above - below)
    first = jnp.where(iota((8, cells), 0) == 0, slope[6:7, :], 0.0)
    terms = VISCOSITY * (above + below) - lines[0:1, :] * slope - first
    return lines[7:8, :] * (TIME_STEP * terms)


def line_kernel(
    scale_dft, loss_scale, recv_ref, table_ref, lift_ref, mix_ref, weight_ref, proj_ref, projt_ref,
    send_ref, back_ref, coef_ref,
):
    blocks = recv_ref.shape[0]
    cells = blocks * 128
    rows = 48
    lines = jnp.concatenate([recv_ref[b] for b in range(blocks)], axis=1)
    both = table_ref[...]
    lifted = dot(lift_ref[...], lines, NN).astype(BF16)
    coeffs = dot(both, lifted, NT) * scale_dft
    coeffs16 = coeffs.astype(BF16)
    wide = jnp.concatenate([coeffs16] * 32, axis=1)
    mode_row = iota(wide.shape, 0) & 31
    mode_col = iota(wide.shape, 1) >> 6
    wide = jnp.where(mode_row == mode_col, wide, jnp.zeros_like(wide))
    product = dot(wide, weight_ref[...], NN)
    turned = pltpu.roll(product, 64, 1)
    parts = []
    for line in range(2):
        real = slice(64 * line, 64 * line + 32)
        imag = slice(64 * line + 32, 64 * line + 64)
        parts.append(product[real] - turned[imag])
        parts.append(turned[real] + product[imag])
    mixed = jnp.concatenate(parts, axis=0)
    mixed_t = jnp.transpose(mixed)[0:64].astype(BF16)
    hidden = dot(mixed_t, both, NN) * (2.0 * scale_dft) + dot(mix_ref[...], lifted, NN)
    square = hidden * hidden
    inner = GELU_A * (hidden + GELU_B * (square * hidden))
    tanh = jnp.tanh(inner)
    half = 0.5 * (1.0 + tanh)
    active = (hidden * half).astype(BF16)
    slope = half + (0.5 * GELU_A) * hidden * (1.0 - tanh * tanh) * (1.0 + (3.0 * GELU_B) * square)
    predicted = dot(projt_ref[...], active, NN)
    wide_lines = lines.astype(F32)
    target = pltpu.roll(wide_lines, 5, 0) + neighbour_terms(wide_lines, rows)
    misfit = (predicted - target) * loss_scale
    misfit = jnp.where(iota(misfit.shape, 0) < 3, misfit, 0.0)
    high = misfit.astype(BF16)
    low = (misfit - high.astype(F32)).astype(BF16)
    proj = proj_ref[...]
    back = slope * (dot(proj, high, NN) + dot(proj, low, NN))
    back16 = back.astype(BF16)
    mix_terms = dot(lines, back16, NT)
    back_mixed = dot(both, back16, NT) * (2.0 * scale_dft)
    back_ref[...] = jnp.concatenate([back_mixed[0:64], back_mixed[64:128]], axis=1)
    coef_ref[...] = jnp.concatenate([coeffs[0:64], coeffs[64:128]], axis=1)
    mix_high = mix_terms.astype(BF16)
    mix_low = (mix_terms - mix_high.astype(F32)).astype(BF16)
    tail = jnp.concatenate([mix_high, mix_low], axis=1)
    for j in range(8):
        chunk = jnp.concatenate(
            [
                back_ref[pl.ds(j, 8, stride=8), :],
                coef_ref[pl.ds(j, 8, stride=8), :],
                tail.astype(F32),
            ],
            axis=0,
        ).astype(BF16)
        for q in range(4):
            send_ref[4 * j + q] = chunk


def grad_kernel(recv_ref, send_ref, wide_ref, grad_ref):
    quarter = lax.rem(lax.axis_index("gx"), 4)
    blocks, height = recv_ref.shape[:2]
    for b in range(blocks):
        wide_ref[b * height : (b + 1) * height, :] = recv_ref[b].astype(F32)

    def rows(k):
        return wide_ref[pl.ds(k, blocks, stride=height), :]

    for g in range(4):
        back_re, back_im, coef_re, coef_im = rows(g), rows(4 + g), rows(8 + g), rows(12 + g)
        outs = []
        for left, right in (
            ([coef_re, coef_im], [back_re, back_im]),
            ([coef_re, -coef_im], [back_im, back_re]),
        ):
            left = jnp.concatenate(left, axis=0).astype(BF16)
            right = jnp.concatenate(right, axis=0).astype(BF16)
            outs.append(dot(left, right, TN))
        real, imag = outs
        lane = iota(real.shape, 1)
        low = jnp.where(lane < 64, real, pltpu.roll(imag, 64, 1))
        high = jnp.where(lane < 64, pltpu.roll(real, 64, 1), imag)
        grad_ref[g] = low[0:64] + high[64:128]
    mix = []
    for i in range(3):
        total = jnp.sum(rows(16 + i), axis=0, keepdims=True)
        mix.append(total + pltpu.roll(total, 64, 1))
    for g in range(4):
        own = grad_ref[g, pl.ds(quarter * 16, 16), :]
        for c in range(4):
            k = 4 * g + c
            send_ref[k, 0:4, :] = own[4 * c : 4 * c + 4]
            for i in range(3):
                send_ref[k, 4 + i : 5 + i, :] = mix[i]
            send_ref[k, 7:8, :] = mix[0]


def final_kernel(recv_ref, lift_ref, grad_ref, mix_ref):
    total = recv_ref[0]
    for k in range(1, recv_ref.shape[0]):
        total = total + recv_ref[k]
    grad_ref[...] = total[0:4]
    lift = lift_ref[...].astype(F32)
    mix = lift[:, 0:1] * total[4:5, 0:64]
    mix = mix + lift[:, 1:2] * total[5:6, 0:64]
    mix_ref[...] = mix + lift[:, 2:3] * total[6:7, 0:64]


def table_kernel(blocks, rows, mode_ref, table_ref):
    modes = mode_ref.shape[1]
    square = (modes, modes)
    index = jnp.where(iota(square, 0) == iota(square, 1), mode_ref[...].astype(F32), 0.0)
    index = jnp.sum(index, axis=1, keepdims=True).astype(jnp.int32)
    shape = (modes, 128)
    lane = iota(shape, 1)
    unit = 2.0 * math.pi / (blocks * rows)
    outer = unit * (((index * lane) & (blocks - 1)) * rows).astype(F32)
    cell = jnp.where(lane >= rows, lane - rows, lane)
    cell = jnp.where(lane < 2 * rows, cell, 0)
    inner = unit * (index * cell).astype(F32)
    outer_cos, outer_sin = jnp.cos(outer), jnp.sin(outer)
    inner_cos, inner_sin = jnp.cos(inner), jnp.sin(inner)
    planes = [lane < rows, (lane >= rows) & (lane < 2 * rows)]
    factors = [(jnp.where(p, inner_cos, 0.0), jnp.where(p, inner_sin, 0.0)) for p in planes]
    for b in range(blocks):
        cos_b = outer_cos[:, b : b + 1]
        sin_b = outer_sin[:, b : b + 1]
        parts = []
        for cos_c, sin_c in factors:
            parts.append(cos_b * cos_c - sin_b * sin_c)
            parts.append(-(sin_b * cos_c) - cos_b * sin_c)
        table_ref[:, b * 128 : (b + 1) * 128] = jnp.concatenate(parts, axis=0).astype(BF16)


def local(slot_field, solid, lift_weight, spectral_weight, mix_weight, project_weight, mode_index):
    tile = slot_field[0]
    planes, rows, lanes = tile.shape
    blocks = lax.axis_size("gx")
    x_length = rows * blocks
    cell_total = x_length * lanes * lax.axis_size("gy") * planes
    loss_scale = 16.0 / math.sqrt(cell_total)
    scale_dft = 1.0 / math.sqrt(x_length)
    lift_t = jnp.pad(lift_weight.T, ((0, 0), (0, 5)))
    mix_t = mix_weight.T
    proj = jnp.pad(project_weight, ((0, 0), (0, 5)))
    proj_t = proj.T

    def shift(array, axis, step):
        count = lax.axis_size(axis)
        pairs = [(i, i + step) for i in range(count) if 0 <= i + step < count]
        return lax.ppermute(array, axis, pairs)

    edge = jax.ShapeDtypeStruct((planes, lanes), F32)
    right, left = call(edge_kernel, [edge] * 2, tile)
    rims = [shift(right, "gy", 1), shift(left, "gy", -1)]
    rims = jnp.stack(rims + [jnp.zeros_like(right)] * 6, axis=1)
    payload = jnp.concatenate([tile, rims], axis=1)
    fields = lax.all_gather(payload, "grp", axis=0)

    rim = jax.ShapeDtypeStruct((8, lanes), F32)
    send, low, high = call(
        lambda *refs: source_kernel(rows, *refs),
        [jax.ShapeDtypeStruct((blocks * 8, 128), BF16), rim, rim],
        fields,
        solid,
    )
    mode_index, low, high, send = lax.optimization_barrier((mode_index, low, high, send))
    recv = lax.all_to_all(
        send.reshape(blocks, 8, 128), "gx", split_axis=0, concat_axis=0, tiled=True
    )
    table = call(
        lambda *refs: table_kernel(blocks, rows, *refs),
        jax.ShapeDtypeStruct((128, blocks * 128), BF16),
        mode_index.reshape(1, -1),
    )
    below, above = shift(high, "gx", 1), shift(low, "gx", -1)
    recv, below, above = lax.optimization_barrier((recv, below, above))
    new_velocity = call(
        lambda *refs: velocity_kernel(rows, *refs),
        jax.ShapeDtypeStruct((3, planes, rows, lanes), F32),
        fields,
        solid,
        below,
        above,
    )
    send = call(
        lambda *refs: line_kernel(scale_dft, loss_scale, *refs),
        jax.ShapeDtypeStruct((blocks, 24, 128), BF16),
        recv,
        table,
        lift_t,
        mix_t,
        spectral_weight,
        proj,
        proj_t,
        scratch=[pltpu.VMEM((64, 128), F32), pltpu.VMEM((64, 128), F32)],
    )
    recv = lax.all_to_all(send, "gx", split_axis=0, concat_axis=0, tiled=True)
    send = call(
        grad_kernel,
        jax.ShapeDtypeStruct((16, 8, 128), F32),
        recv,
        scratch=[pltpu.VMEM((blocks * 24, 128), F32), pltpu.VMEM((4, 64, 128), F32)],
    )
    recv = lax.all_to_all(send, ("grp", "gy"), split_axis=0, concat_axis=0, tiled=True)
    spectral_grad, mix_grad = call(
        final_kernel,
        [jax.ShapeDtypeStruct((4, 128), F32), jax.ShapeDtypeStruct((64, 64), F32)],
        recv,
        lift_t,
    )
    return new_velocity, spectral_grad, mix_grad


def solution(mesh):
    in_specs = (P("grp", None, "gx", "gy"), P(None, "gx", "gy"), P(), P(), P(), P(), P())
    out_specs = (P(None, None, "gx", "gy"), P(("grp", "gx", "gy"), None), P())
    return jax.shard_map(local, mesh=mesh, in_specs=in_specs, out_specs=out_specs, check_vma=False)
```

```python
import math

import jax
import jax.numpy as jnp
from jax import lax
from jax.experimental import pallas as pl
from jax.experimental.pallas import tpu as pltpu
from jax.sharding import PartitionSpec as P

VISCOSITY = 0.05
TIME_STEP = 0.1
F32 = jnp.float32
BF16 = jnp.bfloat16
GELU_A = math.sqrt(2.0 / math.pi)
GELU_B = 0.044715
VMEM = pl.BlockSpec(memory_space=pltpu.VMEM)
NT = (((1,), (1,)), ((), ()))
NN = (((1,), (0,)), ((), ()))
TN = (((0,), (0,)), ((), ()))


def dot(a, b, dims):
    return lax.dot_general(a, b, dims, preferred_element_type=F32)


def iota(shape, axis):
    return lax.broadcasted_iota(jnp.int32, shape, axis)


def call(kernel, out_shape, *args, scratch=()):
    count = len(out_shape) if isinstance(out_shape, (tuple, list)) else 1
    return pl.pallas_call(
        kernel,
        out_shape=out_shape,
        in_specs=[VMEM] * len(args),
        out_specs=[VMEM] * count if isinstance(out_shape, (tuple, list)) else VMEM,
        scratch_shapes=list(scratch),
        compiler_params=pltpu.CompilerParams(vmem_limit_bytes=40 * 1024 * 1024),
    )(*args)


def edge_kernel(tile_ref, right_ref, left_ref):
    rows, lanes = tile_ref.shape[1:]
    same = iota((rows, lanes), 0) == iota((rows, lanes), 1)
    for z in range(2):
        tile = tile_ref[z]
        for ref, lane in ((right_ref, lanes - 1), (left_ref, 0)):
            column = jnp.broadcast_to(tile[:, lane : lane + 1], (rows, lanes))
            ref[z : z + 1, :] = jnp.sum(jnp.where(same, column, 0.0), axis=0, keepdims=True)


def section(rows, fields_ref, solid_ref, rims):
    lanes = fields_ref.shape[3]
    row = iota((rows, lanes), 0)
    lane = iota((rows, lanes), 1)
    same = row == lane
    centre = [[fields_ref[f, z, 0:rows, :] for z in range(2)] for f in range(4)]

    def near(f, z):
        tile = centre[f][z]
        below = above = 0.0
        if rims is not None:
            below, above = (rim[2 * f + z : 2 * f + z + 1, :] for rim in rims)
        x_down = jnp.where(row == 0, below, pltpu.roll(tile, 1, 0))
        x_up = jnp.where(row == rows - 1, above, pltpu.roll(tile, rows - 1, 0))
        sides = []
        for k in (0, 1):
            line = jnp.broadcast_to(fields_ref[f, z, rows + k : rows + k + 1, :], (rows, lanes))
            sides.append(jnp.sum(jnp.where(same, line, 0.0), axis=1, keepdims=True))
        y_down = jnp.where(lane == 0, sides[0], pltpu.roll(tile, 1, 1))
        y_up = jnp.where(lane == lanes - 1, sides[1], pltpu.roll(tile, lanes - 1, 1))
        return x_up, x_down, y_up, y_down

    results = []
    for z in range(2):
        fluid = 1.0 - solid_ref[z].astype(F32)
        velocity = [centre[f][z] for f in range(3)]
        sign = 0.5 if z == 0 else -0.5
        px_up, px_down, py_up, py_down = near(3, z)
        press = (0.5 * (px_up - px_down), 0.5 * (py_up - py_down), sign * centre[3][1 - z])
        new = []
        for f in range(3):
            x_up, x_down, y_up, y_down = near(f, z)
            other = centre[f][1 - z]
            advect = (
                velocity[0] * (0.5 * (x_up - x_down))
                + velocity[1] * (0.5 * (y_up - y_down))
                + velocity[2] * (sign * other)
            )
            lap = other + x_up + x_down + y_up + y_down - 6.0 * velocity[f]
            update = velocity[f] + TIME_STEP * (VISCOSITY * lap - advect - press[f])
            new.append(update * fluid)
        results.append(velocity + new + [centre[3][z], fluid])
    return results


def source_kernel(rows, fields_ref, solid_ref, send_ref, rim_ref):
    blocks = send_ref.shape[0]
    lanes = fields_ref.shape[3]
    role = lax.axis_index("grp")
    own = lax.axis_index("gx")
    results = section(rows, fields_ref, solid_ref, None)
    for f in range(4):
        for z in range(2):
            for k, row in ((0, 0), (1, rows - 1)):
                rim_ref[k, 2 * f + z : 2 * f + z + 1, :] = fields_ref[f, z, row : row + 1, :]
    rims = []
    for k in range(2):
        high = rim_ref[k].astype(BF16).astype(F32)
        rims.append(jnp.concatenate([high, rim_ref[k] - high], axis=0))
    values = [jnp.concatenate([p.astype(BF16) for p in parts], axis=1) for parts in results]
    pad = jnp.zeros((128 - 2 * rows, 8 * lanes), BF16)
    stacked = jnp.concatenate(values + [pad], axis=0)
    shape = (blocks * 8, 8 * lanes)
    out_row = iota(shape, 0)
    wanted = (out_row & 7) * lanes + (out_row >> 3) + role * blocks
    pick = jnp.where(iota(shape, 1) == wanted, 1.0, 0.0).astype(BF16)
    lines = dot(pick, stacked, NT)
    for b in range(blocks):
        rim = jnp.where(b > own, rims[1], rims[0])
        send_ref[b] = jnp.concatenate([lines[8 * b : 8 * b + 8], rim], axis=0).astype(BF16)


def velocity_kernel(rows, fields_ref, solid_ref, recv_ref, new_ref):
    last = recv_ref.shape[0] - 1
    own = lax.axis_index("gx")
    rims = []
    for index, inside in ((own - 1, own > 0), (own + 1, own < last)):
        message = recv_ref[jnp.minimum(jnp.maximum(index, 0), last)].astype(F32)
        rims.append(jnp.where(inside, message[8:16] + message[16:24], 0.0))
    results = section(rows, fields_ref, solid_ref, rims)
    for z in range(2):
        for f in range(3):
            new_ref[f, z] = results[z][3 + f]


def neighbour_terms(lines, rows):
    cells = lines.shape[1]
    lane = iota((8, cells), 1)
    place = lane & 127
    starts = ((place == 0) | (place == rows)) & (lane >= 128)
    stops = ((place == rows - 1) | (place == 2 * rows - 1)) & (lane < cells - 128)
    hop = 128 - rows + 1
    below = jnp.where(starts, pltpu.roll(lines, hop, 1), 0.0)
    above = jnp.where(stops, pltpu.roll(lines, cells - hop, 1), 0.0)
    slope = 0.5 * (above - below)
    first = jnp.where(iota((8, cells), 0) == 0, slope[6:7, :], 0.0)
    terms = VISCOSITY * (above + below) - lines[0:1, :] * slope - first
    return lines[7:8, :] * (TIME_STEP * terms)


def line_kernel(
    scale_dft, loss_scale, recv_ref, table_ref, lift_ref, mix_ref, weight_ref, proj_ref, projt_ref,
    send_ref, back_ref, coef_ref,
):
    blocks = recv_ref.shape[0]
    cells = blocks * 128
    rows = 48
    lines = jnp.concatenate([recv_ref[b, 0:8, :] for b in range(blocks)], axis=1)
    both = table_ref[...]
    lifted = dot(lift_ref[...], lines, NN).astype(BF16)
    coeffs = dot(both, lifted, NT) * scale_dft
    coeffs16 = coeffs.astype(BF16)
    wide = jnp.concatenate([coeffs16] * 32, axis=1)
    mode_row = iota(wide.shape, 0) & 31
    mode_col = iota(wide.shape, 1) >> 6
    wide = jnp.where(mode_row == mode_col, wide, jnp.zeros_like(wide))
    product = dot(wide, weight_ref[...], NN)
    turned = pltpu.roll(product, 64, 1)
    parts = []
    for line in range(2):
        real = slice(64 * line, 64 * line + 32)
        imag = slice(64 * line + 32, 64 * line + 64)
        parts.append(product[real] - turned[imag])
        parts.append(turned[real] + product[imag])
    mixed = jnp.concatenate(parts, axis=0)
    mixed_t = jnp.transpose(mixed)[0:64].astype(BF16)
    hidden = dot(mixed_t, both, NN) * (2.0 * scale_dft) + dot(mix_ref[...], lifted, NN)
    square = hidden * hidden
    inner = GELU_A * (hidden + GELU_B * (square * hidden))
    tanh = jnp.tanh(inner)
    half = 0.5 * (1.0 + tanh)
    active = (hidden * half).astype(BF16)
    slope = half + (0.5 * GELU_A) * hidden * (1.0 - tanh * tanh) * (1.0 + (3.0 * GELU_B) * square)
    predicted = dot(projt_ref[...], active, NN)
    wide_lines = lines.astype(F32)
    target = pltpu.roll(wide_lines, 5, 0) + neighbour_terms(wide_lines, rows)
    misfit = (predicted - target) * loss_scale
    misfit = jnp.where(iota(misfit.shape, 0) < 3, misfit, 0.0)
    high = misfit.astype(BF16)
    low = (misfit - high.astype(F32)).astype(BF16)
    proj = proj_ref[...]
    back = slope * (dot(proj, high, NN) + dot(proj, low, NN))
    back16 = back.astype(BF16)
    mix_terms = dot(lines, back16, NT)
    back_mixed = dot(both, back16, NT) * (2.0 * scale_dft)
    back_ref[...] = jnp.concatenate([back_mixed[0:64], back_mixed[64:128]], axis=1)
    coef_ref[...] = jnp.concatenate([coeffs[0:64], coeffs[64:128]], axis=1)
    mix_high = mix_terms.astype(BF16)
    mix_low = (mix_terms - mix_high.astype(F32)).astype(BF16)
    tail = jnp.concatenate([mix_high, mix_low], axis=1)
    for j in range(8):
        chunk = jnp.concatenate(
            [
                back_ref[pl.ds(j, 8, stride=8), :],
                coef_ref[pl.ds(j, 8, stride=8), :],
                tail.astype(F32),
            ],
            axis=0,
        ).astype(BF16)
        for q in range(4):
            send_ref[4 * j + q] = chunk


def grad_kernel(recv_ref, send_ref, wide_ref, grad_ref):
    quarter = lax.rem(lax.axis_index("gx"), 4)
    blocks, height = recv_ref.shape[:2]
    for b in range(blocks):
        wide_ref[b * height : (b + 1) * height, :] = recv_ref[b].astype(F32)

    def rows(k):
        return wide_ref[pl.ds(k, blocks, stride=height), :]

    for g in range(4):
        back_re, back_im, coef_re, coef_im = rows(g), rows(4 + g), rows(8 + g), rows(12 + g)
        outs = []
        for left, right in (
            ([coef_re, coef_im], [back_re, back_im]),
            ([coef_re, -coef_im], [back_im, back_re]),
        ):
            left = jnp.concatenate(left, axis=0).astype(BF16)
            right = jnp.concatenate(right, axis=0).astype(BF16)
            outs.append(dot(left, right, TN))
        real, imag = outs
        lane = iota(real.shape, 1)
        low = jnp.where(lane < 64, real, pltpu.roll(imag, 64, 1))
        high = jnp.where(lane < 64, pltpu.roll(real, 64, 1), imag)
        grad_ref[g] = low[0:64] + high[64:128]
    mix = []
    for i in range(3):
        total = jnp.sum(rows(16 + i), axis=0, keepdims=True)
        mix.append(total + pltpu.roll(total, 64, 1))
    for g in range(4):
        own = grad_ref[g, pl.ds(quarter * 16, 16), :]
        for c in range(4):
            k = 4 * g + c
            send_ref[k, 0:4, :] = own[4 * c : 4 * c + 4]
            for i in range(3):
                send_ref[k, 4 + i : 5 + i, :] = mix[i]
            send_ref[k, 7:8, :] = mix[0]


def final_kernel(recv_ref, lift_ref, grad_ref, mix_ref):
    total = recv_ref[0]
    for k in range(1, recv_ref.shape[0]):
        total = total + recv_ref[k]
    grad_ref[...] = total[0:4]
    lift = lift_ref[...].astype(F32)
    mix = lift[:, 0:1] * total[4:5, 0:64]
    mix = mix + lift[:, 1:2] * total[5:6, 0:64]
    mix_ref[...] = mix + lift[:, 2:3] * total[6:7, 0:64]


def table_kernel(blocks, rows, mode_ref, table_ref):
    modes = mode_ref.shape[1]
    square = (modes, modes)
    index = jnp.where(iota(square, 0) == iota(square, 1), mode_ref[...].astype(F32), 0.0)
    index = jnp.sum(index, axis=1, keepdims=True).astype(jnp.int32)
    shape = (modes, 128)
    lane = iota(shape, 1)
    unit = 2.0 * math.pi / (blocks * rows)
    outer = unit * (((index * lane) & (blocks - 1)) * rows).astype(F32)
    cell = jnp.where(lane >= rows, lane - rows, lane)
    cell = jnp.where(lane < 2 * rows, cell, 0)
    inner = unit * (index * cell).astype(F32)
    outer_cos, outer_sin = jnp.cos(outer), jnp.sin(outer)
    inner_cos, inner_sin = jnp.cos(inner), jnp.sin(inner)
    planes = [lane < rows, (lane >= rows) & (lane < 2 * rows)]
    factors = [(jnp.where(p, inner_cos, 0.0), jnp.where(p, inner_sin, 0.0)) for p in planes]
    for b in range(blocks):
        cos_b = outer_cos[:, b : b + 1]
        sin_b = outer_sin[:, b : b + 1]
        parts = []
        for cos_c, sin_c in factors:
            parts.append(cos_b * cos_c - sin_b * sin_c)
            parts.append(-(sin_b * cos_c) - cos_b * sin_c)
        table_ref[:, b * 128 : (b + 1) * 128] = jnp.concatenate(parts, axis=0).astype(BF16)


def local(slot_field, solid, lift_weight, spectral_weight, mix_weight, project_weight, mode_index):
    tile = slot_field[0]
    planes, rows, lanes = tile.shape
    blocks = lax.axis_size("gx")
    x_length = rows * blocks
    cell_total = x_length * lanes * lax.axis_size("gy") * planes
    loss_scale = 16.0 / math.sqrt(cell_total)
    scale_dft = 1.0 / math.sqrt(x_length)
    lift_t = jnp.pad(lift_weight.T, ((0, 0), (0, 5)))
    mix_t = mix_weight.T
    proj = jnp.pad(project_weight, ((0, 0), (0, 5)))
    proj_t = proj.T

    def shift(array, axis, step):
        count = lax.axis_size(axis)
        pairs = [(i, i + step) for i in range(count) if 0 <= i + step < count]
        return lax.ppermute(array, axis, pairs)

    edge = jax.ShapeDtypeStruct((planes, lanes), F32)
    right, left = call(edge_kernel, [edge] * 2, tile)
    rims = [shift(right, "gy", 1), shift(left, "gy", -1)]
    rims = jnp.stack(rims + [jnp.zeros_like(right)] * 6, axis=1)
    payload = jnp.concatenate([tile, rims], axis=1)
    fields = lax.all_gather(payload, "grp", axis=0)

    send = call(
        lambda *refs: source_kernel(rows, *refs),
        jax.ShapeDtypeStruct((blocks, 24, 128), BF16),
        fields,
        solid,
        scratch=[pltpu.VMEM((2, 8, lanes), F32)],
    )
    mode_index, send = lax.optimization_barrier((mode_index, send))
    recv = lines = lax.all_to_all(send, "gx", split_axis=0, concat_axis=0, tiled=True)
    table = call(
        lambda *refs: table_kernel(blocks, rows, *refs),
        jax.ShapeDtypeStruct((128, blocks * 128), BF16),
        mode_index.reshape(1, -1),
    )
    new_velocity = call(
        lambda *refs: velocity_kernel(rows, *refs),
        jax.ShapeDtypeStruct((3, planes, rows, lanes), F32),
        fields,
        solid,
        lines,
    )
    send = call(
        lambda *refs: line_kernel(scale_dft, loss_scale, *refs),
        jax.ShapeDtypeStruct((blocks, 24, 128), BF16),
        recv,
        table,
        lift_t,
        mix_t,
        spectral_weight,
        proj,
        proj_t,
        scratch=[pltpu.VMEM((64, 128), F32), pltpu.VMEM((64, 128), F32)],
    )
    recv = lax.all_to_all(send, "gx", split_axis=0, concat_axis=0, tiled=True)
    send = call(
        grad_kernel,
        jax.ShapeDtypeStruct((16, 8, 128), F32),
        recv,
        scratch=[pltpu.VMEM((blocks * 24, 128), F32), pltpu.VMEM((4, 64, 128), F32)],
    )
    recv = lax.all_to_all(send, ("grp", "gy"), split_axis=0, concat_axis=0, tiled=True)
    spectral_grad, mix_grad = call(
        final_kernel,
        [jax.ShapeDtypeStruct((4, 128), F32), jax.ShapeDtypeStruct((64, 64), F32)],
        recv,
        lift_t,
    )
    return new_velocity, spectral_grad, mix_grad


def solution(mesh):
    in_specs = (P("grp", None, "gx", "gy"), P(None, "gx", "gy"), P(), P(), P(), P(), P())
    out_specs = (P(None, None, "gx", "gy"), P(("grp", "gx", "gy"), None), P())
    return jax.shard_map(local, mesh=mesh, in_specs=in_specs, out_specs=out_specs, check_vma=False)
```

```python
import math

import jax
import jax.numpy as jnp
from jax import lax
from jax.experimental import pallas as pl
from jax.experimental.pallas import tpu as pltpu
from jax.sharding import PartitionSpec as P

VISCOSITY = 0.05
TIME_STEP = 0.1
F32 = jnp.float32
BF16 = jnp.bfloat16
GELU_A = math.sqrt(2.0 / math.pi)
GELU_B = 0.044715
VMEM = pl.BlockSpec(memory_space=pltpu.VMEM)
NT = (((1,), (1,)), ((), ()))
NN = (((1,), (0,)), ((), ()))
TN = (((0,), (0,)), ((), ()))


def dot(a, b, dims):
    return lax.dot_general(a, b, dims, preferred_element_type=F32)


def iota(shape, axis):
    return lax.broadcasted_iota(jnp.int32, shape, axis)


def call(kernel, out_shape, *args, scratch=()):
    count = len(out_shape) if isinstance(out_shape, (tuple, list)) else 1
    return pl.pallas_call(
        kernel,
        out_shape=out_shape,
        in_specs=[VMEM] * len(args),
        out_specs=[VMEM] * count if isinstance(out_shape, (tuple, list)) else VMEM,
        scratch_shapes=list(scratch),
        compiler_params=pltpu.CompilerParams(vmem_limit_bytes=40 * 1024 * 1024),
    )(*args)


def edge_kernel(tile_ref, right_ref, left_ref):
    rows, lanes = tile_ref.shape[1:]
    same = iota((rows, lanes), 0) == iota((rows, lanes), 1)
    for z in range(2):
        tile = tile_ref[z]
        for ref, lane in ((right_ref, lanes - 1), (left_ref, 0)):
            column = jnp.broadcast_to(tile[:, lane : lane + 1], (rows, lanes))
            ref[z : z + 1, :] = jnp.sum(jnp.where(same, column, 0.0), axis=0, keepdims=True)


def section(rows, fields_ref, solid_ref, rims):
    lanes = fields_ref.shape[3]
    row = iota((rows, lanes), 0)
    lane = iota((rows, lanes), 1)
    same = row == lane
    centre = [[fields_ref[f, z, 0:rows, :] for z in range(2)] for f in range(4)]

    def near(f, z):
        tile = centre[f][z]
        below = above = 0.0
        if rims is not None:
            below, above = (rim[2 * f + z : 2 * f + z + 1, :] for rim in rims)
        x_down = jnp.where(row == 0, below, pltpu.roll(tile, 1, 0))
        x_up = jnp.where(row == rows - 1, above, pltpu.roll(tile, rows - 1, 0))
        sides = []
        for k in (0, 1):
            line = jnp.broadcast_to(fields_ref[f, z, rows + k : rows + k + 1, :], (rows, lanes))
            sides.append(jnp.sum(jnp.where(same, line, 0.0), axis=1, keepdims=True))
        y_down = jnp.where(lane == 0, sides[0], pltpu.roll(tile, 1, 1))
        y_up = jnp.where(lane == lanes - 1, sides[1], pltpu.roll(tile, lanes - 1, 1))
        return x_up, x_down, y_up, y_down

    results = []
    for z in range(2):
        fluid = 1.0 - solid_ref[z].astype(F32)
        velocity = [centre[f][z] for f in range(3)]
        sign = 0.5 if z == 0 else -0.5
        px_up, px_down, py_up, py_down = near(3, z)
        press = (0.5 * (px_up - px_down), 0.5 * (py_up - py_down), sign * centre[3][1 - z])
        new = []
        for f in range(3):
            x_up, x_down, y_up, y_down = near(f, z)
            other = centre[f][1 - z]
            advect = (
                velocity[0] * (0.5 * (x_up - x_down))
                + velocity[1] * (0.5 * (y_up - y_down))
                + velocity[2] * (sign * other)
            )
            lap = other + x_up + x_down + y_up + y_down - 6.0 * velocity[f]
            update = velocity[f] + TIME_STEP * (VISCOSITY * lap - advect - press[f])
            new.append(update * fluid)
        results.append(velocity + new + [centre[3][z], fluid])
    return results


def source_kernel(rows, fields_ref, solid_ref, send_ref, rim_ref):
    blocks = send_ref.shape[0]
    lanes = fields_ref.shape[3]
    role = lax.axis_index("grp")
    own = lax.axis_index("gx")
    results = section(rows, fields_ref, solid_ref, None)
    for f in range(4):
        for z in range(2):
            for k, row in ((0, 0), (1, rows - 1)):
                rim_ref[k, 2 * f + z : 2 * f + z + 1, :] = fields_ref[f, z, row : row + 1, :]
    rims = [rim_ref[k] for k in range(2)]
    values = [jnp.concatenate([p.astype(BF16) for p in parts], axis=1) for parts in results]
    pad = jnp.zeros((128 - 2 * rows, 8 * lanes), BF16)
    stacked = jnp.concatenate(values + [pad], axis=0)
    shape = (blocks * 8, 8 * lanes)
    out_row = iota(shape, 0)
    wanted = (out_row & 7) * lanes + (out_row >> 3) + role * blocks
    pick = jnp.where(iota(shape, 1) == wanted, 1.0, 0.0).astype(BF16)
    lines = dot(pick, stacked, NT)
    for b in range(blocks):
        rim = jnp.where(b > own, rims[1], rims[0])
        send_ref[b] = jnp.concatenate([lines[8 * b : 8 * b + 8], rim], axis=0).astype(BF16)


def neighbour_terms(lines, rows):
    cells = lines.shape[1]
    lane = iota((8, cells), 1)
    place = lane & 127
    starts = ((place == 0) | (place == rows)) & (lane >= 128)
    stops = ((place == rows - 1) | (place == 2 * rows - 1)) & (lane < cells - 128)
    hop = 128 - rows + 1
    below = jnp.where(starts, pltpu.roll(lines, hop, 1), 0.0)
    above = jnp.where(stops, pltpu.roll(lines, cells - hop, 1), 0.0)
    slope = 0.5 * (above - below)
    first = jnp.where(iota((8, cells), 0) == 0, slope[6:7, :], 0.0)
    terms = VISCOSITY * (above + below) - lines[0:1, :] * slope - first
    return lines[7:8, :] * (TIME_STEP * terms)


def line_kernel(
    scale_dft, loss_scale, recv_ref, table_ref, small_ref, mix_ref, weight_ref, send_ref, back_ref,
    coef_ref,
):
    blocks = recv_ref.shape[0]
    cells = blocks * 128
    rows = 48
    lines = jnp.concatenate([recv_ref[b, 0:8, :] for b in range(blocks)], axis=1)
    both = table_ref[...]
    lift, proj = small_ref[0:8, :], small_ref[8:16, :]
    lifted = dot(lift, lines, TN).astype(BF16)
    coeffs = dot(both, lifted, NT) * scale_dft
    coeffs16 = coeffs.astype(BF16)
    wide = jnp.concatenate([coeffs16] * 32, axis=1)
    mode_row = iota(wide.shape, 0) & 31
    mode_col = iota(wide.shape, 1) >> 6
    wide = jnp.where(mode_row == mode_col, wide, jnp.zeros_like(wide))
    product = dot(wide, weight_ref[...], NN)
    turned = pltpu.roll(product, 64, 1)
    parts = []
    for line in range(2):
        real = slice(64 * line, 64 * line + 32)
        imag = slice(64 * line + 32, 64 * line + 64)
        parts.append(product[real] - turned[imag])
        parts.append(turned[real] + product[imag])
    mixed = jnp.concatenate(parts, axis=0)
    mixed_t = jnp.transpose(mixed)[0:64].astype(BF16)
    hidden = dot(mixed_t, both, NN) * (2.0 * scale_dft) + dot(mix_ref[...], lifted, TN)
    square = hidden * hidden
    inner = GELU_A * (hidden + GELU_B * (square * hidden))
    tanh = jnp.tanh(inner)
    half = 0.5 * (1.0 + tanh)
    active = (hidden * half).astype(BF16)
    slope = half + (0.5 * GELU_A) * hidden * (1.0 - tanh * tanh) * (1.0 + (3.0 * GELU_B) * square)
    predicted = dot(proj, active, NN)
    wide_lines = lines.astype(F32)
    target = pltpu.roll(wide_lines, 5, 0) + neighbour_terms(wide_lines, rows)
    misfit = (predicted - target) * loss_scale
    misfit = jnp.where(iota(misfit.shape, 0) < 3, misfit, 0.0)
    high = misfit.astype(BF16)
    low = (misfit - high.astype(F32)).astype(BF16)
    back = slope * (dot(proj, high, TN) + dot(proj, low, TN))
    back16 = back.astype(BF16)
    mix_terms = dot(lines, back16, NT)
    back_mixed = dot(both, back16, NT) * (2.0 * scale_dft)
    back_ref[...] = jnp.concatenate([back_mixed[0:64], back_mixed[64:128]], axis=1)
    coef_ref[...] = jnp.concatenate([coeffs[0:64], coeffs[64:128]], axis=1)
    mix_high = mix_terms.astype(BF16)
    mix_low = (mix_terms - mix_high.astype(F32)).astype(BF16)
    tail = jnp.concatenate([mix_high, mix_low], axis=1).astype(F32)[0:4]
    lane = iota((4, 128), 1) & 63
    for j in range(8):
        back_j = back_ref[pl.ds(j, 8, stride=8), :]
        coef_j = coef_ref[pl.ds(j, 8, stride=8), :]
        real, imag = coef_j[0:4], coef_j[4:8]
        halves = (
            jnp.where(lane < 32, real, pltpu.roll(imag, 32, 1)),
            jnp.where(lane < 32, pltpu.roll(real, 96, 1), imag),
        )
        for k, half in enumerate(halves):
            chunk = jnp.concatenate([back_j, half, tail], axis=0).astype(BF16)
            send_ref[4 * j + 2 * k] = chunk
            send_ref[4 * j + 2 * k + 1] = chunk


def grad_kernel(recv_ref, send_ref, wide_ref, grad_ref):
    side = lax.rem(lax.axis_index("gx"), 2)
    blocks, height = recv_ref.shape[:2]
    for b in range(blocks):
        wide_ref[b * height : (b + 1) * height, :] = recv_ref[b].astype(F32)

    def rows(k):
        return wide_ref[pl.ds(k, blocks, stride=height), :]

    lane = iota((32, 128), 1)
    for g in range(4):
        coef = rows(8 + g).astype(BF16)
        by_real = dot(coef, rows(g).astype(BF16), TN)
        by_imag = dot(coef, rows(4 + g).astype(BF16), TN)
        real = [by_real[k : k + 32] + by_imag[k + 32 : k + 64] for k in (0, 64)]
        imag = [by_imag[k : k + 32] - by_real[k + 32 : k + 64] for k in (0, 64)]
        low = real[0] + pltpu.roll(real[1], 64, 1)
        high = pltpu.roll(imag[0], 64, 1) + imag[1]
        grad_ref[g] = jnp.where(lane < 64, low, high)
    mix = []
    for i in range(3):
        total = jnp.sum(rows(12 + i), axis=0, keepdims=True)
        mix.append(total + pltpu.roll(total, 64, 1))
    for g in range(4):
        own = grad_ref[g, pl.ds(side * 16, 16), :]
        for c in range(4):
            k = 4 * g + c
            send_ref[k, 0:4, :] = own[4 * c : 4 * c + 4]
            for i in range(3):
                send_ref[k, 4 + i : 5 + i, :] = mix[i]
            send_ref[k, 7:8, :] = mix[0]


def final_kernel(
    rows, recv_ref, small_ref, fields_ref, solid_ref, lines_ref, grad_ref, mix_ref, new_ref
):
    last = lines_ref.shape[0] - 1
    own = lax.axis_index("gx")
    rims = []
    for index, inside in ((own - 1, own > 0), (own + 1, own < last)):
        message = lines_ref[jnp.minimum(jnp.maximum(index, 0), last)].astype(F32)
        rims.append(jnp.where(inside, message[8:16], 0.0))
    results = section(rows, fields_ref, solid_ref, rims)
    for z in range(2):
        for f in range(3):
            new_ref[f, z] = results[z][3 + f]
    total = recv_ref[0]
    for k in range(1, recv_ref.shape[0]):
        total = total + recv_ref[k]
    grad_ref[...] = total[0:4]
    mix = lax.dot_general(
        small_ref[0:8, :].astype(F32),
        pltpu.roll(total, 4, 0),
        TN,
        precision=lax.Precision.HIGHEST,
        preferred_element_type=F32,
    )
    mix_ref[...] = mix[:, 0:64]


def table_kernel(blocks, rows, mode_ref, table_ref):
    modes = mode_ref.shape[1]
    square = (modes, modes)
    index = jnp.where(iota(square, 0) == iota(square, 1), mode_ref[...].astype(F32), 0.0)
    index = jnp.sum(index, axis=1, keepdims=True).astype(jnp.int32)
    shape = (modes, 128)
    lane = iota(shape, 1)
    unit = 2.0 * math.pi / (blocks * rows)
    outer = unit * (((index * lane) & (blocks - 1)) * rows).astype(F32)
    cell = jnp.where(lane >= rows, lane - rows, lane)
    cell = jnp.where(lane < 2 * rows, cell, 0)
    inner = unit * (index * cell).astype(F32)
    outer_cos, outer_sin = jnp.cos(outer), jnp.sin(outer)
    inner_cos, inner_sin = jnp.cos(inner), jnp.sin(inner)
    planes = [lane < rows, (lane >= rows) & (lane < 2 * rows)]
    factors = [(jnp.where(p, inner_cos, 0.0), jnp.where(p, inner_sin, 0.0)) for p in planes]
    for b in range(blocks):
        cos_b = outer_cos[:, b : b + 1]
        sin_b = outer_sin[:, b : b + 1]
        parts = []
        for cos_c, sin_c in factors:
            parts.append(cos_b * cos_c - sin_b * sin_c)
            parts.append(-(sin_b * cos_c) - cos_b * sin_c)
        table_ref[:, b * 128 : (b + 1) * 128] = jnp.concatenate(parts, axis=0).astype(BF16)


def local(slot_field, solid, lift_weight, spectral_weight, mix_weight, project_weight, mode_index):
    tile = slot_field[0]
    planes, rows, lanes = tile.shape
    blocks = lax.axis_size("gx")
    x_length = rows * blocks
    cell_total = x_length * lanes * lax.axis_size("gy") * planes
    loss_scale = 16.0 / math.sqrt(cell_total)
    scale_dft = 1.0 / math.sqrt(x_length)
    none = jnp.zeros((5, lift_weight.shape[1]), BF16)
    small = jnp.concatenate([lift_weight, none, project_weight.T, none], axis=0)

    def shift(array, axis, step):
        count = lax.axis_size(axis)
        pairs = [(i, i + step) for i in range(count) if 0 <= i + step < count]
        return lax.ppermute(array, axis, pairs)

    edge = jax.ShapeDtypeStruct((planes, lanes), F32)
    right, left = call(edge_kernel, [edge] * 2, tile)
    rims = [shift(right, "gy", 1), shift(left, "gy", -1)]
    rims = jnp.stack(rims + [jnp.zeros_like(right)] * 6, axis=1)
    payload = jnp.concatenate([tile, rims], axis=1)
    table = call(
        lambda *refs: table_kernel(blocks, rows, *refs),
        jax.ShapeDtypeStruct((128, blocks * 128), BF16),
        mode_index.reshape(1, -1),
    )
    payload, table, small = lax.optimization_barrier((payload, table, small))
    fields = lax.all_gather(payload, "grp", axis=0)

    send = call(
        lambda *refs: source_kernel(rows, *refs),
        jax.ShapeDtypeStruct((blocks, 16, 128), BF16),
        fields,
        solid,
        scratch=[pltpu.VMEM((2, 8, lanes), F32)],
    )
    recv = lines = lax.all_to_all(send, "gx", split_axis=0, concat_axis=0, tiled=True)
    send = call(
        lambda *refs: line_kernel(scale_dft, loss_scale, *refs),
        jax.ShapeDtypeStruct((blocks, 16, 128), BF16),
        recv,
        table,
        small,
        mix_weight,
        spectral_weight,
        scratch=[pltpu.VMEM((64, 128), F32), pltpu.VMEM((64, 128), F32)],
    )
    recv = lax.all_to_all(send, "gx", split_axis=0, concat_axis=0, tiled=True)
    send = call(
        grad_kernel,
        jax.ShapeDtypeStruct((16, 8, 128), F32),
        recv,
        scratch=[pltpu.VMEM((blocks * 16, 128), F32), pltpu.VMEM((4, 32, 128), F32)],
    )
    recv = lax.all_to_all(send, ("grp", "gy"), split_axis=0, concat_axis=0, tiled=True)
    spectral_grad, mix_grad, new_velocity = call(
        lambda *refs: final_kernel(rows, *refs),
        [
            jax.ShapeDtypeStruct((4, 128), F32),
            jax.ShapeDtypeStruct((64, 64), F32),
            jax.ShapeDtypeStruct((3, planes, rows, lanes), F32),
        ],
        recv,
        small,
        fields,
        solid,
        lines,
    )
    return new_velocity, spectral_grad, mix_grad


def solution(mesh):
    in_specs = (P("grp", None, "gx", "gy"), P(None, "gx", "gy"), P(), P(), P(), P(), P())
    out_specs = (P(None, None, "gx", "gy"), P(("grp", "gx", "gy"), None), P())
    return jax.shard_map(local, mesh=mesh, in_specs=in_specs, out_specs=out_specs, check_vma=False)
```

```python
import math

import jax
import jax.numpy as jnp
from jax import lax
from jax.experimental import pallas as pl
from jax.experimental.pallas import tpu as pltpu
from jax.sharding import PartitionSpec as P

VISCOSITY = 0.05
TIME_STEP = 0.1
F32 = jnp.float32
BF16 = jnp.bfloat16
GELU_A = math.sqrt(2.0 / math.pi)
GELU_B = 0.044715
VMEM = pl.BlockSpec(memory_space=pltpu.VMEM)
NT = (((1,), (1,)), ((), ()))
NN = (((1,), (0,)), ((), ()))
TN = (((0,), (0,)), ((), ()))


def dot(a, b, dims):
    return lax.dot_general(a, b, dims, preferred_element_type=F32)


def iota(shape, axis):
    return lax.broadcasted_iota(jnp.int32, shape, axis)


def call(kernel, out_shape, *args, scratch=()):
    count = len(out_shape) if isinstance(out_shape, (tuple, list)) else 1
    return pl.pallas_call(
        kernel,
        out_shape=out_shape,
        in_specs=[VMEM] * len(args),
        out_specs=[VMEM] * count if isinstance(out_shape, (tuple, list)) else VMEM,
        scratch_shapes=list(scratch),
        compiler_params=pltpu.CompilerParams(vmem_limit_bytes=40 * 1024 * 1024),
    )(*args)


def as_row(column, shape):
    same = iota(shape, 0) == iota(shape, 1)
    return jnp.sum(jnp.where(same, jnp.broadcast_to(column, shape), 0.0), axis=0, keepdims=True)


def as_column(row, shape):
    same = iota(shape, 0) == iota(shape, 1)
    return jnp.sum(jnp.where(same, jnp.broadcast_to(row, shape), 0.0), axis=1, keepdims=True)


def edge_kernel(tile_ref, solid_ref, first_ref, last_ref):
    rows, lanes = tile_ref.shape[1:]
    shape = (rows, lanes)
    first_ref[...] = jnp.zeros_like(first_ref)
    last = []
    for z in range(2):
        tile = tile_ref[z]
        fluid = 1.0 - solid_ref[z].astype(F32)
        for k, column in enumerate((tile[:, 0:1], tile[:, 1:2], fluid[:, 0:1])):
            first_ref[2 * k + z : 2 * k + z + 1, :] = as_row(column, shape)
        last.append(as_row(tile[:, lanes - 1 : lanes], shape))
    last_ref[...] = jnp.broadcast_to(last[0] + pltpu.roll(last[1], 64, 1), last_ref.shape)


def section(centre, sides, rims, fluids):
    rows, lanes = centre[0][0].shape
    row = iota((rows, lanes), 0)

    def near(f, z):
        tile = centre[f][z]
        below = above = 0.0
        if rims is not None:
            below, above = (rim[2 * f + z : 2 * f + z + 1, :] for rim in rims)
        x_down = jnp.where(row == 0, below, pltpu.roll(tile, 1, 0))
        x_up = jnp.where(row == rows - 1, above, pltpu.roll(tile, rows - 1, 0))
        y_up, y_down = sides[f][z]
        return x_up, x_down, y_up, y_down

    results = []
    for z in range(2):
        velocity = [centre[f][z] for f in range(3)]
        sign = 0.5 if z == 0 else -0.5
        px_up, px_down, py_up, py_down = near(3, z)
        press = (0.5 * (px_up - px_down), 0.5 * (py_up - py_down), sign * centre[3][1 - z])
        new = []
        for f in range(3):
            x_up, x_down, y_up, y_down = near(f, z)
            other = centre[f][1 - z]
            advect = (
                velocity[0] * (0.5 * (x_up - x_down))
                + velocity[1] * (0.5 * (y_up - y_down))
                + velocity[2] * (sign * other)
            )
            lap = other + x_up + x_down + y_up + y_down - 6.0 * velocity[f]
            update = velocity[f] + TIME_STEP * (VISCOSITY * lap - advect - press[f])
            new.append(update * fluids[z])
        results.append(velocity + new + [centre[3][z], fluids[z]])
    return results


def source_kernel(rows, fields_ref, solid_ref, edge_ref, send_ref, rim_ref):
    blocks = send_ref.shape[0]
    lanes = fields_ref.shape[3]
    shape = (rows, lanes)
    lane = iota(shape, 1)
    end = lane == lanes - 1
    role = lax.axis_index("grp")
    own = lax.axis_index("gx")
    last = lax.axis_index("gy") == lax.axis_size("gy") - 1
    centre, sides = [], []
    for f in range(4):
        centre.append([])
        sides.append([])
        for z in range(2):
            tile = fields_ref[f, z, 0:rows, :]
            one, two = (
                as_column(fields_ref[f, z, rows + k : rows + k + 1, :], shape) for k in (0, 1)
            )
            here = jnp.where(end, one, pltpu.roll(tile, lanes - 1, 1))
            above = jnp.where((lane == lanes - 2) & last, 0.0, pltpu.roll(here, lanes - 1, 1))
            centre[f].append(here)
            sides[f].append((jnp.where(end, two, above), jnp.where(end & last, 0.0, tile)))
    fluids = []
    for z in range(2):
        fluid = pltpu.roll(1.0 - solid_ref[z].astype(F32), lanes - 1, 1)
        fluids.append(jnp.where(end, as_column(edge_ref[4 + z : 5 + z, :], shape), fluid))
    results = section(centre, sides, None, fluids)
    for f in range(4):
        for z in range(2):
            for k, row in ((0, 0), (1, rows - 1)):
                rim_ref[k, 2 * f + z : 2 * f + z + 1, :] = fields_ref[f, z, row : row + 1, :]
    rims = [rim_ref[k] for k in range(2)]
    values = [jnp.concatenate([p.astype(BF16) for p in parts], axis=1) for parts in results]
    pad = jnp.zeros((128 - 2 * rows, 8 * lanes), BF16)
    stacked = jnp.concatenate(values + [pad], axis=0)
    shape = (blocks * 8, 8 * lanes)
    out_row = iota(shape, 0)
    wanted = (out_row & 7) * lanes + (out_row >> 3) + role * blocks
    pick = jnp.where(iota(shape, 1) == wanted, 1.0, 0.0).astype(BF16)
    lines = dot(pick, stacked, NT)
    for b in range(blocks):
        rim = jnp.where(b > own, rims[1], rims[0])
        send_ref[b] = jnp.concatenate([lines[8 * b : 8 * b + 8], rim], axis=0).astype(BF16)


def neighbour_terms(lines, rows):
    cells = lines.shape[1]
    lane = iota((8, cells), 1)
    place = lane & 127
    starts = ((place == 0) | (place == rows)) & (lane >= 128)
    stops = ((place == rows - 1) | (place == 2 * rows - 1)) & (lane < cells - 128)
    hop = 128 - rows + 1
    below = jnp.where(starts, pltpu.roll(lines, hop, 1), 0.0)
    above = jnp.where(stops, pltpu.roll(lines, cells - hop, 1), 0.0)
    slope = 0.5 * (above - below)
    first = jnp.where(iota((8, cells), 0) == 0, slope[6:7, :], 0.0)
    terms = VISCOSITY * (above + below) - lines[0:1, :] * slope - first
    return lines[7:8, :] * (TIME_STEP * terms)


def line_kernel(
    scale_dft, loss_scale, recv_ref, table_ref, small_ref, mix_ref, weight_ref, send_ref, back_ref,
    coef_ref,
):
    blocks = recv_ref.shape[0]
    cells = blocks * 128
    rows = 48
    lines = jnp.concatenate([recv_ref[b, 0:8, :] for b in range(blocks)], axis=1)
    both = table_ref[...]
    lift, proj = small_ref[0:8, :], small_ref[8:16, :]
    lifted = dot(lift, lines, TN).astype(BF16)
    coeffs = dot(both, lifted, NT) * scale_dft
    coeffs16 = coeffs.astype(BF16)
    wide = jnp.concatenate([coeffs16] * 32, axis=1)
    mode_row = iota(wide.shape, 0) & 31
    mode_col = iota(wide.shape, 1) >> 6
    wide = jnp.where(mode_row == mode_col, wide, jnp.zeros_like(wide))
    product = dot(wide, weight_ref[...], NN)
    turned = pltpu.roll(product, 64, 1)
    parts = []
    for line in range(2):
        real = slice(64 * line, 64 * line + 32)
        imag = slice(64 * line + 32, 64 * line + 64)
        parts.append(product[real] - turned[imag])
        parts.append(turned[real] + product[imag])
    mixed = jnp.concatenate(parts, axis=0)
    mixed_t = jnp.transpose(mixed)[0:64].astype(BF16)
    hidden = dot(mixed_t, both, NN) * (2.0 * scale_dft) + dot(mix_ref[...], lifted, TN)
    square = hidden * hidden
    inner = GELU_A * (hidden + GELU_B * (square * hidden))
    tanh = jnp.tanh(inner)
    half = 0.5 * (1.0 + tanh)
    active = (hidden * half).astype(BF16)
    slope = half + (0.5 * GELU_A) * hidden * (1.0 - tanh * tanh) * (1.0 + (3.0 * GELU_B) * square)
    predicted = dot(proj, active, NN)
    wide_lines = lines.astype(F32)
    target = pltpu.roll(wide_lines, 5, 0) + neighbour_terms(wide_lines, rows)
    misfit = (predicted - target) * loss_scale
    misfit = jnp.where(iota(misfit.shape, 0) < 3, misfit, 0.0)
    high = misfit.astype(BF16)
    low = (misfit - high.astype(F32)).astype(BF16)
    back = slope * (dot(proj, high, TN) + dot(proj, low, TN))
    back16 = back.astype(BF16)
    mix_terms = dot(lines, back16, NT)
    back_mixed = dot(both, back16, NT) * (2.0 * scale_dft)
    back_ref[...] = jnp.concatenate([back_mixed[0:64], back_mixed[64:128]], axis=1)
    coef_ref[...] = jnp.concatenate([coeffs[0:64], coeffs[64:128]], axis=1)
    mix_high = mix_terms.astype(BF16)
    mix_low = (mix_terms - mix_high.astype(F32)).astype(BF16)
    tail = jnp.concatenate([mix_high, mix_low], axis=1).astype(F32)[0:4]
    lane = iota((4, 128), 1) & 63
    for j in range(8):
        back_j = back_ref[pl.ds(j, 8, stride=8), :]
        coef_j = coef_ref[pl.ds(j, 8, stride=8), :]
        real, imag = coef_j[0:4], coef_j[4:8]
        halves = (
            jnp.where(lane < 32, real, pltpu.roll(imag, 32, 1)),
            jnp.where(lane < 32, pltpu.roll(real, 96, 1), imag),
        )
        for k, half in enumerate(halves):
            chunk = jnp.concatenate([back_j, half, tail], axis=0).astype(BF16)
            send_ref[4 * j + 2 * k] = chunk
            send_ref[4 * j + 2 * k + 1] = chunk


def grad_kernel(recv_ref, last_ref, send_ref, wide_ref, grad_ref):
    side = lax.rem(lax.axis_index("gx"), 2)
    blocks, height = recv_ref.shape[:2]
    for b in range(blocks):
        wide_ref[b * height : (b + 1) * height, :] = recv_ref[b].astype(F32)

    def rows(k):
        return wide_ref[pl.ds(k, blocks, stride=height), :]

    lane = iota((32, 128), 1)
    for g in range(4):
        coef = rows(8 + g).astype(BF16)
        by_real = dot(coef, rows(g).astype(BF16), TN)
        by_imag = dot(coef, rows(4 + g).astype(BF16), TN)
        real = [by_real[k : k + 32] + by_imag[k + 32 : k + 64] for k in (0, 64)]
        imag = [by_imag[k : k + 32] - by_real[k + 32 : k + 64] for k in (0, 64)]
        low = real[0] + pltpu.roll(real[1], 64, 1)
        high = pltpu.roll(imag[0], 64, 1) + imag[1]
        grad_ref[g] = jnp.where(lane < 64, low, high)
    mix = []
    for i in range(3):
        total = jnp.sum(rows(12 + i), axis=0, keepdims=True)
        mix.append(total + pltpu.roll(total, 64, 1))
    for g in range(4):
        own = grad_ref[g, pl.ds(side * 16, 16), :]
        for c in range(4):
            k = 4 * g + c
            send_ref[k, 0:4, :] = own[4 * c : 4 * c + 4]
            for i in range(3):
                send_ref[k, 4 + i : 5 + i, :] = mix[i]
            send_ref[k, 7:8, :] = last_ref[0:1, :]


def final_kernel(
    rows, recv_ref, small_ref, fields_ref, solid_ref, lines_ref, grad_ref, mix_ref, new_ref
):
    lanes = fields_ref.shape[3]
    shape = (rows, lanes)
    lane = iota(shape, 1)
    last = lines_ref.shape[0] - 1
    own = lax.axis_index("gx")
    rims = []
    for index, inside in ((own - 1, own > 0), (own + 1, own < last)):
        message = lines_ref[jnp.minimum(jnp.maximum(index, 0), last)].astype(F32)
        rims.append(jnp.where(inside, message[8:16], 0.0))
    place, count = lax.axis_index("gy"), lax.axis_size("gy")
    centre, sides = [], []
    for f in range(4):
        below = recv_ref[f * count + jnp.maximum(place - 1, 0)][7:8, :]
        below = jnp.where(place > 0, below, 0.0)
        centre.append([fields_ref[f, z, 0:rows, :] for z in range(2)])
        sides.append([])
        for z in range(2):
            above = jnp.where(place < count - 1, fields_ref[f, z, rows : rows + 1, :], 0.0)
            line = below if z == 0 else pltpu.roll(below, 64, 1)
            tile = centre[f][z]
            y_up = jnp.where(
                lane == lanes - 1, as_column(above, shape), pltpu.roll(tile, lanes - 1, 1)
            )
            y_down = jnp.where(lane == 0, as_column(line, shape), pltpu.roll(tile, 1, 1))
            sides[f].append((y_up, y_down))
    fluids = [1.0 - solid_ref[z].astype(F32) for z in range(2)]
    results = section(centre, sides, rims, fluids)
    for z in range(2):
        for f in range(3):
            new_ref[f, z] = results[z][3 + f]
    total = recv_ref[0]
    for k in range(1, recv_ref.shape[0]):
        total = total + recv_ref[k]
    grad_ref[...] = total[0:4]
    mix = lax.dot_general(
        small_ref[0:8, :].astype(F32),
        pltpu.roll(total, 4, 0),
        TN,
        precision=lax.Precision.HIGHEST,
        preferred_element_type=F32,
    )
    mix_ref[...] = mix[:, 0:64]


def table_kernel(blocks, rows, mode_ref, table_ref):
    modes = mode_ref.shape[1]
    square = (modes, modes)
    index = jnp.where(iota(square, 0) == iota(square, 1), mode_ref[...].astype(F32), 0.0)
    index = jnp.sum(index, axis=1, keepdims=True).astype(jnp.int32)
    shape = (modes, 128)
    lane = iota(shape, 1)
    unit = 2.0 * math.pi / (blocks * rows)
    outer = unit * (((index * lane) & (blocks - 1)) * rows).astype(F32)
    cell = jnp.where(lane >= rows, lane - rows, lane)
    cell = jnp.where(lane < 2 * rows, cell, 0)
    inner = unit * (index * cell).astype(F32)
    outer_cos, outer_sin = jnp.cos(outer), jnp.sin(outer)
    inner_cos, inner_sin = jnp.cos(inner), jnp.sin(inner)
    planes = [lane < rows, (lane >= rows) & (lane < 2 * rows)]
    factors = [(jnp.where(p, inner_cos, 0.0), jnp.where(p, inner_sin, 0.0)) for p in planes]
    for b in range(blocks):
        cos_b = outer_cos[:, b : b + 1]
        sin_b = outer_sin[:, b : b + 1]
        parts = []
        for cos_c, sin_c in factors:
            parts.append(cos_b * cos_c - sin_b * sin_c)
            parts.append(-(sin_b * cos_c) - cos_b * sin_c)
        table_ref[:, b * 128 : (b + 1) * 128] = jnp.concatenate(parts, axis=0).astype(BF16)


def local(slot_field, solid, lift_weight, spectral_weight, mix_weight, project_weight, mode_index):
    tile = slot_field[0]
    planes, rows, lanes = tile.shape
    blocks = lax.axis_size("gx")
    x_length = rows * blocks
    cell_total = x_length * lanes * lax.axis_size("gy") * planes
    loss_scale = 16.0 / math.sqrt(cell_total)
    scale_dft = 1.0 / math.sqrt(x_length)
    none = jnp.zeros((5, lift_weight.shape[1]), BF16)
    small = jnp.concatenate([lift_weight, none, project_weight.T, none], axis=0)

    def shift(array, axis, step):
        count = lax.axis_size(axis)
        pairs = [(i, (i + step) % count) for i in range(count)]
        return lax.ppermute(array, axis, pairs)

    edge = jax.ShapeDtypeStruct((8, lanes), F32)
    first, last = call(edge_kernel, [edge] * 2, tile, solid)
    edge = shift(first, "gy", -1)
    rims = jnp.stack([edge[0:2], edge[2:4]] + [jnp.zeros_like(edge[0:2])] * 6, axis=1)
    payload = jnp.concatenate([tile, rims], axis=1)
    table = call(
        lambda *refs: table_kernel(blocks, rows, *refs),
        jax.ShapeDtypeStruct((128, blocks * 128), BF16),
        mode_index.reshape(1, -1),
    )
    payload, table, small = lax.optimization_barrier((payload, table, small))
    fields = lax.all_gather(payload, "grp", axis=0)

    send = call(
        lambda *refs: source_kernel(rows, *refs),
        jax.ShapeDtypeStruct((blocks, 16, 128), BF16),
        fields,
        solid,
        edge,
        scratch=[pltpu.VMEM((2, 8, lanes), F32)],
    )
    recv = lines = lax.all_to_all(send, "gx", split_axis=0, concat_axis=0, tiled=True)
    send = call(
        lambda *refs: line_kernel(scale_dft, loss_scale, *refs),
        jax.ShapeDtypeStruct((blocks, 16, 128), BF16),
        recv,
        table,
        small,
        mix_weight,
        spectral_weight,
        scratch=[pltpu.VMEM((64, 128), F32), pltpu.VMEM((64, 128), F32)],
    )
    recv = lax.all_to_all(send, "gx", split_axis=0, concat_axis=0, tiled=True)
    send = call(
        grad_kernel,
        jax.ShapeDtypeStruct((16, 8, 128), F32),
        recv,
        last,
        scratch=[pltpu.VMEM((blocks * 16, 128), F32), pltpu.VMEM((4, 32, 128), F32)],
    )
    recv = lax.all_to_all(send, ("grp", "gy"), split_axis=0, concat_axis=0, tiled=True)
    spectral_grad, mix_grad, new_velocity = call(
        lambda *refs: final_kernel(rows, *refs),
        [
            jax.ShapeDtypeStruct((4, 128), F32),
            jax.ShapeDtypeStruct((64, 64), F32),
            jax.ShapeDtypeStruct((3, planes, rows, lanes), F32),
        ],
        recv,
        small,
        fields,
        solid,
        lines,
    )
    return new_velocity, spectral_grad, mix_grad


def solution(mesh):
    in_specs = (P("grp", None, "gx", "gy"), P(None, "gx", "gy"), P(), P(), P(), P(), P())
    out_specs = (P(None, None, "gx", "gy"), P(("grp", "gx", "gy"), None), P())
    return jax.shard_map(local, mesh=mesh, in_specs=in_specs, out_specs=out_specs, check_vma=False)
```

```python
import math

import jax
import jax.numpy as jnp
from jax import lax
from jax.experimental import pallas as pl
from jax.experimental.pallas import tpu as pltpu
from jax.sharding import PartitionSpec as P

VISCOSITY = 0.05
TIME_STEP = 0.1
F32 = jnp.float32
BF16 = jnp.bfloat16
GELU_A = math.sqrt(2.0 / math.pi)
GELU_B = 0.044715
VMEM = pl.BlockSpec(memory_space=pltpu.VMEM)
NT = (((1,), (1,)), ((), ()))
NN = (((1,), (0,)), ((), ()))
TN = (((0,), (0,)), ((), ()))


def dot(a, b, dims):
    return lax.dot_general(a, b, dims, preferred_element_type=F32)


def iota(shape, axis):
    return lax.broadcasted_iota(jnp.int32, shape, axis)


def call(kernel, out_shape, *args, scratch=(), space=VMEM, limit=40):
    count = len(out_shape) if isinstance(out_shape, (tuple, list)) else 1
    return pl.pallas_call(
        kernel,
        out_shape=out_shape,
        in_specs=[space] * len(args),
        out_specs=[VMEM] * count if isinstance(out_shape, (tuple, list)) else VMEM,
        scratch_shapes=list(scratch),
        compiler_params=pltpu.CompilerParams(vmem_limit_bytes=limit * 1024 * 1024),
    )(*args)


def as_row(column, shape):
    same = iota(shape, 0) == iota(shape, 1)
    return jnp.sum(jnp.where(same, jnp.broadcast_to(column, shape), 0.0), axis=0, keepdims=True)


def as_column(row, shape):
    same = iota(shape, 0) == iota(shape, 1)
    return jnp.sum(jnp.where(same, jnp.broadcast_to(row, shape), 0.0), axis=1, keepdims=True)


def turned(rows):
    pad = jnp.zeros((128 - rows.shape[0], 128), F32)
    return jnp.transpose(jnp.concatenate([rows, pad], axis=0))


def edge_kernel(tile_hbm, solid_hbm, first_ref, last_ref, tile_ref, solid_ref, sems):
    copies = [
        pltpu.make_async_copy(tile_hbm, tile_ref, sems.at[0]),
        pltpu.make_async_copy(solid_hbm, solid_ref, sems.at[1]),
    ]
    for copy in copies:
        copy.start()
    for copy in copies:
        copy.wait()
    rows, lanes = tile_ref.shape[1:]
    shape = (rows, lanes)
    first_ref[...] = jnp.zeros_like(first_ref)
    last = []
    for z in range(2):
        tile = tile_ref[z]
        fluid = 1.0 - solid_ref[z].astype(F32)
        for k, column in enumerate((tile[:, 0:1], tile[:, 1:2], fluid[:, 0:1])):
            first_ref[2 * k + z : 2 * k + z + 1, :] = as_row(column, shape)
        last.append(as_row(tile[:, lanes - 1 : lanes], shape))
    last_ref[...] = jnp.broadcast_to(last[0] + pltpu.roll(last[1], 64, 1), last_ref.shape)


def section(centre, sides, rims, fluids):
    rows, lanes = centre[0][0].shape
    row = iota((rows, lanes), 0)

    def near(f, z):
        tile = centre[f][z]
        below = above = 0.0
        if rims is not None:
            below, above = (rim[2 * f + z : 2 * f + z + 1, :] for rim in rims)
        x_down = jnp.where(row == 0, below, pltpu.roll(tile, 1, 0))
        x_up = jnp.where(row == rows - 1, above, pltpu.roll(tile, rows - 1, 0))
        y_up, y_down = sides[f][z]
        return x_up, x_down, y_up, y_down

    results = []
    for z in range(2):
        velocity = [centre[f][z] for f in range(3)]
        sign = 0.5 if z == 0 else -0.5
        px_up, px_down, py_up, py_down = near(3, z)
        press = (0.5 * (px_up - px_down), 0.5 * (py_up - py_down), sign * centre[3][1 - z])
        new = []
        for f in range(3):
            x_up, x_down, y_up, y_down = near(f, z)
            other = centre[f][1 - z]
            advect = (
                velocity[0] * (0.5 * (x_up - x_down))
                + velocity[1] * (0.5 * (y_up - y_down))
                + velocity[2] * (sign * other)
            )
            lap = other + x_up + x_down + y_up + y_down - 6.0 * velocity[f]
            update = velocity[f] + TIME_STEP * (VISCOSITY * lap - advect - press[f])
            new.append(update * fluids[z])
        results.append(velocity + new + [centre[3][z], fluids[z]])
    return results


def source_kernel(rows, fields_ref, solid_ref, edge_ref, send_ref, rim_ref):
    blocks = send_ref.shape[0]
    lanes = fields_ref.shape[3]
    shape = (rows, lanes)
    lane = iota(shape, 1)
    end = lane == lanes - 1
    role = lax.axis_index("grp")
    own = lax.axis_index("gx")
    last = lax.axis_index("gy") == lax.axis_size("gy") - 1
    blocks_of = [fields_ref[f, z, rows : rows + 8, :] for f in range(4) for z in range(2)]
    columns = turned(jnp.concatenate(blocks_of, axis=0))[0:rows]
    centre, sides = [], []
    for f in range(4):
        centre.append([])
        sides.append([])
        for z in range(2):
            tile = fields_ref[f, z, 0:rows, :]
            place = 8 * (2 * f + z)
            one = pltpu.roll(columns, lanes - 1 - place, 1)
            two = pltpu.roll(columns, lanes - 2 - place, 1)
            above = jnp.where(lane >= lanes - 2, two, pltpu.roll(tile, lanes - 2, 1))
            above = jnp.where((lane == lanes - 2) & last, 0.0, above)
            centre[f].append(jnp.where(end, one, pltpu.roll(tile, lanes - 1, 1)))
            sides[f].append((above, jnp.where(end & last, 0.0, tile)))
    fluids = []
    for z in range(2):
        fluid = pltpu.roll(1.0 - solid_ref[z].astype(F32), lanes - 1, 1)
        fluids.append(jnp.where(end, as_column(edge_ref[4 + z : 5 + z, :], shape), fluid))
    results = section(centre, sides, None, fluids)
    for f in range(4):
        for z in range(2):
            for k, row in ((0, 0), (1, rows - 1)):
                rim_ref[k, 2 * f + z : 2 * f + z + 1, :] = fields_ref[f, z, row : row + 1, :]
    rims = [rim_ref[k] for k in range(2)]
    values = [jnp.concatenate([p.astype(BF16) for p in parts], axis=1) for parts in results]
    pad = jnp.zeros((128 - 2 * rows, 8 * lanes), BF16)
    stacked = jnp.concatenate(values + [pad], axis=0)
    shape = (blocks * 8, 8 * lanes)
    out_row = iota(shape, 0)
    wanted = (out_row & 7) * lanes + (out_row >> 3) + role * blocks
    pick = jnp.where(iota(shape, 1) == wanted, 1.0, 0.0).astype(BF16)
    lines = dot(pick, stacked, NT)
    for b in range(blocks):
        rim = jnp.where(b > own, rims[1], rims[0])
        send_ref[b] = jnp.concatenate([lines[8 * b : 8 * b + 8], rim], axis=0).astype(BF16)


def neighbour_terms(lines, rows):
    cells = lines.shape[1]
    lane = iota((8, cells), 1)
    place = lane & 127
    starts = ((place == 0) | (place == rows)) & (lane >= 128)
    stops = ((place == rows - 1) | (place == 2 * rows - 1)) & (lane < cells - 128)
    hop = 128 - rows + 1
    below = jnp.where(starts, pltpu.roll(lines, hop, 1), 0.0)
    above = jnp.where(stops, pltpu.roll(lines, cells - hop, 1), 0.0)
    slope = 0.5 * (above - below)
    first = jnp.where(iota((8, cells), 0) == 0, slope[6:7, :], 0.0)
    terms = VISCOSITY * (above + below) - lines[0:1, :] * slope - first
    return lines[7:8, :] * (TIME_STEP * terms)


def line_kernel(
    scale_dft, loss_scale, recv_ref, table_ref, turned_ref, small_ref, mix_ref, weight_ref, send_ref,
    back_ref, coef_ref,
):
    blocks = recv_ref.shape[0]
    rows = 48
    lines = jnp.concatenate([recv_ref[b, 0:8, :] for b in range(blocks)], axis=1)
    both = table_ref[...]
    cells_by_modes = turned_ref[...]
    lift, proj = small_ref[0:8, :], small_ref[8:16, :]
    lifted = dot(lift, lines, TN).astype(BF16)
    coeffs = jnp.transpose(dot(lifted, cells_by_modes, NN) * scale_dft)
    coeffs16 = coeffs.astype(BF16)
    wide = jnp.concatenate([coeffs16] * 32, axis=1)
    mode_row = iota(wide.shape, 0) & 31
    mode_col = iota(wide.shape, 1) >> 6
    wide = jnp.where(mode_row == mode_col, wide, jnp.zeros_like(wide))
    product = dot(wide, weight_ref[...], NN)
    swapped = pltpu.roll(product, 64, 1)
    parts = []
    for line in range(2):
        real = slice(64 * line, 64 * line + 32)
        imag = slice(64 * line + 32, 64 * line + 64)
        parts.append(product[real] - swapped[imag])
        parts.append(swapped[real] + product[imag])
    mixed = jnp.concatenate(parts, axis=0)
    mixed_t = jnp.transpose(mixed)[0:64].astype(BF16)
    hidden = dot(mixed_t, both, NN) * (2.0 * scale_dft) + dot(mix_ref[...], lifted, TN)
    square = hidden * hidden
    tanh = jnp.tanh(hidden * (GELU_A + (GELU_A * GELU_B) * square))
    half = 0.5 + 0.5 * tanh
    active = (hidden * half).astype(BF16)
    rise = 0.5 * GELU_A + (1.5 * GELU_A * GELU_B) * square
    slope = half + hidden * (1.0 - tanh * tanh) * rise
    predicted = dot(proj, active, NN)
    wide_lines = lines.astype(F32)
    target = pltpu.roll(wide_lines, 5, 0) + neighbour_terms(wide_lines, rows)
    misfit = (predicted - target) * loss_scale
    misfit = jnp.where(iota(misfit.shape, 0) < 3, misfit, 0.0)
    high = misfit.astype(BF16).astype(F32)
    parts = jnp.concatenate([high, misfit - high], axis=0).astype(BF16)
    twice = jnp.concatenate([proj.astype(F32)] * 2, axis=0).astype(BF16)
    back16 = (slope * dot(twice, parts, TN)).astype(BF16)
    mix_terms = jnp.transpose(dot(back16, lines, NT))
    back_mixed = jnp.transpose(dot(back16, cells_by_modes, NN)) * (2.0 * scale_dft)
    back_ref[...] = jnp.concatenate([back_mixed[0:64], back_mixed[64:128]], axis=1)
    coef_ref[...] = jnp.concatenate([coeffs[0:64], coeffs[64:128]], axis=1)
    mix_high = mix_terms.astype(BF16)
    mix_low = (mix_terms - mix_high.astype(F32)).astype(BF16)
    tail = jnp.concatenate([mix_high, mix_low], axis=1).astype(F32)[0:4]
    lane = iota((4, 128), 1) & 63
    for j in range(8):
        back_j = back_ref[pl.ds(j, 8, stride=8), :]
        coef_j = coef_ref[pl.ds(j, 8, stride=8), :]
        real, imag = coef_j[0:4], coef_j[4:8]
        halves = (
            jnp.where(lane < 32, real, pltpu.roll(imag, 32, 1)),
            jnp.where(lane < 32, pltpu.roll(real, 96, 1), imag),
        )
        for k, half in enumerate(halves):
            chunk = jnp.concatenate([back_j, half, tail], axis=0).astype(BF16)
            send_ref[4 * j + 2 * k] = chunk
            send_ref[4 * j + 2 * k + 1] = chunk


def grad_kernel(recv_ref, last_ref, send_ref, wide_ref, grad_ref):
    side = lax.rem(lax.axis_index("gx"), 2)
    blocks, height = recv_ref.shape[:2]
    for b in range(blocks):
        wide_ref[b * height : (b + 1) * height, :] = recv_ref[b].astype(F32)

    def rows(k):
        return wide_ref[pl.ds(k, blocks, stride=height), :]

    lane = iota((32, 128), 1)
    for g in range(4):
        coef = rows(8 + g).astype(BF16)
        by_real = dot(coef, rows(g).astype(BF16), TN)
        by_imag = dot(coef, rows(4 + g).astype(BF16), TN)
        real = [by_real[k : k + 32] + by_imag[k + 32 : k + 64] for k in (0, 64)]
        imag = [by_imag[k : k + 32] - by_real[k + 32 : k + 64] for k in (0, 64)]
        low = real[0] + pltpu.roll(real[1], 64, 1)
        high = pltpu.roll(imag[0], 64, 1) + imag[1]
        grad_ref[g] = jnp.where(lane < 64, low, high)
    mix = []
    for i in range(3):
        total = jnp.sum(rows(12 + i), axis=0, keepdims=True)
        mix.append(total + pltpu.roll(total, 64, 1))
    for g in range(4):
        own = grad_ref[g, pl.ds(side * 16, 16), :]
        for c in range(4):
            k = 4 * g + c
            send_ref[k, 0:4, :] = own[4 * c : 4 * c + 4]
            for i in range(3):
                send_ref[k, 4 + i : 5 + i, :] = mix[i]
            send_ref[k, 7:8, :] = last_ref[0:1, :]


def final_kernel(
    rows, recv_ref, small_ref, fields_ref, solid_ref, lines_ref, grad_ref, mix_ref, new_ref
):
    lanes = fields_ref.shape[3]
    shape = (rows, lanes)
    lane = iota(shape, 1)
    last = lines_ref.shape[0] - 1
    own = lax.axis_index("gx")
    rims = []
    for index, inside in ((own - 1, own > 0), (own + 1, own < last)):
        message = lines_ref[jnp.minimum(jnp.maximum(index, 0), last)].astype(F32)
        rims.append(jnp.where(inside, message[8:16], 0.0))
    place, count = lax.axis_index("gy"), lax.axis_size("gy")
    stack = []
    for f in range(4):
        below = recv_ref[f * count + jnp.maximum(place - 1, 0)][7:8, :]
        for z in range(2):
            line = below if z == 0 else pltpu.roll(below, 64, 1)
            block = fields_ref[f, z, rows : rows + 8, :]
            stack.append(jnp.where(iota(block.shape, 0) == 2, line, block))
    columns = turned(jnp.concatenate(stack, axis=0))[0:rows]
    centre, sides = [], []
    for f in range(4):
        centre.append([fields_ref[f, z, 0:rows, :] for z in range(2)])
        sides.append([])
        for z in range(2):
            at = 8 * (2 * f + z)
            tile = centre[f][z]
            edge = jnp.where(place < count - 1, pltpu.roll(columns, lanes - 1 - at, 1), 0.0)
            y_up = jnp.where(lane == lanes - 1, edge, pltpu.roll(tile, lanes - 1, 1))
            edge = pltpu.roll(columns, (lanes - 2 - at) % lanes, 1)
            edge = jnp.where(place > 0, edge, 0.0)
            y_down = jnp.where(lane == 0, edge, pltpu.roll(tile, 1, 1))
            sides[f].append((y_up, y_down))
    fluids = [1.0 - solid_ref[z].astype(F32) for z in range(2)]
    results = section(centre, sides, rims, fluids)
    for z in range(2):
        for f in range(3):
            new_ref[f, z] = results[z][3 + f]
    total = recv_ref[0]
    for k in range(1, recv_ref.shape[0]):
        total = total + recv_ref[k]
    grad_ref[...] = total[0:4]
    mix = lax.dot_general(
        small_ref[0:8, :].astype(F32),
        pltpu.roll(total, 4, 0),
        TN,
        precision=lax.Precision.HIGHEST,
        preferred_element_type=F32,
    )
    mix_ref[...] = mix[:, 0:64]


def table_kernel(blocks, rows, mode_ref, table_ref, turned_ref):
    modes = mode_ref.shape[1]
    unit = 2.0 * math.pi / (blocks * rows)
    along = mode_ref[...].astype(F32)
    along = jnp.concatenate([along] * (128 // modes), axis=1)
    down = jnp.where((iota((128, 128), 0) == iota((128, 128), 1)), along, 0.0)
    down = jnp.sum(down, axis=1, keepdims=True).astype(jnp.int32)
    along = along.astype(jnp.int32)

    def factors(index, axis):
        other = iota((128, 128), 1 - axis)
        kind = iota((128, 128), axis)
        imag = ((kind // modes) & 1) == 1
        outer = unit * (((index * other) & (blocks - 1)) * rows).astype(F32)
        cell = other - jnp.where(kind >= 2 * modes, rows, 0)
        valid = (cell >= 0) & (cell < rows)
        inner = unit * (index * jnp.where(valid, cell, 0)).astype(F32)
        outer_cos, outer_sin = jnp.cos(outer), jnp.sin(outer)
        by_cos = jnp.where(imag, -outer_sin, outer_cos)
        by_sin = jnp.where(imag, -outer_cos, -outer_sin)
        inner_cos = jnp.where(valid, jnp.cos(inner), 0.0)
        inner_sin = jnp.where(valid, jnp.sin(inner), 0.0)
        return by_cos, by_sin, inner_cos, inner_sin

    by_cos, by_sin, inner_cos, inner_sin = factors(down, 0)
    for b in range(blocks):
        block = by_cos[:, b : b + 1] * inner_cos + by_sin[:, b : b + 1] * inner_sin
        table_ref[:, b * 128 : (b + 1) * 128] = block.astype(BF16)
    by_cos, by_sin, inner_cos, inner_sin = factors(along, 1)
    for b in range(blocks):
        block = by_cos[b : b + 1, :] * inner_cos + by_sin[b : b + 1, :] * inner_sin
        turned_ref[b * 128 : (b + 1) * 128, :] = block.astype(BF16)


def local(slot_field, solid, lift_weight, spectral_weight, mix_weight, project_weight, mode_index):
    tile = slot_field[0]
    planes, rows, lanes = tile.shape
    blocks = lax.axis_size("gx")
    x_length = rows * blocks
    cell_total = x_length * lanes * lax.axis_size("gy") * planes
    loss_scale = 16.0 / math.sqrt(cell_total)
    scale_dft = 1.0 / math.sqrt(x_length)
    none = jnp.zeros((5, lift_weight.shape[1]), BF16)
    small = jnp.concatenate([lift_weight, none, project_weight.T, none], axis=0)

    def shift(array, axis, step):
        count = lax.axis_size(axis)
        pairs = [(i, (i + step) % count) for i in range(count)]
        return lax.ppermute(array, axis, pairs)

    edge = jax.ShapeDtypeStruct((8, lanes), F32)
    first, last = call(
        edge_kernel,
        [edge] * 2,
        tile,
        solid,
        scratch=[
            pltpu.VMEM(tile.shape, F32),
            pltpu.VMEM(solid.shape, jnp.int32),
            pltpu.SemaphoreType.DMA((2,)),
        ],
        space=pl.BlockSpec(memory_space=pl.ANY),
        limit=60,
    )
    edge = shift(first, "gy", -1)
    rims = jnp.stack([edge[0:2], edge[2:4]] + [jnp.zeros_like(edge[0:2])] * 6, axis=1)
    payload = jnp.concatenate([tile, rims], axis=1)
    table, cells_by_modes = call(
        lambda *refs: table_kernel(blocks, rows, *refs),
        [
            jax.ShapeDtypeStruct((128, blocks * 128), BF16),
            jax.ShapeDtypeStruct((blocks * 128, 128), BF16),
        ],
        mode_index.reshape(1, -1),
    )
    payload, table, cells_by_modes, small = lax.optimization_barrier(
        (payload, table, cells_by_modes, small)
    )
    fields = lax.all_gather(payload, "grp", axis=0)

    send = call(
        lambda *refs: source_kernel(rows, *refs),
        jax.ShapeDtypeStruct((blocks, 16, 128), BF16),
        fields,
        solid,
        edge,
        scratch=[pltpu.VMEM((2, 8, lanes), F32)],
    )
    recv = lines = lax.all_to_all(send, "gx", split_axis=0, concat_axis=0, tiled=True)
    send = call(
        lambda *refs: line_kernel(scale_dft, loss_scale, *refs),
        jax.ShapeDtypeStruct((blocks, 16, 128), BF16),
        recv,
        table,
        cells_by_modes,
        small,
        mix_weight,
        spectral_weight,
        scratch=[pltpu.VMEM((64, 128), F32), pltpu.VMEM((64, 128), F32)],
    )
    recv = lax.all_to_all(send, "gx", split_axis=0, concat_axis=0, tiled=True)
    send = call(
        grad_kernel,
        jax.ShapeDtypeStruct((16, 8, 128), F32),
        recv,
        last,
        scratch=[pltpu.VMEM((blocks * 16, 128), F32), pltpu.VMEM((4, 32, 128), F32)],
    )
    recv = lax.all_to_all(send, ("grp", "gy"), split_axis=0, concat_axis=0, tiled=True)
    spectral_grad, mix_grad, new_velocity = call(
        lambda *refs: final_kernel(rows, *refs),
        [
            jax.ShapeDtypeStruct((4, 128), F32),
            jax.ShapeDtypeStruct((64, 64), F32),
            jax.ShapeDtypeStruct((3, planes, rows, lanes), F32),
        ],
        recv,
        small,
        fields,
        solid,
        lines,
    )
    return new_velocity, spectral_grad, mix_grad


def solution(mesh):
    in_specs = (P("grp", None, "gx", "gy"), P(None, "gx", "gy"), P(), P(), P(), P(), P())
    out_specs = (P(None, None, "gx", "gy"), P(("grp", "gx", "gy"), None), P())
    return jax.shard_map(local, mesh=mesh, in_specs=in_specs, out_specs=out_specs, check_vma=False)
```

```python
import math

import jax
import jax.numpy as jnp
from jax import lax
from jax.experimental import pallas as pl
from jax.experimental.pallas import tpu as pltpu
from jax.sharding import PartitionSpec as P

VISCOSITY = 0.05
TIME_STEP = 0.1
F32 = jnp.float32
BF16 = jnp.bfloat16
GELU_A = math.sqrt(2.0 / math.pi)
GELU_B = 0.044715
VMEM = pl.BlockSpec(memory_space=pltpu.VMEM)
NT = (((1,), (1,)), ((), ()))
NN = (((1,), (0,)), ((), ()))
TN = (((0,), (0,)), ((), ()))


def dot(a, b, dims):
    return lax.dot_general(a, b, dims, preferred_element_type=F32)


def iota(shape, axis):
    return lax.broadcasted_iota(jnp.int32, shape, axis)


def call(kernel, out_shape, *args, scratch=()):
    count = len(out_shape) if isinstance(out_shape, (tuple, list)) else 1
    return pl.pallas_call(
        kernel,
        out_shape=out_shape,
        in_specs=[VMEM] * len(args),
        out_specs=[VMEM] * count if isinstance(out_shape, (tuple, list)) else VMEM,
        scratch_shapes=list(scratch),
        compiler_params=pltpu.CompilerParams(vmem_limit_bytes=40 * 1024 * 1024),
    )(*args)


def as_row(column, shape):
    same = iota(shape, 0) == iota(shape, 1)
    return jnp.sum(jnp.where(same, jnp.broadcast_to(column, shape), 0.0), axis=0, keepdims=True)


def turned(rows):
    pad = jnp.zeros((128 - rows.shape[0], 128), F32)
    return jnp.transpose(jnp.concatenate([rows, pad], axis=0))


def edge_kernel(fields_ref, solid_ref, edge_ref):
    lanes = fields_ref.shape[3]
    lane = iota(edge_ref.shape, 1)
    edge = jnp.zeros(edge_ref.shape, F32)
    for f in range(4):
        for z in range(2):
            place = 2 * (2 * f + z)
            tile = fields_ref[f, z]
            tile = pltpu.roll(tile, place, 1) if place else tile
            edge = jnp.where((lane >> 1) == 2 * f + z, tile, edge)
    for z in range(2):
        fluid = pltpu.roll(1.0 - solid_ref[z].astype(F32), 16 + z, 1)
        edge = jnp.where(lane == 16 + z, fluid, edge)
    edge_ref[...] = edge


def section(centre, sides, rims, fluids):
    rows, lanes = centre[0][0].shape
    row = iota((rows, lanes), 0)

    def near(f, z):
        tile = centre[f][z]
        below = above = 0.0
        if rims is not None:
            below, above = (rim[2 * f + z : 2 * f + z + 1, :] for rim in rims)
        x_down = jnp.where(row == 0, below, pltpu.roll(tile, 1, 0))
        x_up = jnp.where(row == rows - 1, above, pltpu.roll(tile, rows - 1, 0))
        y_up, y_down = sides[f][z]
        return x_up, x_down, y_up, y_down

    results = []
    for z in range(2):
        velocity = [centre[f][z] for f in range(3)]
        sign = 0.5 if z == 0 else -0.5
        px_up, px_down, py_up, py_down = near(3, z)
        press = (0.5 * (px_up - px_down), 0.5 * (py_up - py_down), sign * centre[3][1 - z])
        new = []
        for f in range(3):
            x_up, x_down, y_up, y_down = near(f, z)
            other = centre[f][1 - z]
            advect = (
                velocity[0] * (0.5 * (x_up - x_down))
                + velocity[1] * (0.5 * (y_up - y_down))
                + velocity[2] * (sign * other)
            )
            lap = other + x_up + x_down + y_up + y_down - 6.0 * velocity[f]
            update = velocity[f] + TIME_STEP * (VISCOSITY * lap - advect - press[f])
            new.append(update * fluids[z])
        results.append(velocity + new + [centre[3][z], fluids[z]])
    return results


def source_kernel(fields_ref, solid_ref, edge_ref, send_ref, rim_ref):
    blocks = send_ref.shape[0]
    rows, lanes = fields_ref.shape[2:]
    lane = iota((rows, lanes), 1)
    end = lane == lanes - 1
    role = lax.axis_index("grp")
    own = lax.axis_index("gx")
    last = lax.axis_index("gy") == lax.axis_size("gy") - 1
    columns = edge_ref[...]
    centre, sides = [], []
    for f in range(4):
        centre.append([])
        sides.append([])
        for z in range(2):
            tile = fields_ref[f, z]
            place = 2 * (2 * f + z)
            one = pltpu.roll(columns, lanes - 1 - place, 1)
            two = pltpu.roll(columns, lanes - 2 - place, 1)
            above = jnp.where(lane >= lanes - 2, two, pltpu.roll(tile, lanes - 2, 1))
            above = jnp.where((lane == lanes - 2) & last, 0.0, above)
            centre[f].append(jnp.where(end, one, pltpu.roll(tile, lanes - 1, 1)))
            sides[f].append((above, jnp.where(end & last, 0.0, tile)))
    fluids = []
    for z in range(2):
        fluid = pltpu.roll(1.0 - solid_ref[z].astype(F32), lanes - 1, 1)
        fluids.append(jnp.where(end, pltpu.roll(columns, lanes - 17 - z, 1), fluid))
    results = section(centre, sides, None, fluids)
    for f in range(4):
        for z in range(2):
            for k, row in ((0, 0), (1, rows - 1)):
                rim_ref[k, 2 * f + z : 2 * f + z + 1, :] = fields_ref[f, z, row : row + 1, :]
    rims = [rim_ref[k] for k in range(2)]
    values = [jnp.concatenate([p.astype(BF16) for p in parts], axis=1) for parts in results]
    pad = jnp.zeros((128 - 2 * rows, 8 * lanes), BF16)
    stacked = jnp.concatenate(values + [pad], axis=0)
    shape = (blocks * 8, 8 * lanes)
    out_row = iota(shape, 0)
    wanted = (out_row & 7) * lanes + (out_row >> 3) + role * blocks
    pick = jnp.where(iota(shape, 1) == wanted, 1.0, 0.0).astype(BF16)
    lines = dot(pick, stacked, NT)
    for b in range(blocks):
        rim = jnp.where(b > own, rims[1], rims[0])
        send_ref[b] = jnp.concatenate([lines[8 * b : 8 * b + 8], rim], axis=0).astype(BF16)


def neighbour_terms(lines, rows):
    cells = lines.shape[1]
    lane = iota((8, cells), 1)
    place = lane & 127
    starts = ((place == 0) | (place == rows)) & (lane >= 128)
    stops = ((place == rows - 1) | (place == 2 * rows - 1)) & (lane < cells - 128)
    hop = 128 - rows + 1
    below = jnp.where(starts, pltpu.roll(lines, hop, 1), 0.0)
    above = jnp.where(stops, pltpu.roll(lines, cells - hop, 1), 0.0)
    slope = 0.5 * (above - below)
    first = jnp.where(iota((8, cells), 0) == 0, slope[6:7, :], 0.0)
    terms = VISCOSITY * (above + below) - lines[0:1, :] * slope - first
    return lines[7:8, :] * (TIME_STEP * terms)


def line_kernel(
    scale_dft, loss_scale, recv_ref, table_ref, turned_ref, small_ref, mix_ref, weight_ref, send_ref,
    back_ref, coef_ref,
):
    blocks = recv_ref.shape[0]
    rows = 48
    lines = jnp.concatenate([recv_ref[b, 0:8, :] for b in range(blocks)], axis=1)
    both = table_ref[...]
    cells_by_modes = turned_ref[...]
    lift, proj = small_ref[0:8, :], small_ref[8:16, :]
    lifted = dot(lift, lines, TN).astype(BF16)
    coeffs = jnp.transpose(dot(lifted, cells_by_modes, NN) * scale_dft)
    coeffs16 = coeffs.astype(BF16)
    wide = jnp.concatenate([coeffs16] * 32, axis=1)
    mode_row = iota(wide.shape, 0) & 31
    mode_col = iota(wide.shape, 1) >> 6
    wide = jnp.where(mode_row == mode_col, wide, jnp.zeros_like(wide))
    product = dot(wide, weight_ref[...], NN)
    swapped = pltpu.roll(product, 64, 1)
    parts = []
    for line in range(2):
        real = slice(64 * line, 64 * line + 32)
        imag = slice(64 * line + 32, 64 * line + 64)
        parts.append(product[real] - swapped[imag])
        parts.append(swapped[real] + product[imag])
    mixed = jnp.concatenate(parts, axis=0)
    mixed_t = jnp.transpose(mixed)[0:64].astype(BF16)
    hidden = dot(mixed_t, both, NN) * (2.0 * scale_dft) + dot(mix_ref[...], lifted, TN)
    square = hidden * hidden
    tanh = jnp.tanh(hidden * (GELU_A + (GELU_A * GELU_B) * square))
    half = 0.5 + 0.5 * tanh
    active = (hidden * half).astype(BF16)
    rise = 0.5 * GELU_A + (1.5 * GELU_A * GELU_B) * square
    slope = half + hidden * (1.0 - tanh * tanh) * rise
    predicted = dot(proj, active, NN)
    wide_lines = lines.astype(F32)
    target = pltpu.roll(wide_lines, 5, 0) + neighbour_terms(wide_lines, rows)
    misfit = (predicted - target) * loss_scale
    misfit = jnp.where(iota(misfit.shape, 0) < 3, misfit, 0.0)
    high = misfit.astype(BF16).astype(F32)
    parts = jnp.concatenate([high, misfit - high], axis=0).astype(BF16)
    twice = jnp.concatenate([proj.astype(F32)] * 2, axis=0).astype(BF16)
    back16 = (slope * dot(twice, parts, TN)).astype(BF16)
    mix_terms = jnp.transpose(dot(back16, lines, NT))
    back_mixed = jnp.transpose(dot(back16, cells_by_modes, NN)) * (2.0 * scale_dft)
    back_ref[...] = jnp.concatenate([back_mixed[0:64], back_mixed[64:128]], axis=1)
    coef_ref[...] = jnp.concatenate([coeffs[0:64], coeffs[64:128]], axis=1)
    mix_high = mix_terms.astype(BF16)
    mix_low = (mix_terms - mix_high.astype(F32)).astype(BF16)
    tail = jnp.concatenate([mix_high, mix_low], axis=1).astype(F32)[0:4]
    lane = iota((4, 128), 1) & 63
    for j in range(8):
        back_j = back_ref[pl.ds(j, 8, stride=8), :]
        coef_j = coef_ref[pl.ds(j, 8, stride=8), :]
        real, imag = coef_j[0:4], coef_j[4:8]
        halves = (
            jnp.where(lane < 32, real, pltpu.roll(imag, 32, 1)),
            jnp.where(lane < 32, pltpu.roll(real, 96, 1), imag),
        )
        for k, half in enumerate(halves):
            chunk = jnp.concatenate([back_j, half, tail], axis=0).astype(BF16)
            send_ref[4 * j + 2 * k] = chunk
            send_ref[4 * j + 2 * k + 1] = chunk


def grad_kernel(recv_ref, last_ref, send_ref, wide_ref, grad_ref):
    side = lax.rem(lax.axis_index("gx"), 2)
    blocks, height = recv_ref.shape[:2]
    for b in range(blocks):
        wide_ref[b * height : (b + 1) * height, :] = recv_ref[b].astype(F32)

    def rows(k):
        return wide_ref[pl.ds(k, blocks, stride=height), :]

    lane = iota((32, 128), 1)
    for g in range(4):
        coef = rows(8 + g).astype(BF16)
        by_real = dot(coef, rows(g).astype(BF16), TN)
        by_imag = dot(coef, rows(4 + g).astype(BF16), TN)
        real = [by_real[k : k + 32] + by_imag[k + 32 : k + 64] for k in (0, 64)]
        imag = [by_imag[k : k + 32] - by_real[k + 32 : k + 64] for k in (0, 64)]
        low = real[0] + pltpu.roll(real[1], 64, 1)
        high = pltpu.roll(imag[0], 64, 1) + imag[1]
        grad_ref[g] = jnp.where(lane < 64, low, high)
    mix = []
    for i in range(3):
        total = jnp.sum(rows(12 + i), axis=0, keepdims=True)
        mix.append(total + pltpu.roll(total, 64, 1))
    for g in range(4):
        own = grad_ref[g, pl.ds(side * 16, 16), :]
        for c in range(4):
            k = 4 * g + c
            send_ref[k, 0:4, :] = own[4 * c : 4 * c + 4]
            for i in range(3):
                send_ref[k, 4 + i : 5 + i, :] = mix[i]
            send_ref[k, 7:8, :] = last_ref[0:1, :]


def final_kernel(
    recv_ref, small_ref, fields_ref, solid_ref, edge_ref, lines_ref, grad_ref, mix_ref, new_ref
):
    rows, lanes = fields_ref.shape[2:]
    lane = iota((rows, lanes), 1)
    last = lines_ref.shape[0] - 1
    own = lax.axis_index("gx")
    rims = []
    for index, inside in ((own - 1, own > 0), (own + 1, own < last)):
        message = lines_ref[jnp.minimum(jnp.maximum(index, 0), last)].astype(F32)
        rims.append(jnp.where(inside, message[8:16], 0.0))
    place, count = lax.axis_index("gy"), lax.axis_size("gy")
    stack = []
    for f in range(4):
        below = recv_ref[f * count + jnp.maximum(place - 1, 0)][7:8, :]
        stack += [below, pltpu.roll(below, 64, 1)]
    lower = jnp.where(place > 0, turned(jnp.concatenate(stack, axis=0))[0:rows], 0.0)
    upper = jnp.where(place < count - 1, edge_ref[...], 0.0)
    centre, sides = [], []
    for f in range(4):
        centre.append([fields_ref[f, z] for z in range(2)])
        sides.append([])
        for z in range(2):
            at = 2 * f + z
            tile = centre[f][z]
            edge = pltpu.roll(upper, lanes - 1 - 2 * at, 1)
            y_up = jnp.where(lane == lanes - 1, edge, pltpu.roll(tile, lanes - 1, 1))
            edge = pltpu.roll(lower, lanes - at, 1) if at else lower
            y_down = jnp.where(lane == 0, edge, pltpu.roll(tile, 1, 1))
            sides[f].append((y_up, y_down))
    fluids = [1.0 - solid_ref[z].astype(F32) for z in range(2)]
    results = section(centre, sides, rims, fluids)
    for z in range(2):
        for f in range(3):
            new_ref[f, z] = results[z][3 + f]
    total = recv_ref[0]
    for k in range(1, recv_ref.shape[0]):
        total = total + recv_ref[k]
    grad_ref[...] = total[0:4]
    mix = lax.dot_general(
        small_ref[0:8, :].astype(F32),
        pltpu.roll(total, 4, 0),
        TN,
        precision=lax.Precision.HIGHEST,
        preferred_element_type=F32,
    )
    mix_ref[...] = mix[:, 0:64]


def table_kernel(blocks, mode_ref, tile_ref, table_ref, turned_ref, last_ref):
    rows, lanes = tile_ref.shape[1:]
    ends = [as_row(tile_ref[z, :, lanes - 1 : lanes], (rows, lanes)) for z in range(2)]
    last_ref[...] = jnp.broadcast_to(ends[0] + pltpu.roll(ends[1], 64, 1), last_ref.shape)
    modes = mode_ref.shape[1]
    unit = 2.0 * math.pi / (blocks * rows)
    square = (modes, modes)
    index = jnp.where(iota(square, 0) == iota(square, 1), mode_ref[...].astype(F32), 0.0)
    index = jnp.sum(index, axis=1, keepdims=True).astype(jnp.int32)
    lane = iota((modes, 128), 1)
    outer = unit * (((index * lane) & (blocks - 1)) * rows).astype(F32)
    cell = jnp.where(lane >= rows, lane - rows, lane)
    inner = unit * (index * jnp.where(lane < 2 * rows, cell, 0)).astype(F32)
    outer_cos, outer_sin = jnp.cos(outer), jnp.sin(outer)
    inner_cos, inner_sin = jnp.cos(inner), jnp.sin(inner)
    by_cos = jnp.concatenate([outer_cos, -outer_sin] * 2, axis=0)
    by_sin = jnp.concatenate([-outer_sin, -outer_cos] * 2, axis=0)
    low = iota((128, 128), 0) < 2 * modes
    lane = iota((128, 128), 1)
    start = jnp.where(low, 0, rows)
    valid = (lane >= start) & (lane < start + rows)
    inner_cos = jnp.where(valid, jnp.concatenate([inner_cos] * 4, axis=0), 0.0)
    inner_sin = jnp.where(valid, jnp.concatenate([inner_sin] * 4, axis=0), 0.0)
    for b in range(blocks):
        block = by_cos[:, b : b + 1] * inner_cos + by_sin[:, b : b + 1] * inner_sin
        table_ref[:, b * 128 : (b + 1) * 128] = block.astype(BF16)
    by_cos, by_sin = jnp.transpose(by_cos), jnp.transpose(by_sin)
    inner_cos, inner_sin = jnp.transpose(inner_cos), jnp.transpose(inner_sin)
    for b in range(blocks):
        block = by_cos[b : b + 1, :] * inner_cos + by_sin[b : b + 1, :] * inner_sin
        turned_ref[b * 128 : (b + 1) * 128, :] = block.astype(BF16)


def local(slot_field, solid, lift_weight, spectral_weight, mix_weight, project_weight, mode_index):
    tile = slot_field[0]
    planes, rows, lanes = tile.shape
    blocks = lax.axis_size("gx")
    x_length = rows * blocks
    cell_total = x_length * lanes * lax.axis_size("gy") * planes
    loss_scale = 16.0 / math.sqrt(cell_total)
    scale_dft = 1.0 / math.sqrt(x_length)
    none = jnp.zeros((5, lift_weight.shape[1]), BF16)
    small = jnp.concatenate([lift_weight, none, project_weight.T, none], axis=0)

    def shift(array, axis, step):
        count = lax.axis_size(axis)
        pairs = [(i, (i + step) % count) for i in range(count)]
        return lax.ppermute(array, axis, pairs)

    fields = lax.all_gather(slot_field, "grp", axis=0, tiled=True)
    edge = call(edge_kernel, jax.ShapeDtypeStruct((rows, lanes), F32), fields, solid)
    edge = shift(edge, "gy", -1)
    table, cells_by_modes, last = call(
        lambda *refs: table_kernel(blocks, *refs),
        [
            jax.ShapeDtypeStruct((128, blocks * 128), BF16),
            jax.ShapeDtypeStruct((blocks * 128, 128), BF16),
            jax.ShapeDtypeStruct((8, lanes), F32),
        ],
        mode_index.reshape(1, -1),
        tile,
    )
    edge, table, cells_by_modes, last, small = lax.optimization_barrier(
        (edge, table, cells_by_modes, last, small)
    )
    send = call(
        source_kernel,
        jax.ShapeDtypeStruct((blocks, 16, 128), BF16),
        fields,
        solid,
        edge,
        scratch=[pltpu.VMEM((2, 8, lanes), F32)],
    )
    recv = lines = lax.all_to_all(send, "gx", split_axis=0, concat_axis=0, tiled=True)
    send = call(
        lambda *refs: line_kernel(scale_dft, loss_scale, *refs),
        jax.ShapeDtypeStruct((blocks, 16, 128), BF16),
        recv,
        table,
        cells_by_modes,
        small,
        mix_weight,
        spectral_weight,
        scratch=[pltpu.VMEM((64, 128), F32), pltpu.VMEM((64, 128), F32)],
    )
    recv = lax.all_to_all(send, "gx", split_axis=0, concat_axis=0, tiled=True)
    send = call(
        grad_kernel,
        jax.ShapeDtypeStruct((16, 8, 128), F32),
        recv,
        last,
        scratch=[pltpu.VMEM((blocks * 16, 128), F32), pltpu.VMEM((4, 32, 128), F32)],
    )
    recv = lax.all_to_all(send, ("grp", "gy"), split_axis=0, concat_axis=0, tiled=True)
    spectral_grad, mix_grad, new_velocity = call(
        final_kernel,
        [
            jax.ShapeDtypeStruct((4, 128), F32),
            jax.ShapeDtypeStruct((64, 64), F32),
            jax.ShapeDtypeStruct((3, planes, rows, lanes), F32),
        ],
        recv,
        small,
        fields,
        solid,
        edge,
        lines,
    )
    return new_velocity, spectral_grad, mix_grad


def solution(mesh):
    in_specs = (P("grp", None, "gx", "gy"), P(None, "gx", "gy"), P(), P(), P(), P(), P())
    out_specs = (P(None, None, "gx", "gy"), P(("grp", "gx", "gy"), None), P())
    return jax.shard_map(local, mesh=mesh, in_specs=in_specs, out_specs=out_specs, check_vma=False)
```

```python
import math

import jax
import jax.numpy as jnp
from jax import lax
from jax.experimental import pallas as pl
from jax.experimental.pallas import tpu as pltpu
from jax.sharding import PartitionSpec as P

VISCOSITY = 0.05
TIME_STEP = 0.1
F32 = jnp.float32
BF16 = jnp.bfloat16
GELU_A = math.sqrt(2.0 / math.pi)
GELU_B = 0.044715
VMEM = pl.BlockSpec(memory_space=pltpu.VMEM)
NT = (((1,), (1,)), ((), ()))
NN = (((1,), (0,)), ((), ()))
TN = (((0,), (0,)), ((), ()))


def dot(a, b, dims):
    return lax.dot_general(a, b, dims, preferred_element_type=F32)


def iota(shape, axis):
    return lax.broadcasted_iota(jnp.int32, shape, axis)


def call(kernel, out_shape, *args, scratch=()):
    count = len(out_shape) if isinstance(out_shape, (tuple, list)) else 1
    return pl.pallas_call(
        kernel,
        out_shape=out_shape,
        in_specs=[VMEM] * len(args),
        out_specs=[VMEM] * count if isinstance(out_shape, (tuple, list)) else VMEM,
        scratch_shapes=list(scratch),
        compiler_params=pltpu.CompilerParams(vmem_limit_bytes=40 * 1024 * 1024),
    )(*args)


def as_row(column, shape):
    same = iota(shape, 0) == iota(shape, 1)
    return jnp.sum(jnp.where(same, jnp.broadcast_to(column, shape), 0.0), axis=0, keepdims=True)


def turned(rows):
    pad = jnp.zeros((128 - rows.shape[0], 128), F32)
    return jnp.transpose(jnp.concatenate([rows, pad], axis=0))


def edge_kernel(fields_ref, solid_ref, edge_ref, low_ref, high_ref):
    rows, lanes = fields_ref.shape[2:]
    lane = iota(edge_ref.shape, 1)
    edge = jnp.zeros(edge_ref.shape, F32)
    for f in range(4):
        for z in range(2):
            place = 2 * (2 * f + z)
            tile = fields_ref[f, z]
            tile = pltpu.roll(tile, place, 1) if place else tile
            edge = jnp.where((lane >> 1) == 2 * f + z, tile, edge)
            low_ref[2 * f + z : 2 * f + z + 1, :] = fields_ref[f, z, 0:1, :]
            high_ref[2 * f + z : 2 * f + z + 1, :] = fields_ref[f, z, rows - 1 : rows, :]
    for z in range(2):
        fluid = pltpu.roll(1.0 - solid_ref[z].astype(F32), 16 + z, 1)
        edge = jnp.where(lane == 16 + z, fluid, edge)
    edge_ref[...] = edge


def section(centre, sides, rims, fluids):
    rows, lanes = centre[0][0].shape
    row = iota((rows, lanes), 0)

    def near(f, z):
        tile = centre[f][z]
        below = above = 0.0
        if rims is not None:
            below, above = (rim[2 * f + z : 2 * f + z + 1, :] for rim in rims)
        x_down = jnp.where(row == 0, below, pltpu.roll(tile, 1, 0))
        x_up = jnp.where(row == rows - 1, above, pltpu.roll(tile, rows - 1, 0))
        y_up, y_down = sides[f][z]
        return x_up, x_down, y_up, y_down

    results = []
    for z in range(2):
        velocity = [centre[f][z] for f in range(3)]
        sign = 0.5 if z == 0 else -0.5
        px_up, px_down, py_up, py_down = near(3, z)
        press = (0.5 * (px_up - px_down), 0.5 * (py_up - py_down), sign * centre[3][1 - z])
        new = []
        for f in range(3):
            x_up, x_down, y_up, y_down = near(f, z)
            other = centre[f][1 - z]
            advect = (
                velocity[0] * (0.5 * (x_up - x_down))
                + velocity[1] * (0.5 * (y_up - y_down))
                + velocity[2] * (sign * other)
            )
            lap = other + x_up + x_down + y_up + y_down - 6.0 * velocity[f]
            update = velocity[f] + TIME_STEP * (VISCOSITY * lap - advect - press[f])
            new.append(update * fluids[z])
        results.append(velocity + new + [centre[3][z], fluids[z]])
    return results


def source_kernel(fields_ref, solid_ref, edge_ref, send_ref):
    blocks = send_ref.shape[0] // 8
    rows, lanes = fields_ref.shape[2:]
    lane = iota((rows, lanes), 1)
    end = lane == lanes - 1
    role = lax.axis_index("grp")
    last = lax.axis_index("gy") == lax.axis_size("gy") - 1
    columns = edge_ref[...]
    centre, sides = [], []
    for f in range(4):
        centre.append([])
        sides.append([])
        for z in range(2):
            tile = fields_ref[f, z]
            place = 2 * (2 * f + z)
            one = pltpu.roll(columns, lanes - 1 - place, 1)
            two = pltpu.roll(columns, lanes - 2 - place, 1)
            above = jnp.where(lane >= lanes - 2, two, pltpu.roll(tile, lanes - 2, 1))
            above = jnp.where((lane == lanes - 2) & last, 0.0, above)
            centre[f].append(jnp.where(end, one, pltpu.roll(tile, lanes - 1, 1)))
            sides[f].append((above, jnp.where(end & last, 0.0, tile)))
    fluids = []
    for z in range(2):
        fluid = pltpu.roll(1.0 - solid_ref[z].astype(F32), lanes - 1, 1)
        fluids.append(jnp.where(end, pltpu.roll(columns, lanes - 17 - z, 1), fluid))
    results = section(centre, sides, None, fluids)
    values = [jnp.concatenate([p.astype(BF16) for p in parts], axis=1) for parts in results]
    pad = jnp.zeros((128 - 2 * rows, 8 * lanes), BF16)
    stacked = jnp.concatenate(values + [pad], axis=0)
    shape = (blocks * 8, 8 * lanes)
    out_row = iota(shape, 0)
    wanted = (out_row & 7) * lanes + (out_row >> 3) + role * blocks
    pick = jnp.where(iota(shape, 1) == wanted, 1.0, 0.0).astype(BF16)
    lines = dot(pick, stacked, NT)
    send_ref[...] = lines.astype(BF16)


def neighbour_terms(lines, rows):
    cells = lines.shape[1]
    lane = iota((8, cells), 1)
    place = lane & 127
    starts = ((place == 0) | (place == rows)) & (lane >= 128)
    stops = ((place == rows - 1) | (place == 2 * rows - 1)) & (lane < cells - 128)
    hop = 128 - rows + 1
    below = jnp.where(starts, pltpu.roll(lines, hop, 1), 0.0)
    above = jnp.where(stops, pltpu.roll(lines, cells - hop, 1), 0.0)
    slope = 0.5 * (above - below)
    first = jnp.where(iota((8, cells), 0) == 0, slope[6:7, :], 0.0)
    terms = VISCOSITY * (above + below) - lines[0:1, :] * slope - first
    return lines[7:8, :] * (TIME_STEP * terms)


def line_kernel(
    scale_dft, loss_scale, recv_ref, table_ref, turned_ref, small_ref, mix_ref, weight_ref, send_ref,
    back_ref, coef_ref,
):
    blocks = recv_ref.shape[0]
    rows = 48
    lines = jnp.concatenate([recv_ref[b, 0:8, :] for b in range(blocks)], axis=1)
    both = table_ref[...]
    cells_by_modes = turned_ref[...]
    lift, proj = small_ref[0:8, :], small_ref[8:16, :]
    lifted = dot(lift, lines, TN).astype(BF16)
    coeffs = jnp.transpose(dot(lifted, cells_by_modes, NN) * scale_dft)
    coeffs16 = coeffs.astype(BF16)
    wide = jnp.concatenate([coeffs16] * 32, axis=1)
    mode_row = iota(wide.shape, 0) & 31
    mode_col = iota(wide.shape, 1) >> 6
    wide = jnp.where(mode_row == mode_col, wide, jnp.zeros_like(wide))
    product = dot(wide, weight_ref[...], NN)
    swapped = pltpu.roll(product, 64, 1)
    parts = []
    for line in range(2):
        real = slice(64 * line, 64 * line + 32)
        imag = slice(64 * line + 32, 64 * line + 64)
        parts.append(product[real] - swapped[imag])
        parts.append(swapped[real] + product[imag])
    mixed = jnp.concatenate(parts, axis=0)
    mixed_t = jnp.transpose(mixed)[0:64].astype(BF16)
    hidden = dot(mixed_t, both, NN) * (2.0 * scale_dft) + dot(mix_ref[...], lifted, TN)
    square = hidden * hidden
    tanh = jnp.tanh(hidden * (GELU_A + (GELU_A * GELU_B) * square))
    half = 0.5 + 0.5 * tanh
    active = (hidden * half).astype(BF16)
    rise = 0.5 * GELU_A + (1.5 * GELU_A * GELU_B) * square
    slope = half + hidden * (1.0 - tanh * tanh) * rise
    predicted = dot(proj, active, NN)
    wide_lines = lines.astype(F32)
    target = pltpu.roll(wide_lines, 5, 0) + neighbour_terms(wide_lines, rows)
    misfit = (predicted - target) * loss_scale
    misfit = jnp.where(iota(misfit.shape, 0) < 3, misfit, 0.0)
    high = misfit.astype(BF16).astype(F32)
    parts = jnp.concatenate([high, misfit - high], axis=0).astype(BF16)
    twice = jnp.concatenate([proj.astype(F32)] * 2, axis=0).astype(BF16)
    back16 = (slope * dot(twice, parts, TN)).astype(BF16)
    mix_terms = jnp.transpose(dot(back16, lines, NT))
    back_mixed = jnp.transpose(dot(back16, cells_by_modes, NN)) * (2.0 * scale_dft)
    back_ref[...] = jnp.concatenate([back_mixed[0:64], back_mixed[64:128]], axis=1)
    coef_ref[...] = jnp.concatenate([coeffs[0:64], coeffs[64:128]], axis=1)
    mix_high = mix_terms.astype(BF16)
    mix_low = (mix_terms - mix_high.astype(F32)).astype(BF16)
    tail = jnp.concatenate([mix_high, mix_low], axis=1).astype(F32)[0:4]
    lane = iota((4, 128), 1) & 63
    for j in range(8):
        back_j = back_ref[pl.ds(j, 8, stride=8), :]
        coef_j = coef_ref[pl.ds(j, 8, stride=8), :]
        real, imag = coef_j[0:4], coef_j[4:8]
        halves = (
            jnp.where(lane < 32, real, pltpu.roll(imag, 32, 1)),
            jnp.where(lane < 32, pltpu.roll(real, 96, 1), imag),
        )
        for k, half in enumerate(halves):
            chunk = jnp.concatenate([back_j, half, tail], axis=0).astype(BF16)
            send_ref[4 * j + 2 * k] = chunk
            send_ref[4 * j + 2 * k + 1] = chunk


def grad_kernel(recv_ref, last_ref, send_ref, wide_ref, grad_ref):
    side = lax.rem(lax.axis_index("gx"), 2)
    blocks, height = recv_ref.shape[:2]
    for b in range(blocks):
        wide_ref[b * height : (b + 1) * height, :] = recv_ref[b].astype(F32)

    def rows(k):
        return wide_ref[pl.ds(k, blocks, stride=height), :]

    lane = iota((32, 128), 1)
    for g in range(4):
        coef = rows(8 + g).astype(BF16)
        by_real = dot(coef, rows(g).astype(BF16), TN)
        by_imag = dot(coef, rows(4 + g).astype(BF16), TN)
        real = [by_real[k : k + 32] + by_imag[k + 32 : k + 64] for k in (0, 64)]
        imag = [by_imag[k : k + 32] - by_real[k + 32 : k + 64] for k in (0, 64)]
        low = real[0] + pltpu.roll(real[1], 64, 1)
        high = pltpu.roll(imag[0], 64, 1) + imag[1]
        grad_ref[g] = jnp.where(lane < 64, low, high)
    mix = []
    for i in range(3):
        total = jnp.sum(rows(12 + i), axis=0, keepdims=True)
        mix.append(total + pltpu.roll(total, 64, 1))
    for g in range(4):
        own = grad_ref[g, pl.ds(side * 16, 16), :]
        for c in range(4):
            k = 4 * g + c
            send_ref[k, 0:4, :] = own[4 * c : 4 * c + 4]
            for i in range(3):
                send_ref[k, 4 + i : 5 + i, :] = mix[i]
            send_ref[k, 7:8, :] = last_ref[0:1, :]


def final_kernel(
    recv_ref, small_ref, fields_ref, solid_ref, edge_ref, below_ref, above_ref, grad_ref, mix_ref,
    new_ref,
):
    rows, lanes = fields_ref.shape[2:]
    lane = iota((rows, lanes), 1)
    rims = [below_ref[...], above_ref[...]]
    place, count = lax.axis_index("gy"), lax.axis_size("gy")
    stack = []
    for f in range(4):
        below = recv_ref[f * count + jnp.maximum(place - 1, 0)][7:8, :]
        stack += [below, pltpu.roll(below, 64, 1)]
    lower = jnp.where(place > 0, turned(jnp.concatenate(stack, axis=0))[0:rows], 0.0)
    upper = jnp.where(place < count - 1, edge_ref[...], 0.0)
    centre, sides = [], []
    for f in range(4):
        centre.append([fields_ref[f, z] for z in range(2)])
        sides.append([])
        for z in range(2):
            at = 2 * f + z
            tile = centre[f][z]
            edge = pltpu.roll(upper, lanes - 1 - 2 * at, 1)
            y_up = jnp.where(lane == lanes - 1, edge, pltpu.roll(tile, lanes - 1, 1))
            edge = pltpu.roll(lower, lanes - at, 1) if at else lower
            y_down = jnp.where(lane == 0, edge, pltpu.roll(tile, 1, 1))
            sides[f].append((y_up, y_down))
    fluids = [1.0 - solid_ref[z].astype(F32) for z in range(2)]
    results = section(centre, sides, rims, fluids)
    for z in range(2):
        for f in range(3):
            new_ref[f, z] = results[z][3 + f]
    total = recv_ref[0]
    for k in range(1, recv_ref.shape[0]):
        total = total + recv_ref[k]
    grad_ref[...] = total[0:4]
    mix = lax.dot_general(
        small_ref[0:8, :].astype(F32),
        pltpu.roll(total, 4, 0),
        TN,
        precision=lax.Precision.HIGHEST,
        preferred_element_type=F32,
    )
    mix_ref[...] = mix[:, 0:64]


def table_kernel(blocks, mode_ref, tile_ref, table_ref, turned_ref, last_ref):
    rows, lanes = tile_ref.shape[1:]
    ends = [as_row(tile_ref[z, :, lanes - 1 : lanes], (rows, lanes)) for z in range(2)]
    last_ref[...] = jnp.broadcast_to(ends[0] + pltpu.roll(ends[1], 64, 1), last_ref.shape)
    modes = mode_ref.shape[1]
    unit = 2.0 * math.pi / (blocks * rows)
    square = (modes, modes)
    index = jnp.where(iota(square, 0) == iota(square, 1), mode_ref[...].astype(F32), 0.0)
    index = jnp.sum(index, axis=1, keepdims=True).astype(jnp.int32)
    lane = iota((modes, 128), 1)
    outer = unit * (((index * lane) & (blocks - 1)) * rows).astype(F32)
    cell = jnp.where(lane >= rows, lane - rows, lane)
    inner = unit * (index * jnp.where(lane < 2 * rows, cell, 0)).astype(F32)
    outer_cos, outer_sin = jnp.cos(outer), jnp.sin(outer)
    inner_cos, inner_sin = jnp.cos(inner), jnp.sin(inner)
    by_cos = jnp.concatenate([outer_cos, -outer_sin] * 2, axis=0)
    by_sin = jnp.concatenate([-outer_sin, -outer_cos] * 2, axis=0)
    low = iota((128, 128), 0) < 2 * modes
    lane = iota((128, 128), 1)
    start = jnp.where(low, 0, rows)
    valid = (lane >= start) & (lane < start + rows)
    inner_cos = jnp.where(valid, jnp.concatenate([inner_cos] * 4, axis=0), 0.0)
    inner_sin = jnp.where(valid, jnp.concatenate([inner_sin] * 4, axis=0), 0.0)
    for b in range(blocks):
        block = by_cos[:, b : b + 1] * inner_cos + by_sin[:, b : b + 1] * inner_sin
        table_ref[:, b * 128 : (b + 1) * 128] = block.astype(BF16)
    by_cos, by_sin = jnp.transpose(by_cos), jnp.transpose(by_sin)
    inner_cos, inner_sin = jnp.transpose(inner_cos), jnp.transpose(inner_sin)
    for b in range(blocks):
        block = by_cos[b : b + 1, :] * inner_cos + by_sin[b : b + 1, :] * inner_sin
        turned_ref[b * 128 : (b + 1) * 128, :] = block.astype(BF16)


def local(slot_field, solid, lift_weight, spectral_weight, mix_weight, project_weight, mode_index):
    tile = slot_field[0]
    planes, rows, lanes = tile.shape
    blocks = lax.axis_size("gx")
    x_length = rows * blocks
    cell_total = x_length * lanes * lax.axis_size("gy") * planes
    loss_scale = 16.0 / math.sqrt(cell_total)
    scale_dft = 1.0 / math.sqrt(x_length)
    none = jnp.zeros((5, lift_weight.shape[1]), BF16)
    small = jnp.concatenate([lift_weight, none, project_weight.T, none], axis=0)

    def shift(array, axis, step, ring):
        count = lax.axis_size(axis)
        pairs = [(i, (i + step) % count) for i in range(count) if ring or 0 <= i + step < count]
        return lax.ppermute(array, axis, pairs)

    fields = lax.all_gather(slot_field, "grp", axis=0, tiled=True)
    rim = jax.ShapeDtypeStruct((8, lanes), F32)
    edge, low, high = call(
        edge_kernel, [jax.ShapeDtypeStruct((rows, lanes), F32), rim, rim], fields, solid
    )
    edge = shift(edge, "gy", -1, True)
    below, above = shift(high, "gx", 1, False), shift(low, "gx", -1, False)
    table, cells_by_modes, last = call(
        lambda *refs: table_kernel(blocks, *refs),
        [
            jax.ShapeDtypeStruct((128, blocks * 128), BF16),
            jax.ShapeDtypeStruct((blocks * 128, 128), BF16),
            jax.ShapeDtypeStruct((8, lanes), F32),
        ],
        mode_index.reshape(1, -1),
        tile,
    )
    edge, below, above, table, cells_by_modes, last, small = lax.optimization_barrier(
        (edge, below, above, table, cells_by_modes, last, small)
    )
    send = call(
        source_kernel,
        jax.ShapeDtypeStruct((blocks * 8, 128), BF16),
        fields,
        solid,
        edge,
    )
    send = send.reshape(blocks, 8, 128)
    recv = lax.all_to_all(send, "gx", split_axis=0, concat_axis=0, tiled=True)
    send = call(
        lambda *refs: line_kernel(scale_dft, loss_scale, *refs),
        jax.ShapeDtypeStruct((blocks, 16, 128), BF16),
        recv,
        table,
        cells_by_modes,
        small,
        mix_weight,
        spectral_weight,
        scratch=[pltpu.VMEM((64, 128), F32), pltpu.VMEM((64, 128), F32)],
    )
    recv = lax.all_to_all(send, "gx", split_axis=0, concat_axis=0, tiled=True)
    send = call(
        grad_kernel,
        jax.ShapeDtypeStruct((16, 8, 128), F32),
        recv,
        last,
        scratch=[pltpu.VMEM((blocks * 16, 128), F32), pltpu.VMEM((4, 32, 128), F32)],
    )
    recv = lax.all_to_all(send, ("grp", "gy"), split_axis=0, concat_axis=0, tiled=True)
    spectral_grad, mix_grad, new_velocity = call(
        final_kernel,
        [
            jax.ShapeDtypeStruct((4, 128), F32),
            jax.ShapeDtypeStruct((64, 64), F32),
            jax.ShapeDtypeStruct((3, planes, rows, lanes), F32),
        ],
        recv,
        small,
        fields,
        solid,
        edge,
        below,
        above,
    )
    return new_velocity, spectral_grad, mix_grad


def solution(mesh):
    in_specs = (P("grp", None, "gx", "gy"), P(None, "gx", "gy"), P(), P(), P(), P(), P())
    out_specs = (P(None, None, "gx", "gy"), P(("grp", "gx", "gy"), None), P())
    return jax.shard_map(local, mesh=mesh, in_specs=in_specs, out_specs=out_specs, check_vma=False)
```

```python
import math

import jax
import jax.numpy as jnp
from jax import lax
from jax.experimental import pallas as pl
from jax.experimental.pallas import tpu as pltpu
from jax.sharding import PartitionSpec as P

VISCOSITY = 0.05
TIME_STEP = 0.1
F32 = jnp.float32
BF16 = jnp.bfloat16
GELU_A = math.sqrt(2.0 / math.pi)
GELU_B = 0.044715
VMEM = pl.BlockSpec(memory_space=pltpu.VMEM)
NT = (((1,), (1,)), ((), ()))
NN = (((1,), (0,)), ((), ()))
TN = (((0,), (0,)), ((), ()))


def dot(a, b, dims):
    return lax.dot_general(a, b, dims, preferred_element_type=F32)


def iota(shape, axis):
    return lax.broadcasted_iota(jnp.int32, shape, axis)


def call(kernel, out_shape, *args, scratch=()):
    count = len(out_shape) if isinstance(out_shape, (tuple, list)) else 1
    return pl.pallas_call(
        kernel,
        out_shape=out_shape,
        in_specs=[VMEM] * len(args),
        out_specs=[VMEM] * count if isinstance(out_shape, (tuple, list)) else VMEM,
        scratch_shapes=list(scratch),
        compiler_params=pltpu.CompilerParams(vmem_limit_bytes=40 * 1024 * 1024),
    )(*args)


def as_row(column, shape):
    same = iota(shape, 0) == iota(shape, 1)
    return jnp.sum(jnp.where(same, jnp.broadcast_to(column, shape), 0.0), axis=0, keepdims=True)


def turned(rows):
    pad = jnp.zeros((128 - rows.shape[0], 128), F32)
    return jnp.transpose(jnp.concatenate([rows, pad], axis=0))


def edge_kernel(fields_ref, solid_ref, edge_ref):
    rows, lanes = fields_ref.shape[2:]
    lane = iota((rows, lanes), 1)
    edge = jnp.zeros((rows, lanes), F32)
    for f in range(4):
        for z in range(2):
            place = 2 * (2 * f + z)
            tile = fields_ref[f, z]
            tile = pltpu.roll(tile, place, 1) if place else tile
            edge = jnp.where((lane >> 1) == 2 * f + z, tile, edge)
    for z in range(2):
        fluid = pltpu.roll(1.0 - solid_ref[z].astype(F32), 16 + z, 1)
        edge = jnp.where(lane == 16 + z, fluid, edge)
    folded = edge[0:8]
    for k in range(1, rows // 8):
        folded = folded + pltpu.roll(edge[8 * k : 8 * k + 8], 18 * k, 1)
    edge_ref[...] = folded


def unfolded(folded, rows):
    parts = [pltpu.roll(folded, 128 - 18 * k, 1) if k else folded for k in range(rows // 8)]
    return jnp.concatenate(parts, axis=0)


def section(centre, sides, rims, fluids):
    rows, lanes = centre[0][0].shape
    row = iota((rows, lanes), 0)

    def near(f, z):
        tile = centre[f][z]
        below = above = 0.0
        if rims is not None:
            below, above = (rim[2 * f + z : 2 * f + z + 1, :] for rim in rims)
        x_down = jnp.where(row == 0, below, pltpu.roll(tile, 1, 0))
        x_up = jnp.where(row == rows - 1, above, pltpu.roll(tile, rows - 1, 0))
        y_up, y_down = sides[f][z]
        return x_up, x_down, y_up, y_down

    results = []
    for z in range(2):
        velocity = [centre[f][z] for f in range(3)]
        sign = 0.5 if z == 0 else -0.5
        px_up, px_down, py_up, py_down = near(3, z)
        press = (0.5 * (px_up - px_down), 0.5 * (py_up - py_down), sign * centre[3][1 - z])
        new = []
        for f in range(3):
            x_up, x_down, y_up, y_down = near(f, z)
            other = centre[f][1 - z]
            advect = (
                velocity[0] * (0.5 * (x_up - x_down))
                + velocity[1] * (0.5 * (y_up - y_down))
                + velocity[2] * (sign * other)
            )
            lap = other + x_up + x_down + y_up + y_down - 6.0 * velocity[f]
            update = velocity[f] + TIME_STEP * (VISCOSITY * lap - advect - press[f])
            new.append(update * fluids[z])
        results.append(velocity + new + [centre[3][z], fluids[z]])
    return results


def source_kernel(fields_ref, solid_ref, edge_ref, send_ref, rim_ref):
    blocks = send_ref.shape[0]
    rows, lanes = fields_ref.shape[2:]
    lane = iota((rows, lanes), 1)
    end = lane == lanes - 1
    role = lax.axis_index("grp")
    own = lax.axis_index("gx")
    last = lax.axis_index("gy") == lax.axis_size("gy") - 1
    columns = unfolded(edge_ref[...], rows)
    centre, sides = [], []
    for f in range(4):
        centre.append([])
        sides.append([])
        for z in range(2):
            tile = fields_ref[f, z]
            place = 2 * (2 * f + z)
            one = pltpu.roll(columns, lanes - 1 - place, 1)
            two = pltpu.roll(columns, lanes - 2 - place, 1)
            above = jnp.where(lane >= lanes - 2, two, pltpu.roll(tile, lanes - 2, 1))
            above = jnp.where((lane == lanes - 2) & last, 0.0, above)
            centre[f].append(jnp.where(end, one, pltpu.roll(tile, lanes - 1, 1)))
            sides[f].append((above, jnp.where(end & last, 0.0, tile)))
    fluids = []
    for z in range(2):
        fluid = pltpu.roll(1.0 - solid_ref[z].astype(F32), lanes - 1, 1)
        fluids.append(jnp.where(end, pltpu.roll(columns, lanes - 17 - z, 1), fluid))
    results = section(centre, sides, None, fluids)
    for f in range(4):
        for z in range(2):
            for k, row in ((0, 0), (1, rows - 1)):
                rim_ref[k, 2 * f + z : 2 * f + z + 1, :] = fields_ref[f, z, row : row + 1, :]
    rims = [rim_ref[k] for k in range(2)]
    values = [jnp.concatenate([p.astype(BF16) for p in parts], axis=1) for parts in results]
    pad = jnp.zeros((128 - 2 * rows, 8 * lanes), BF16)
    stacked = jnp.concatenate(values + [pad], axis=0)
    shape = (blocks * 8, 8 * lanes)
    out_row = iota(shape, 0)
    wanted = (out_row & 7) * lanes + (out_row >> 3) + role * blocks
    pick = jnp.where(iota(shape, 1) == wanted, 1.0, 0.0).astype(BF16)
    lines = dot(pick, stacked, NT)
    for b in range(blocks):
        rim = jnp.where(b > own, rims[1], rims[0])
        send_ref[b] = jnp.concatenate([lines[8 * b : 8 * b + 8], rim], axis=0).astype(BF16)


def neighbour_terms(lines, rows):
    cells = lines.shape[1]
    lane = iota((8, cells), 1)
    place = lane & 127
    starts = ((place == 0) | (place == rows)) & (lane >= 128)
    stops = ((place == rows - 1) | (place == 2 * rows - 1)) & (lane < cells - 128)
    hop = 128 - rows + 1
    below = jnp.where(starts, pltpu.roll(lines, hop, 1), 0.0)
    above = jnp.where(stops, pltpu.roll(lines, cells - hop, 1), 0.0)
    slope = 0.5 * (above - below)
    first = jnp.where(iota((8, cells), 0) == 0, slope[6:7, :], 0.0)
    terms = VISCOSITY * (above + below) - lines[0:1, :] * slope - first
    return lines[7:8, :] * (TIME_STEP * terms)


def line_kernel(
    scale_dft, loss_scale, recv_ref, table_ref, turned_ref, small_ref, mix_ref, weight_ref, send_ref,
    back_ref, coef_ref,
):
    blocks = recv_ref.shape[0]
    rows = 48
    lines = jnp.concatenate([recv_ref[b, 0:8, :] for b in range(blocks)], axis=1)
    both = table_ref[...]
    cells_by_modes = turned_ref[...]
    lift, proj = small_ref[0:8, :], small_ref[8:16, :]
    lifted = dot(lift, lines, TN).astype(BF16)
    coeffs = jnp.transpose(dot(lifted, cells_by_modes, NN) * scale_dft)
    coeffs16 = coeffs.astype(BF16)
    wide = jnp.concatenate([coeffs16] * 32, axis=1)
    mode_row = iota(wide.shape, 0) & 31
    mode_col = iota(wide.shape, 1) >> 6
    wide = jnp.where(mode_row == mode_col, wide, jnp.zeros_like(wide))
    product = dot(wide, weight_ref[...], NN)
    swapped = pltpu.roll(product, 64, 1)
    parts = []
    for line in range(2):
        real = slice(64 * line, 64 * line + 32)
        imag = slice(64 * line + 32, 64 * line + 64)
        parts.append(product[real] - swapped[imag])
        parts.append(swapped[real] + product[imag])
    mixed = jnp.concatenate(parts, axis=0)
    mixed_t = jnp.transpose(mixed)[0:64].astype(BF16)
    hidden = dot(mixed_t, both, NN) * (2.0 * scale_dft) + dot(mix_ref[...], lifted, TN)
    square = hidden * hidden
    tanh = jnp.tanh(hidden * (GELU_A + (GELU_A * GELU_B) * square))
    half = 0.5 + 0.5 * tanh
    active = (hidden * half).astype(BF16)
    rise = 0.5 * GELU_A + (1.5 * GELU_A * GELU_B) * square
    slope = half + hidden * (1.0 - tanh * tanh) * rise
    predicted = dot(proj, active, NN)
    wide_lines = lines.astype(F32)
    target = pltpu.roll(wide_lines, 5, 0) + neighbour_terms(wide_lines, rows)
    misfit = (predicted - target) * loss_scale
    misfit = jnp.where(iota(misfit.shape, 0) < 3, misfit, 0.0)
    high = misfit.astype(BF16).astype(F32)
    parts = jnp.concatenate([high, misfit - high], axis=0).astype(BF16)
    twice = jnp.concatenate([proj.astype(F32)] * 2, axis=0).astype(BF16)
    back16 = (slope * dot(twice, parts, TN)).astype(BF16)
    mix_terms = jnp.transpose(dot(back16, lines, NT))
    back_mixed = jnp.transpose(dot(back16, cells_by_modes, NN)) * (2.0 * scale_dft)
    back_ref[...] = jnp.concatenate([back_mixed[0:64], back_mixed[64:128]], axis=1)
    coef_ref[...] = jnp.concatenate([coeffs[0:64], coeffs[64:128]], axis=1)
    mix_high = mix_terms.astype(BF16)
    mix_low = (mix_terms - mix_high.astype(F32)).astype(BF16)
    tail = jnp.concatenate([mix_high, mix_low], axis=1).astype(F32)[0:4]
    lane = iota((4, 128), 1) & 63
    for j in range(8):
        back_j = back_ref[pl.ds(j, 8, stride=8), :]
        coef_j = coef_ref[pl.ds(j, 8, stride=8), :]
        real, imag = coef_j[0:4], coef_j[4:8]
        halves = (
            jnp.where(lane < 32, real, pltpu.roll(imag, 32, 1)),
            jnp.where(lane < 32, pltpu.roll(real, 96, 1), imag),
        )
        for k, half in enumerate(halves):
            chunk = jnp.concatenate([back_j, half, tail], axis=0).astype(BF16)
            send_ref[4 * j + 2 * k] = chunk
            send_ref[4 * j + 2 * k + 1] = chunk


def grad_kernel(recv_ref, last_ref, send_ref, wide_ref, grad_ref):
    side = lax.rem(lax.axis_index("gx"), 2)
    blocks, height = recv_ref.shape[:2]
    for b in range(blocks):
        wide_ref[b * height : (b + 1) * height, :] = recv_ref[b].astype(F32)

    def rows(k):
        return wide_ref[pl.ds(k, blocks, stride=height), :]

    lane = iota((32, 128), 1)
    for g in range(4):
        coef = rows(8 + g).astype(BF16)
        by_real = dot(coef, rows(g).astype(BF16), TN)
        by_imag = dot(coef, rows(4 + g).astype(BF16), TN)
        real = [by_real[k : k + 32] + by_imag[k + 32 : k + 64] for k in (0, 64)]
        imag = [by_imag[k : k + 32] - by_real[k + 32 : k + 64] for k in (0, 64)]
        low = real[0] + pltpu.roll(real[1], 64, 1)
        high = pltpu.roll(imag[0], 64, 1) + imag[1]
        grad_ref[g] = jnp.where(lane < 64, low, high)
    mix = []
    for i in range(3):
        total = jnp.sum(rows(12 + i), axis=0, keepdims=True)
        mix.append(total + pltpu.roll(total, 64, 1))
    for g in range(4):
        own = grad_ref[g, pl.ds(side * 16, 16), :]
        for c in range(4):
            k = 4 * g + c
            send_ref[k, 0:4, :] = own[4 * c : 4 * c + 4]
            for i in range(3):
                send_ref[k, 4 + i : 5 + i, :] = mix[i]
            send_ref[k, 7:8, :] = last_ref[0:1, :]


def final_kernel(
    recv_ref, small_ref, fields_ref, solid_ref, edge_ref, lines_ref, grad_ref, mix_ref, new_ref
):
    rows, lanes = fields_ref.shape[2:]
    lane = iota((rows, lanes), 1)
    last = lines_ref.shape[0] - 1
    own = lax.axis_index("gx")
    rims = []
    for index, inside in ((own - 1, own > 0), (own + 1, own < last)):
        message = lines_ref[jnp.minimum(jnp.maximum(index, 0), last)].astype(F32)
        rims.append(jnp.where(inside, message[8:16], 0.0))
    place, count = lax.axis_index("gy"), lax.axis_size("gy")
    stack = []
    for f in range(4):
        below = recv_ref[f * count + jnp.maximum(place - 1, 0)][7:8, :]
        stack += [below, pltpu.roll(below, 64, 1)]
    lower = jnp.where(place > 0, turned(jnp.concatenate(stack, axis=0))[0:rows], 0.0)
    upper = jnp.where(place < count - 1, unfolded(edge_ref[...], rows), 0.0)
    centre, sides = [], []
    for f in range(4):
        centre.append([fields_ref[f, z] for z in range(2)])
        sides.append([])
        for z in range(2):
            at = 2 * f + z
            tile = centre[f][z]
            edge = pltpu.roll(upper, lanes - 1 - 2 * at, 1)
            y_up = jnp.where(lane == lanes - 1, edge, pltpu.roll(tile, lanes - 1, 1))
            edge = pltpu.roll(lower, lanes - at, 1) if at else lower
            y_down = jnp.where(lane == 0, edge, pltpu.roll(tile, 1, 1))
            sides[f].append((y_up, y_down))
    fluids = [1.0 - solid_ref[z].astype(F32) for z in range(2)]
    results = section(centre, sides, rims, fluids)
    for z in range(2):
        for f in range(3):
            new_ref[f, z] = results[z][3 + f]
    total = recv_ref[0]
    for k in range(1, recv_ref.shape[0]):
        total = total + recv_ref[k]
    grad_ref[...] = total[0:4]
    mix = lax.dot_general(
        small_ref[0:8, :].astype(F32),
        pltpu.roll(total, 4, 0),
        TN,
        precision=lax.Precision.HIGHEST,
        preferred_element_type=F32,
    )
    mix_ref[...] = mix[:, 0:64]


def table_kernel(blocks, mode_ref, tile_ref, table_ref, turned_ref, last_ref):
    rows, lanes = tile_ref.shape[1:]
    ends = [as_row(tile_ref[z, :, lanes - 1 : lanes], (rows, lanes)) for z in range(2)]
    last_ref[...] = jnp.broadcast_to(ends[0] + pltpu.roll(ends[1], 64, 1), last_ref.shape)
    modes = mode_ref.shape[1]
    unit = 2.0 * math.pi / (blocks * rows)
    square = (modes, modes)
    index = jnp.where(iota(square, 0) == iota(square, 1), mode_ref[...].astype(F32), 0.0)
    index = jnp.sum(index, axis=1, keepdims=True).astype(jnp.int32)
    lane = iota((modes, 128), 1)
    outer = unit * (((index * lane) & (blocks - 1)) * rows).astype(F32)
    cell = jnp.where(lane >= rows, lane - rows, lane)
    inner = unit * (index * jnp.where(lane < 2 * rows, cell, 0)).astype(F32)
    outer_cos, outer_sin = jnp.cos(outer), jnp.sin(outer)
    inner_cos, inner_sin = jnp.cos(inner), jnp.sin(inner)
    by_cos = jnp.concatenate([outer_cos, -outer_sin] * 2, axis=0)
    by_sin = jnp.concatenate([-outer_sin, -outer_cos] * 2, axis=0)
    low = iota((128, 128), 0) < 2 * modes
    lane = iota((128, 128), 1)
    start = jnp.where(low, 0, rows)
    valid = (lane >= start) & (lane < start + rows)
    inner_cos = jnp.where(valid, jnp.concatenate([inner_cos] * 4, axis=0), 0.0)
    inner_sin = jnp.where(valid, jnp.concatenate([inner_sin] * 4, axis=0), 0.0)
    for b in range(blocks):
        block = by_cos[:, b : b + 1] * inner_cos + by_sin[:, b : b + 1] * inner_sin
        table_ref[:, b * 128 : (b + 1) * 128] = block.astype(BF16)
    by_cos, by_sin = jnp.transpose(by_cos), jnp.transpose(by_sin)
    inner_cos, inner_sin = jnp.transpose(inner_cos), jnp.transpose(inner_sin)
    for b in range(blocks):
        block = by_cos[b : b + 1, :] * inner_cos + by_sin[b : b + 1, :] * inner_sin
        turned_ref[b * 128 : (b + 1) * 128, :] = block.astype(BF16)


def local(slot_field, solid, lift_weight, spectral_weight, mix_weight, project_weight, mode_index):
    tile = slot_field[0]
    planes, rows, lanes = tile.shape
    blocks = lax.axis_size("gx")
    x_length = rows * blocks
    cell_total = x_length * lanes * lax.axis_size("gy") * planes
    loss_scale = 16.0 / math.sqrt(cell_total)
    scale_dft = 1.0 / math.sqrt(x_length)
    none = jnp.zeros((5, lift_weight.shape[1]), BF16)
    small = jnp.concatenate([lift_weight, none, project_weight.T, none], axis=0)

    def shift(array, axis, step):
        count = lax.axis_size(axis)
        pairs = [(i, (i + step) % count) for i in range(count)]
        return lax.ppermute(array, axis, pairs)

    fields = lax.all_gather(slot_field, "grp", axis=0, tiled=True)
    edge = call(edge_kernel, jax.ShapeDtypeStruct((8, lanes), F32), fields, solid)
    edge = shift(edge, "gy", -1)
    table, cells_by_modes, last = call(
        lambda *refs: table_kernel(blocks, *refs),
        [
            jax.ShapeDtypeStruct((128, blocks * 128), BF16),
            jax.ShapeDtypeStruct((blocks * 128, 128), BF16),
            jax.ShapeDtypeStruct((8, lanes), F32),
        ],
        mode_index.reshape(1, -1),
        tile,
    )
    edge, table, cells_by_modes, last, small = lax.optimization_barrier(
        (edge, table, cells_by_modes, last, small)
    )
    send = call(
        source_kernel,
        jax.ShapeDtypeStruct((blocks, 16, 128), BF16),
        fields,
        solid,
        edge,
        scratch=[pltpu.VMEM((2, 8, lanes), F32)],
    )
    recv = lines = lax.all_to_all(send, "gx", split_axis=0, concat_axis=0, tiled=True)
    send = call(
        lambda *refs: line_kernel(scale_dft, loss_scale, *refs),
        jax.ShapeDtypeStruct((blocks, 16, 128), BF16),
        recv,
        table,
        cells_by_modes,
        small,
        mix_weight,
        spectral_weight,
        scratch=[pltpu.VMEM((64, 128), F32), pltpu.VMEM((64, 128), F32)],
    )
    recv = lax.all_to_all(send, "gx", split_axis=0, concat_axis=0, tiled=True)
    send = call(
        grad_kernel,
        jax.ShapeDtypeStruct((16, 8, 128), F32),
        recv,
        last,
        scratch=[pltpu.VMEM((blocks * 16, 128), F32), pltpu.VMEM((4, 32, 128), F32)],
    )
    recv = lax.all_to_all(send, ("grp", "gy"), split_axis=0, concat_axis=0, tiled=True)
    spectral_grad, mix_grad, new_velocity = call(
        final_kernel,
        [
            jax.ShapeDtypeStruct((4, 128), F32),
            jax.ShapeDtypeStruct((64, 64), F32),
            jax.ShapeDtypeStruct((3, planes, rows, lanes), F32),
        ],
        recv,
        small,
        fields,
        solid,
        edge,
        lines,
    )
    return new_velocity, spectral_grad, mix_grad


def solution(mesh):
    in_specs = (P("grp", None, "gx", "gy"), P(None, "gx", "gy"), P(), P(), P(), P(), P())
    out_specs = (P(None, None, "gx", "gy"), P(("grp", "gx", "gy"), None), P())
    return jax.shard_map(local, mesh=mesh, in_specs=in_specs, out_specs=out_specs, check_vma=False)
```

```python
import math

import jax
import jax.numpy as jnp
from jax import lax
from jax.experimental import pallas as pl
from jax.experimental.pallas import tpu as pltpu
from jax.sharding import PartitionSpec as P

VISCOSITY = 0.05
TIME_STEP = 0.1
F32 = jnp.float32
BF16 = jnp.bfloat16
GELU_A = math.sqrt(2.0 / math.pi)
GELU_B = 0.044715
VMEM = pl.BlockSpec(memory_space=pltpu.VMEM)
NT = (((1,), (1,)), ((), ()))
NN = (((1,), (0,)), ((), ()))
TN = (((0,), (0,)), ((), ()))


def dot(a, b, dims):
    return lax.dot_general(a, b, dims, preferred_element_type=F32)


def iota(shape, axis):
    return lax.broadcasted_iota(jnp.int32, shape, axis)


def call(kernel, out_shape, *args, scratch=()):
    count = len(out_shape) if isinstance(out_shape, (tuple, list)) else 1
    return pl.pallas_call(
        kernel,
        out_shape=out_shape,
        in_specs=[VMEM] * len(args),
        out_specs=[VMEM] * count if isinstance(out_shape, (tuple, list)) else VMEM,
        scratch_shapes=list(scratch),
        compiler_params=pltpu.CompilerParams(vmem_limit_bytes=40 * 1024 * 1024),
    )(*args)


def as_row(column, shape):
    same = iota(shape, 0) == iota(shape, 1)
    return jnp.sum(jnp.where(same, jnp.broadcast_to(column, shape), 0.0), axis=0, keepdims=True)


def turned(rows):
    pad = jnp.zeros((128 - rows.shape[0], 128), F32)
    return jnp.transpose(jnp.concatenate([rows, pad], axis=0))


def edge_kernel(fields_ref, solid_ref, edge_ref):
    rows, lanes = fields_ref.shape[2:]
    lane = iota((rows, lanes), 1)
    edge = jnp.zeros((rows, lanes), F32)
    for f in range(4):
        for z in range(2):
            place = 2 * (2 * f + z)
            tile = fields_ref[f, z]
            tile = pltpu.roll(tile, place, 1) if place else tile
            edge = jnp.where((lane >> 1) == 2 * f + z, tile, edge)
    for z in range(2):
        fluid = pltpu.roll(1.0 - solid_ref[z].astype(F32), 16 + z, 1)
        edge = jnp.where(lane == 16 + z, fluid, edge)
    folded = edge[0:8]
    for k in range(1, rows // 8):
        folded = folded + pltpu.roll(edge[8 * k : 8 * k + 8], 18 * k, 1)
    edge_ref[...] = folded


def unfolded(folded, rows):
    parts = [pltpu.roll(folded, 128 - 18 * k, 1) if k else folded for k in range(rows // 8)]
    return jnp.concatenate(parts, axis=0)


def section(centre, sides, rims, fluids):
    rows, lanes = centre[0][0].shape
    row = iota((rows, lanes), 0)

    def near(f, z):
        tile = centre[f][z]
        below = above = 0.0
        if rims is not None:
            below, above = (rim[2 * f + z : 2 * f + z + 1, :] for rim in rims)
        x_down = jnp.where(row == 0, below, pltpu.roll(tile, 1, 0))
        x_up = jnp.where(row == rows - 1, above, pltpu.roll(tile, rows - 1, 0))
        y_up, y_down = sides[f][z]
        return x_up, x_down, y_up, y_down

    results = []
    for z in range(2):
        velocity = [centre[f][z] for f in range(3)]
        sign = 0.5 if z == 0 else -0.5
        px_up, px_down, py_up, py_down = near(3, z)
        press = (0.5 * (px_up - px_down), 0.5 * (py_up - py_down), sign * centre[3][1 - z])
        new = []
        for f in range(3):
            x_up, x_down, y_up, y_down = near(f, z)
            other = centre[f][1 - z]
            advect = (
                velocity[0] * (0.5 * (x_up - x_down))
                + velocity[1] * (0.5 * (y_up - y_down))
                + velocity[2] * (sign * other)
            )
            lap = other + x_up + x_down + y_up + y_down - 6.0 * velocity[f]
            update = velocity[f] + TIME_STEP * (VISCOSITY * lap - advect - press[f])
            new.append(update * fluids[z])
        results.append(velocity + new + [centre[3][z], fluids[z]])
    return results


def source_kernel(fields_ref, solid_ref, edge_ref, send_ref, rim_ref):
    blocks = send_ref.shape[0]
    rows, lanes = fields_ref.shape[2:]
    lane = iota((rows, lanes), 1)
    end = lane == lanes - 1
    role = lax.axis_index("grp")
    own = lax.axis_index("gx")
    last = lax.axis_index("gy") == lax.axis_size("gy") - 1
    columns = unfolded(edge_ref[...], rows)
    centre, sides = [], []
    for f in range(4):
        centre.append([])
        sides.append([])
        for z in range(2):
            tile = fields_ref[f, z]
            place = 2 * (2 * f + z)
            one = pltpu.roll(columns, lanes - 1 - place, 1)
            two = pltpu.roll(columns, lanes - 2 - place, 1)
            above = jnp.where(lane >= lanes - 2, two, pltpu.roll(tile, lanes - 2, 1))
            above = jnp.where((lane == lanes - 2) & last, 0.0, above)
            centre[f].append(jnp.where(end, one, pltpu.roll(tile, lanes - 1, 1)))
            sides[f].append((above, jnp.where(end & last, 0.0, tile)))
    fluids = []
    for z in range(2):
        fluid = pltpu.roll(1.0 - solid_ref[z].astype(F32), lanes - 1, 1)
        fluids.append(jnp.where(end, pltpu.roll(columns, lanes - 17 - z, 1), fluid))
    results = section(centre, sides, None, fluids)
    for f in range(4):
        for z in range(2):
            for k, row in ((0, 0), (1, rows - 1)):
                rim_ref[k, 2 * f + z : 2 * f + z + 1, :] = fields_ref[f, z, row : row + 1, :]
    rims = [rim_ref[k] for k in range(2)]
    values = [jnp.concatenate([p.astype(BF16) for p in parts], axis=1) for parts in results]
    pad = jnp.zeros((128 - 2 * rows, 8 * lanes), BF16)
    stacked = jnp.concatenate(values + [pad], axis=0)
    shape = (blocks * 8, 8 * lanes)
    out_row = iota(shape, 0)
    wanted = (out_row & 7) * lanes + (out_row >> 3) + role * blocks
    pick = jnp.where(iota(shape, 1) == wanted, 1.0, 0.0).astype(BF16)
    lines = dot(pick, stacked, NT)
    for b in range(blocks):
        rim = jnp.where(b > own, rims[1], rims[0])
        send_ref[b] = jnp.concatenate([lines[8 * b : 8 * b + 8], rim], axis=0).astype(BF16)


def neighbour_terms(lines, rows):
    cells = lines.shape[1]
    lane = iota((8, cells), 1)
    place = lane & 127
    starts = ((place == 0) | (place == rows)) & (lane >= 128)
    stops = ((place == rows - 1) | (place == 2 * rows - 1)) & (lane < cells - 128)
    hop = 128 - rows + 1
    below = jnp.where(starts, pltpu.roll(lines, hop, 1), 0.0)
    above = jnp.where(stops, pltpu.roll(lines, cells - hop, 1), 0.0)
    slope = 0.5 * (above - below)
    first = jnp.where(iota((8, cells), 0) == 0, slope[6:7, :], 0.0)
    terms = VISCOSITY * (above + below) - lines[0:1, :] * slope - first
    return lines[7:8, :] * (TIME_STEP * terms)


def line_kernel(
    scale_dft, loss_scale, recv_ref, table_ref, turned_ref, small_ref, mix_ref, weight_ref, send_ref,
    back_ref, coef_ref,
):
    blocks = recv_ref.shape[0]
    rows = 48
    lines = jnp.concatenate([recv_ref[b, 0:8, :] for b in range(blocks)], axis=1)
    both = table_ref[...]
    cells_by_modes = turned_ref[...]
    lift, proj = small_ref[0:8, :], small_ref[8:16, :]
    lifted = dot(lift, lines, TN).astype(BF16)
    coeffs = jnp.transpose(dot(lifted, cells_by_modes, NN) * scale_dft)
    coeffs16 = coeffs.astype(BF16)
    wide = jnp.concatenate([coeffs16] * 32, axis=1)
    mode_row = iota(wide.shape, 0) & 31
    mode_col = iota(wide.shape, 1) >> 6
    wide = jnp.where(mode_row == mode_col, wide, jnp.zeros_like(wide))
    product = dot(wide, weight_ref[...], NN)
    swapped = pltpu.roll(product, 64, 1)
    parts = []
    for line in range(2):
        real = slice(64 * line, 64 * line + 32)
        imag = slice(64 * line + 32, 64 * line + 64)
        parts.append(product[real] - swapped[imag])
        parts.append(swapped[real] + product[imag])
    mixed = jnp.concatenate(parts, axis=0)
    mixed_t = jnp.transpose(mixed)[0:64].astype(BF16)
    hidden = dot(mixed_t, both, NN) * (2.0 * scale_dft) + dot(mix_ref[...], lifted, TN)
    square = hidden * hidden
    tanh = jnp.tanh(hidden * (GELU_A + (GELU_A * GELU_B) * square))
    half = 0.5 + 0.5 * tanh
    active = (hidden * half).astype(BF16)
    rise = 0.5 * GELU_A + (1.5 * GELU_A * GELU_B) * square
    slope = half + hidden * (1.0 - tanh * tanh) * rise
    predicted = dot(proj, active, NN)
    wide_lines = lines.astype(F32)
    target = pltpu.roll(wide_lines, 5, 0) + neighbour_terms(wide_lines, rows)
    misfit = (predicted - target) * loss_scale
    misfit = jnp.where(iota(misfit.shape, 0) < 3, misfit, 0.0)
    high = misfit.astype(BF16).astype(F32)
    parts = jnp.concatenate([high, misfit - high], axis=0).astype(BF16)
    twice = jnp.concatenate([proj.astype(F32)] * 2, axis=0).astype(BF16)
    back16 = (slope * dot(twice, parts, TN)).astype(BF16)
    mix_terms = jnp.transpose(dot(back16, lines, NT))
    back_mixed = jnp.transpose(dot(back16, cells_by_modes, NN)) * (2.0 * scale_dft)
    back_ref[...] = jnp.concatenate([back_mixed[0:64], back_mixed[64:128]], axis=1)
    coef_ref[...] = jnp.concatenate([coeffs[0:64], coeffs[64:128]], axis=1)
    mix_high = mix_terms.astype(BF16)
    mix_low = (mix_terms - mix_high.astype(F32)).astype(BF16)
    tail = jnp.concatenate([mix_high, mix_low], axis=1).astype(F32)[0:4]
    lane = iota((4, 128), 1) & 63
    for j in range(8):
        back_j = back_ref[pl.ds(j, 8, stride=8), :]
        coef_j = coef_ref[pl.ds(j, 8, stride=8), :]
        real, imag = coef_j[0:4], coef_j[4:8]
        halves = (
            jnp.where(lane < 32, real, pltpu.roll(imag, 32, 1)),
            jnp.where(lane < 32, pltpu.roll(real, 96, 1), imag),
        )
        for k, half in enumerate(halves):
            chunk = jnp.concatenate([back_j, half, tail], axis=0).astype(BF16)
            send_ref[4 * j + 2 * k] = chunk
            send_ref[4 * j + 2 * k + 1] = chunk


def grad_kernel(recv_ref, last_ref, send_ref, wide_ref, grad_ref):
    side = lax.rem(lax.axis_index("gx"), 2)
    blocks, height = recv_ref.shape[:2]
    for b in range(blocks):
        wide_ref[b * height : (b + 1) * height, :] = recv_ref[b].astype(F32)

    def rows(k):
        return wide_ref[pl.ds(k, blocks, stride=height), :]

    lane = iota((32, 128), 1)
    for g in range(4):
        coef = rows(8 + g).astype(BF16)
        by_real = dot(coef, rows(g).astype(BF16), TN)
        by_imag = dot(coef, rows(4 + g).astype(BF16), TN)
        real = [by_real[k : k + 32] + by_imag[k + 32 : k + 64] for k in (0, 64)]
        imag = [by_imag[k : k + 32] - by_real[k + 32 : k + 64] for k in (0, 64)]
        low = real[0] + pltpu.roll(real[1], 64, 1)
        high = pltpu.roll(imag[0], 64, 1) + imag[1]
        grad_ref[g] = jnp.where(lane < 64, low, high)
    mix = []
    for i in range(3):
        total = jnp.sum(rows(12 + i), axis=0, keepdims=True)
        mix.append(total + pltpu.roll(total, 64, 1))
    for g in range(4):
        own = grad_ref[g, pl.ds(side * 16, 16), :]
        for c in range(4):
            k = 4 * g + c
            send_ref[k, 0:4, :] = own[4 * c : 4 * c + 4]
            for i in range(3):
                send_ref[k, 4 + i : 5 + i, :] = mix[i]
            send_ref[k, 7:8, :] = last_ref[0:1, :]


def final_kernel(
    recv_ref, small_ref, fields_ref, solid_ref, edge_ref, lines_ref, grad_ref, mix_ref, new_ref
):
    rows, lanes = fields_ref.shape[2:]
    lane = iota((rows, lanes), 1)
    last = lines_ref.shape[0] - 1
    own = lax.axis_index("gx")
    rims = []
    for index, inside in ((own - 1, own > 0), (own + 1, own < last)):
        message = lines_ref[jnp.minimum(jnp.maximum(index, 0), last)].astype(F32)
        rims.append(jnp.where(inside, message[8:16], 0.0))
    place, count = lax.axis_index("gy"), lax.axis_size("gy")
    stack = []
    for f in range(4):
        below = recv_ref[f * count + jnp.maximum(place - 1, 0)][7:8, :]
        stack += [below, pltpu.roll(below, 64, 1)]
    lower = jnp.where(place > 0, turned(jnp.concatenate(stack, axis=0))[0:rows], 0.0)
    upper = jnp.where(place < count - 1, unfolded(edge_ref[...], rows), 0.0)
    centre, sides = [], []
    for f in range(4):
        centre.append([fields_ref[f, z] for z in range(2)])
        sides.append([])
        for z in range(2):
            at = 2 * f + z
            tile = centre[f][z]
            edge = pltpu.roll(upper, lanes - 1 - 2 * at, 1)
            y_up = jnp.where(lane == lanes - 1, edge, pltpu.roll(tile, lanes - 1, 1))
            edge = pltpu.roll(lower, lanes - at, 1) if at else lower
            y_down = jnp.where(lane == 0, edge, pltpu.roll(tile, 1, 1))
            sides[f].append((y_up, y_down))
    fluids = [1.0 - solid_ref[z].astype(F32) for z in range(2)]
    results = section(centre, sides, rims, fluids)
    for z in range(2):
        for f in range(3):
            new_ref[f, z] = results[z][3 + f]
    total = recv_ref[0]
    for k in range(1, recv_ref.shape[0]):
        total = total + recv_ref[k]
    grad_ref[...] = total[0:4]
    mix = lax.dot_general(
        small_ref[0:8, :].astype(F32),
        pltpu.roll(total, 4, 0),
        TN,
        precision=lax.Precision.HIGHEST,
        preferred_element_type=F32,
    )
    mix_ref[...] = mix[:, 0:64]


def table_kernel(blocks, mode_ref, tile_ref, table_ref, turned_ref, last_ref):
    rows, lanes = tile_ref.shape[1:]
    ends = [as_row(tile_ref[z, :, lanes - 1 : lanes], (rows, lanes)) for z in range(2)]
    last_ref[...] = jnp.broadcast_to(ends[0] + pltpu.roll(ends[1], 64, 1), last_ref.shape)
    modes = mode_ref.shape[1]
    unit = 2.0 * math.pi / (blocks * rows)
    square = (modes, modes)
    index = jnp.where(iota(square, 0) == iota(square, 1), mode_ref[...].astype(F32), 0.0)
    index = jnp.sum(index, axis=1, keepdims=True).astype(jnp.int32)
    lane = iota((modes, 128), 1)
    outer = unit * (((index * lane) & (blocks - 1)) * rows).astype(F32)
    cell = jnp.where(lane >= rows, lane - rows, lane)
    inner = unit * (index * jnp.where(lane < 2 * rows, cell, 0)).astype(F32)
    outer_cos, outer_sin = jnp.cos(outer), jnp.sin(outer)
    inner_cos, inner_sin = jnp.cos(inner), jnp.sin(inner)
    by_cos = jnp.concatenate([outer_cos, -outer_sin] * 2, axis=0)
    by_sin = jnp.concatenate([-outer_sin, -outer_cos] * 2, axis=0)
    low = iota((128, 128), 0) < 2 * modes
    lane = iota((128, 128), 1)
    start = jnp.where(low, 0, rows)
    valid = (lane >= start) & (lane < start + rows)
    inner_cos = jnp.where(valid, jnp.concatenate([inner_cos] * 4, axis=0), 0.0)
    inner_sin = jnp.where(valid, jnp.concatenate([inner_sin] * 4, axis=0), 0.0)
    for b in range(blocks):
        block = by_cos[:, b : b + 1] * inner_cos + by_sin[:, b : b + 1] * inner_sin
        table_ref[:, b * 128 : (b + 1) * 128] = block.astype(BF16)
    by_cos, by_sin = jnp.transpose(by_cos), jnp.transpose(by_sin)
    inner_cos, inner_sin = jnp.transpose(inner_cos), jnp.transpose(inner_sin)
    for b in range(blocks):
        block = by_cos[b : b + 1, :] * inner_cos + by_sin[b : b + 1, :] * inner_sin
        turned_ref[b * 128 : (b + 1) * 128, :] = block.astype(BF16)


def local(slot_field, solid, lift_weight, spectral_weight, mix_weight, project_weight, mode_index):
    tile = slot_field[0]
    planes, rows, lanes = tile.shape
    blocks = lax.axis_size("gx")
    x_length = rows * blocks
    cell_total = x_length * lanes * lax.axis_size("gy") * planes
    loss_scale = 16.0 / math.sqrt(cell_total)
    scale_dft = 1.0 / math.sqrt(x_length)
    none = jnp.zeros((5, lift_weight.shape[1]), BF16)
    small = jnp.concatenate([lift_weight, none, project_weight.T, none], axis=0)

    fields = lax.all_gather(slot_field, "grp", axis=0, tiled=True)
    edge = call(edge_kernel, jax.ShapeDtypeStruct((8, lanes), F32), fields, solid)
    groups, count = lax.axis_size("grp"), lax.axis_size("gy")
    pairs = []
    for g in range(groups):
        pairs += [(g * count + i + 1, g * count + i) for i in range(count - 1)]
        pairs.append(((g + groups // 2) % groups * count, g * count + count - 1))
    edge = lax.ppermute(edge, ("grp", "gy"), pairs)
    table, cells_by_modes, last = call(
        lambda *refs: table_kernel(blocks, *refs),
        [
            jax.ShapeDtypeStruct((128, blocks * 128), BF16),
            jax.ShapeDtypeStruct((blocks * 128, 128), BF16),
            jax.ShapeDtypeStruct((8, lanes), F32),
        ],
        mode_index.reshape(1, -1),
        tile,
    )
    edge, table, cells_by_modes, last, small = lax.optimization_barrier(
        (edge, table, cells_by_modes, last, small)
    )
    send = call(
        source_kernel,
        jax.ShapeDtypeStruct((blocks, 16, 128), BF16),
        fields,
        solid,
        edge,
        scratch=[pltpu.VMEM((2, 8, lanes), F32)],
    )
    recv = lines = lax.all_to_all(send, "gx", split_axis=0, concat_axis=0, tiled=True)
    send = call(
        lambda *refs: line_kernel(scale_dft, loss_scale, *refs),
        jax.ShapeDtypeStruct((blocks, 16, 128), BF16),
        recv,
        table,
        cells_by_modes,
        small,
        mix_weight,
        spectral_weight,
        scratch=[pltpu.VMEM((64, 128), F32), pltpu.VMEM((64, 128), F32)],
    )
    recv = lax.all_to_all(send, "gx", split_axis=0, concat_axis=0, tiled=True)
    send = call(
        grad_kernel,
        jax.ShapeDtypeStruct((16, 8, 128), F32),
        recv,
        last,
        scratch=[pltpu.VMEM((blocks * 16, 128), F32), pltpu.VMEM((4, 32, 128), F32)],
    )
    recv = lax.all_to_all(send, ("grp", "gy"), split_axis=0, concat_axis=0, tiled=True)
    spectral_grad, mix_grad, new_velocity = call(
        final_kernel,
        [
            jax.ShapeDtypeStruct((4, 128), F32),
            jax.ShapeDtypeStruct((64, 64), F32),
            jax.ShapeDtypeStruct((3, planes, rows, lanes), F32),
        ],
        recv,
        small,
        fields,
        solid,
        edge,
        lines,
    )
    return new_velocity, spectral_grad, mix_grad


def solution(mesh):
    in_specs = (P("grp", None, "gx", "gy"), P(None, "gx", "gy"), P(), P(), P(), P(), P())
    out_specs = (P(None, None, "gx", "gy"), P(("grp", "gx", "gy"), None), P())
    return jax.shard_map(local, mesh=mesh, in_specs=in_specs, out_specs=out_specs, check_vma=False)
```

```python
import math

import jax
import jax.numpy as jnp
from jax import lax
from jax.experimental import pallas as pl
from jax.experimental.pallas import tpu as pltpu
from jax.sharding import PartitionSpec as P

VISCOSITY = 0.05
TIME_STEP = 0.1
F32 = jnp.float32
BF16 = jnp.bfloat16
GELU_A = math.sqrt(2.0 / math.pi)
GELU_B = 0.044715
VMEM = pl.BlockSpec(memory_space=pltpu.VMEM)
NT = (((1,), (1,)), ((), ()))
NN = (((1,), (0,)), ((), ()))
TN = (((0,), (0,)), ((), ()))


def dot(a, b, dims):
    return lax.dot_general(a, b, dims, preferred_element_type=F32)


def iota(shape, axis):
    return lax.broadcasted_iota(jnp.int32, shape, axis)


def call(kernel, out_shape, *args, scratch=()):
    count = len(out_shape) if isinstance(out_shape, (tuple, list)) else 1
    return pl.pallas_call(
        kernel,
        out_shape=out_shape,
        in_specs=[VMEM] * len(args),
        out_specs=[VMEM] * count if isinstance(out_shape, (tuple, list)) else VMEM,
        scratch_shapes=list(scratch),
        compiler_params=pltpu.CompilerParams(vmem_limit_bytes=40 * 1024 * 1024),
    )(*args)


def as_row(column, shape):
    same = iota(shape, 0) == iota(shape, 1)
    return jnp.sum(jnp.where(same, jnp.broadcast_to(column, shape), 0.0), axis=0, keepdims=True)


def turned(rows):
    pad = jnp.zeros((128 - rows.shape[0], 128), F32)
    return jnp.transpose(jnp.concatenate([rows, pad], axis=0))


def edge_kernel(fields_ref, solid_ref, edge_ref):
    rows, lanes = fields_ref.shape[2:]
    lane = iota((rows, lanes), 1)
    edge = jnp.zeros((rows, lanes), F32)
    for f in range(4):
        for z in range(2):
            place = 2 * (2 * f + z)
            tile = fields_ref[f, z]
            tile = pltpu.roll(tile, place, 1) if place else tile
            edge = jnp.where((lane >> 1) == 2 * f + z, tile, edge)
    for z in range(2):
        fluid = pltpu.roll(1.0 - solid_ref[z].astype(F32), 16 + z, 1)
        edge = jnp.where(lane == 16 + z, fluid, edge)
    folded = edge[0:8]
    for k in range(1, rows // 8):
        folded = folded + pltpu.roll(edge[8 * k : 8 * k + 8], 18 * k, 1)
    edge_ref[...] = folded


def unfolded(folded, rows):
    parts = [pltpu.roll(folded, 128 - 18 * k, 1) if k else folded for k in range(rows // 8)]
    return jnp.concatenate(parts, axis=0)


def section(centre, sides, rims, fluids):
    rows, lanes = centre[0][0].shape
    row = iota((rows, lanes), 0)

    def near(f, z):
        tile = centre[f][z]
        below = above = 0.0
        if rims is not None:
            below, above = (rim[2 * f + z : 2 * f + z + 1, :] for rim in rims)
        x_down = jnp.where(row == 0, below, pltpu.roll(tile, 1, 0))
        x_up = jnp.where(row == rows - 1, above, pltpu.roll(tile, rows - 1, 0))
        y_up, y_down = sides[f][z]
        return x_up, x_down, y_up, y_down

    results = []
    for z in range(2):
        velocity = [centre[f][z] for f in range(3)]
        sign = 0.5 if z == 0 else -0.5
        px_up, px_down, py_up, py_down = near(3, z)
        press = (0.5 * (px_up - px_down), 0.5 * (py_up - py_down), sign * centre[3][1 - z])
        new = []
        for f in range(3):
            x_up, x_down, y_up, y_down = near(f, z)
            other = centre[f][1 - z]
            advect = (
                velocity[0] * (0.5 * (x_up - x_down))
                + velocity[1] * (0.5 * (y_up - y_down))
                + velocity[2] * (sign * other)
            )
            lap = other + x_up + x_down + y_up + y_down - 6.0 * velocity[f]
            update = velocity[f] + TIME_STEP * (VISCOSITY * lap - advect - press[f])
            new.append(update * fluids[z])
        results.append(velocity + new + [centre[3][z], fluids[z]])
    return results


def source_kernel(fields_ref, solid_ref, edge_ref, pick_ref, send_ref, rim_ref):
    blocks = send_ref.shape[0]
    rows, lanes = fields_ref.shape[2:]
    lane = iota((rows, lanes), 1)
    end = lane == lanes - 1
    own = lax.axis_index("gx")
    last = lax.axis_index("gy") == lax.axis_size("gy") - 1
    columns = unfolded(edge_ref[...], rows)
    centre, sides = [], []
    for f in range(4):
        centre.append([])
        sides.append([])
        for z in range(2):
            tile = fields_ref[f, z]
            place = 2 * (2 * f + z)
            one = pltpu.roll(columns, lanes - 1 - place, 1)
            two = pltpu.roll(columns, lanes - 2 - place, 1)
            above = jnp.where(lane >= lanes - 2, two, pltpu.roll(tile, lanes - 2, 1))
            above = jnp.where((lane == lanes - 2) & last, 0.0, above)
            centre[f].append(jnp.where(end, one, pltpu.roll(tile, lanes - 1, 1)))
            sides[f].append((above, jnp.where(end & last, 0.0, tile)))
    fluids = []
    for z in range(2):
        fluid = pltpu.roll(1.0 - solid_ref[z].astype(F32), lanes - 1, 1)
        fluids.append(jnp.where(end, pltpu.roll(columns, lanes - 17 - z, 1), fluid))
    results = section(centre, sides, None, fluids)
    for f in range(4):
        for z in range(2):
            for k, row in ((0, 0), (1, rows - 1)):
                rim_ref[k, 2 * f + z : 2 * f + z + 1, :] = fields_ref[f, z, row : row + 1, :]
    rims = [rim_ref[k] for k in range(2)]
    values = [jnp.concatenate([p.astype(BF16) for p in parts], axis=1) for parts in results]
    pad = jnp.zeros((128 - 2 * rows, 8 * lanes), BF16)
    stacked = jnp.concatenate(values + [pad], axis=0)
    lines = dot(pick_ref[...], stacked, NT)
    for b in range(blocks):
        rim = jnp.where(b > own, rims[1], rims[0])
        send_ref[b] = jnp.concatenate([lines[8 * b : 8 * b + 8], rim], axis=0).astype(BF16)


def neighbour_terms(lines, rows):
    cells = lines.shape[1]
    lane = iota((8, cells), 1)
    place = lane & 127
    starts = ((place == 0) | (place == rows)) & (lane >= 128)
    stops = ((place == rows - 1) | (place == 2 * rows - 1)) & (lane < cells - 128)
    hop = 128 - rows + 1
    below = jnp.where(starts, pltpu.roll(lines, hop, 1), 0.0)
    above = jnp.where(stops, pltpu.roll(lines, cells - hop, 1), 0.0)
    slope = 0.5 * (above - below)
    first = jnp.where(iota((8, cells), 0) == 0, slope[6:7, :], 0.0)
    terms = VISCOSITY * (above + below) - lines[0:1, :] * slope - first
    return lines[7:8, :] * (TIME_STEP * terms)


def line_kernel(
    scale_dft, loss_scale, recv_ref, table_ref, turned_ref, small_ref, mix_ref, weight_ref, send_ref,
    back_ref, coef_ref,
):
    blocks = recv_ref.shape[0]
    rows = 48
    lines = jnp.concatenate([recv_ref[b, 0:8, :] for b in range(blocks)], axis=1)
    both = table_ref[...]
    cells_by_modes = turned_ref[...]
    lift, proj = small_ref[0:8, :], small_ref[8:16, :]
    lifted = dot(lift, lines, TN).astype(BF16)
    coeffs = jnp.transpose(dot(lifted, cells_by_modes, NN) * scale_dft)
    coeffs16 = coeffs.astype(BF16)
    wide = jnp.concatenate([coeffs16] * 32, axis=1)
    mode_row = iota(wide.shape, 0) & 31
    mode_col = iota(wide.shape, 1) >> 6
    wide = jnp.where(mode_row == mode_col, wide, jnp.zeros_like(wide))
    product = dot(wide, weight_ref[...], NN)
    swapped = pltpu.roll(product, 64, 1)
    parts = []
    for line in range(2):
        real = slice(64 * line, 64 * line + 32)
        imag = slice(64 * line + 32, 64 * line + 64)
        parts.append(product[real] - swapped[imag])
        parts.append(swapped[real] + product[imag])
    mixed = jnp.concatenate(parts, axis=0)
    mixed_t = jnp.transpose(mixed)[0:64].astype(BF16)
    hidden = dot(mixed_t, both, NN) * (2.0 * scale_dft) + dot(mix_ref[...], lifted, TN)
    square = hidden * hidden
    tanh = jnp.tanh(hidden * (GELU_A + (GELU_A * GELU_B) * square))
    half = 0.5 + 0.5 * tanh
    active = (hidden * half).astype(BF16)
    rise = 0.5 * GELU_A + (1.5 * GELU_A * GELU_B) * square
    slope = half + hidden * (1.0 - tanh * tanh) * rise
    predicted = dot(proj, active, NN)
    wide_lines = lines.astype(F32)
    target = pltpu.roll(wide_lines, 5, 0) + neighbour_terms(wide_lines, rows)
    misfit = (predicted - target) * loss_scale
    misfit = jnp.where(iota(misfit.shape, 0) < 3, misfit, 0.0)
    high = misfit.astype(BF16).astype(F32)
    parts = jnp.concatenate([high, misfit - high], axis=0).astype(BF16)
    twice = jnp.concatenate([proj.astype(F32)] * 2, axis=0).astype(BF16)
    back16 = (slope * dot(twice, parts, TN)).astype(BF16)
    mix_terms = jnp.transpose(dot(back16, lines, NT))
    back_mixed = jnp.transpose(dot(back16, cells_by_modes, NN)) * (2.0 * scale_dft)
    back_ref[...] = jnp.concatenate([back_mixed[0:64], back_mixed[64:128]], axis=1)
    coef_ref[...] = jnp.concatenate([coeffs[0:64], coeffs[64:128]], axis=1)
    mix_high = mix_terms.astype(BF16)
    mix_low = (mix_terms - mix_high.astype(F32)).astype(BF16)
    tail = jnp.concatenate([mix_high, mix_low], axis=1).astype(F32)[0:4]
    lane = iota((4, 128), 1) & 63
    for j in range(8):
        back_j = back_ref[pl.ds(j, 8, stride=8), :]
        coef_j = coef_ref[pl.ds(j, 8, stride=8), :]
        real, imag = coef_j[0:4], coef_j[4:8]
        halves = (
            jnp.where(lane < 32, real, pltpu.roll(imag, 32, 1)),
            jnp.where(lane < 32, pltpu.roll(real, 96, 1), imag),
        )
        for k, half in enumerate(halves):
            chunk = jnp.concatenate([back_j, half, tail], axis=0).astype(BF16)
            send_ref[4 * j + 2 * k] = chunk
            send_ref[4 * j + 2 * k + 1] = chunk


def grad_kernel(recv_ref, last_ref, send_ref, wide_ref, grad_ref):
    side = lax.rem(lax.axis_index("gx"), 2)
    blocks, height = recv_ref.shape[:2]
    for b in range(blocks):
        wide_ref[b * height : (b + 1) * height, :] = recv_ref[b].astype(F32)

    def rows(k):
        return wide_ref[pl.ds(k, blocks, stride=height), :]

    lane = iota((32, 128), 1)
    for g in range(4):
        coef = rows(8 + g).astype(BF16)
        by_real = dot(coef, rows(g).astype(BF16), TN)
        by_imag = dot(coef, rows(4 + g).astype(BF16), TN)
        real = [by_real[k : k + 32] + by_imag[k + 32 : k + 64] for k in (0, 64)]
        imag = [by_imag[k : k + 32] - by_real[k + 32 : k + 64] for k in (0, 64)]
        low = real[0] + pltpu.roll(real[1], 64, 1)
        high = pltpu.roll(imag[0], 64, 1) + imag[1]
        grad_ref[g] = jnp.where(lane < 64, low, high)
    mix = []
    for i in range(3):
        total = jnp.sum(rows(12 + i), axis=0, keepdims=True)
        mix.append(total + pltpu.roll(total, 64, 1))
    for g in range(4):
        own = grad_ref[g, pl.ds(side * 16, 16), :]
        for c in range(4):
            k = 4 * g + c
            send_ref[k, 0:4, :] = own[4 * c : 4 * c + 4]
            for i in range(3):
                send_ref[k, 4 + i : 5 + i, :] = mix[i]
            send_ref[k, 7:8, :] = last_ref[0:1, :]


def final_kernel(
    recv_ref, small_ref, fields_ref, solid_ref, edge_ref, lines_ref, grad_ref, mix_ref, new_ref
):
    rows, lanes = fields_ref.shape[2:]
    lane = iota((rows, lanes), 1)
    last = lines_ref.shape[0] - 1
    own = lax.axis_index("gx")
    rims = []
    for index, inside in ((own - 1, own > 0), (own + 1, own < last)):
        message = lines_ref[jnp.minimum(jnp.maximum(index, 0), last)].astype(F32)
        rims.append(jnp.where(inside, message[8:16], 0.0))
    place, count = lax.axis_index("gy"), lax.axis_size("gy")
    stack = []
    for f in range(4):
        below = recv_ref[f * count + jnp.maximum(place - 1, 0)][7:8, :]
        stack += [below, pltpu.roll(below, 64, 1)]
    lower = jnp.where(place > 0, turned(jnp.concatenate(stack, axis=0))[0:rows], 0.0)
    upper = jnp.where(place < count - 1, unfolded(edge_ref[...], rows), 0.0)
    centre, sides = [], []
    for f in range(4):
        centre.append([fields_ref[f, z] for z in range(2)])
        sides.append([])
        for z in range(2):
            at = 2 * f + z
            tile = centre[f][z]
            edge = pltpu.roll(upper, lanes - 1 - 2 * at, 1)
            y_up = jnp.where(lane == lanes - 1, edge, pltpu.roll(tile, lanes - 1, 1))
            edge = pltpu.roll(lower, lanes - at, 1) if at else lower
            y_down = jnp.where(lane == 0, edge, pltpu.roll(tile, 1, 1))
            sides[f].append((y_up, y_down))
    fluids = [1.0 - solid_ref[z].astype(F32) for z in range(2)]
    results = section(centre, sides, rims, fluids)
    for z in range(2):
        for f in range(3):
            new_ref[f, z] = results[z][3 + f]
    total = recv_ref[0]
    for k in range(1, recv_ref.shape[0]):
        total = total + recv_ref[k]
    grad_ref[...] = total[0:4]
    mix = lax.dot_general(
        small_ref[0:8, :].astype(F32),
        pltpu.roll(total, 4, 0),
        TN,
        precision=lax.Precision.HIGHEST,
        preferred_element_type=F32,
    )
    mix_ref[...] = mix[:, 0:64]


def table_kernel(blocks, mode_ref, tile_ref, table_ref, turned_ref, last_ref, pick_ref):
    rows, lanes = tile_ref.shape[1:]
    ends = [as_row(tile_ref[z, :, lanes - 1 : lanes], (rows, lanes)) for z in range(2)]
    last_ref[...] = jnp.broadcast_to(ends[0] + pltpu.roll(ends[1], 64, 1), last_ref.shape)
    wanted = iota(pick_ref.shape, 0)
    wanted = (wanted & 7) * lanes + (wanted >> 3) + lax.axis_index("grp") * blocks
    pick_ref[...] = jnp.where(iota(pick_ref.shape, 1) == wanted, 1.0, 0.0).astype(BF16)
    modes = mode_ref.shape[1]
    unit = 2.0 * math.pi / (blocks * rows)
    square = (modes, modes)
    index = jnp.where(iota(square, 0) == iota(square, 1), mode_ref[...].astype(F32), 0.0)
    index = jnp.sum(index, axis=1, keepdims=True).astype(jnp.int32)
    lane = iota((modes, 128), 1)
    outer = unit * (((index * lane) & (blocks - 1)) * rows).astype(F32)
    cell = jnp.where(lane >= rows, lane - rows, lane)
    inner = unit * (index * jnp.where(lane < 2 * rows, cell, 0)).astype(F32)
    outer_cos, outer_sin = jnp.cos(outer), jnp.sin(outer)
    inner_cos, inner_sin = jnp.cos(inner), jnp.sin(inner)
    by_cos = jnp.concatenate([outer_cos, -outer_sin] * 2, axis=0)
    by_sin = jnp.concatenate([-outer_sin, -outer_cos] * 2, axis=0)
    low = iota((128, 128), 0) < 2 * modes
    lane = iota((128, 128), 1)
    start = jnp.where(low, 0, rows)
    valid = (lane >= start) & (lane < start + rows)
    inner_cos = jnp.where(valid, jnp.concatenate([inner_cos] * 4, axis=0), 0.0)
    inner_sin = jnp.where(valid, jnp.concatenate([inner_sin] * 4, axis=0), 0.0)
    for b in range(blocks):
        block = by_cos[:, b : b + 1] * inner_cos + by_sin[:, b : b + 1] * inner_sin
        table_ref[:, b * 128 : (b + 1) * 128] = block.astype(BF16)
    by_cos, by_sin = jnp.transpose(by_cos), jnp.transpose(by_sin)
    inner_cos, inner_sin = jnp.transpose(inner_cos), jnp.transpose(inner_sin)
    for b in range(blocks):
        block = by_cos[b : b + 1, :] * inner_cos + by_sin[b : b + 1, :] * inner_sin
        turned_ref[b * 128 : (b + 1) * 128, :] = block.astype(BF16)


def local(slot_field, solid, lift_weight, spectral_weight, mix_weight, project_weight, mode_index):
    tile = slot_field[0]
    planes, rows, lanes = tile.shape
    blocks = lax.axis_size("gx")
    x_length = rows * blocks
    cell_total = x_length * lanes * lax.axis_size("gy") * planes
    loss_scale = 16.0 / math.sqrt(cell_total)
    scale_dft = 1.0 / math.sqrt(x_length)
    none = jnp.zeros((5, lift_weight.shape[1]), BF16)
    small = jnp.concatenate([lift_weight, none, project_weight.T, none], axis=0)

    fields = lax.all_gather(slot_field, "grp", axis=0, tiled=True)
    edge = call(edge_kernel, jax.ShapeDtypeStruct((8, lanes), F32), fields, solid)
    groups, count = lax.axis_size("grp"), lax.axis_size("gy")
    pairs = []
    for g in range(groups):
        pairs += [(g * count + i + 1, g * count + i) for i in range(count - 1)]
        pairs.append(((g + groups // 2) % groups * count, g * count + count - 1))
    edge = lax.ppermute(edge, ("grp", "gy"), pairs)
    table, cells_by_modes, last, pick = call(
        lambda *refs: table_kernel(blocks, *refs),
        [
            jax.ShapeDtypeStruct((128, blocks * 128), BF16),
            jax.ShapeDtypeStruct((blocks * 128, 128), BF16),
            jax.ShapeDtypeStruct((8, lanes), F32),
            jax.ShapeDtypeStruct((blocks * 8, 8 * lanes), BF16),
        ],
        mode_index.reshape(1, -1),
        tile,
    )
    edge, table, cells_by_modes, last, small, pick = lax.optimization_barrier(
        (edge, table, cells_by_modes, last, small, pick)
    )
    send = call(
        source_kernel,
        jax.ShapeDtypeStruct((blocks, 16, 128), BF16),
        fields,
        solid,
        edge,
        pick,
        scratch=[pltpu.VMEM((2, 8, lanes), F32)],
    )
    recv = lines = lax.all_to_all(send, "gx", split_axis=0, concat_axis=0, tiled=True)
    send = call(
        lambda *refs: line_kernel(scale_dft, loss_scale, *refs),
        jax.ShapeDtypeStruct((blocks, 16, 128), BF16),
        recv,
        table,
        cells_by_modes,
        small,
        mix_weight,
        spectral_weight,
        scratch=[pltpu.VMEM((64, 128), F32), pltpu.VMEM((64, 128), F32)],
    )
    recv = lax.all_to_all(send, "gx", split_axis=0, concat_axis=0, tiled=True)
    send = call(
        grad_kernel,
        jax.ShapeDtypeStruct((16, 8, 128), F32),
        recv,
        last,
        scratch=[pltpu.VMEM((blocks * 16, 128), F32), pltpu.VMEM((4, 32, 128), F32)],
    )
    recv = lax.all_to_all(send, ("grp", "gy"), split_axis=0, concat_axis=0, tiled=True)
    spectral_grad, mix_grad, new_velocity = call(
        final_kernel,
        [
            jax.ShapeDtypeStruct((4, 128), F32),
            jax.ShapeDtypeStruct((64, 64), F32),
            jax.ShapeDtypeStruct((3, planes, rows, lanes), F32),
        ],
        recv,
        small,
        fields,
        solid,
        edge,
        lines,
    )
    return new_velocity, spectral_grad, mix_grad


def solution(mesh):
    in_specs = (P("grp", None, "gx", "gy"), P(None, "gx", "gy"), P(), P(), P(), P(), P())
    out_specs = (P(None, None, "gx", "gy"), P(("grp", "gx", "gy"), None), P())
    return jax.shard_map(local, mesh=mesh, in_specs=in_specs, out_specs=out_specs, check_vma=False)
```

```python
import math

import jax
import jax.numpy as jnp
from jax import lax
from jax.experimental import pallas as pl
from jax.experimental.pallas import tpu as pltpu
from jax.sharding import PartitionSpec as P

VISCOSITY = 0.05
TIME_STEP = 0.1
F32 = jnp.float32
BF16 = jnp.bfloat16
GELU_A = math.sqrt(2.0 / math.pi)
GELU_B = 0.044715
VMEM = pl.BlockSpec(memory_space=pltpu.VMEM)
NT = (((1,), (1,)), ((), ()))
NN = (((1,), (0,)), ((), ()))
TN = (((0,), (0,)), ((), ()))


def dot(a, b, dims):
    return lax.dot_general(a, b, dims, preferred_element_type=F32)


def iota(shape, axis):
    return lax.broadcasted_iota(jnp.int32, shape, axis)


def call(kernel, out_shape, *args, scratch=()):
    count = len(out_shape) if isinstance(out_shape, (tuple, list)) else 1
    return pl.pallas_call(
        kernel,
        out_shape=out_shape,
        in_specs=[VMEM] * len(args),
        out_specs=[VMEM] * count if isinstance(out_shape, (tuple, list)) else VMEM,
        scratch_shapes=list(scratch),
        compiler_params=pltpu.CompilerParams(vmem_limit_bytes=40 * 1024 * 1024),
    )(*args)


def as_row(column, shape):
    same = iota(shape, 0) == iota(shape, 1)
    return jnp.sum(jnp.where(same, jnp.broadcast_to(column, shape), 0.0), axis=0, keepdims=True)


def turned(rows):
    pad = jnp.zeros((128 - rows.shape[0], 128), F32)
    return jnp.transpose(jnp.concatenate([rows, pad], axis=0))


def edge_kernel(fields_ref, solid_ref, edge_ref):
    rows, lanes = fields_ref.shape[2:]
    lane = iota((rows, lanes), 1)
    edge = jnp.zeros((rows, lanes), F32)
    for f in range(4):
        for z in range(2):
            place = 2 * (2 * f + z)
            tile = fields_ref[f, z]
            tile = pltpu.roll(tile, place, 1) if place else tile
            edge = jnp.where((lane >> 1) == 2 * f + z, tile, edge)
    for z in range(2):
        fluid = pltpu.roll(1.0 - solid_ref[z].astype(F32), 16 + z, 1)
        edge = jnp.where(lane == 16 + z, fluid, edge)
    folded = edge[0:8]
    for k in range(1, rows // 8):
        folded = folded + pltpu.roll(edge[8 * k : 8 * k + 8], 18 * k, 1)
    edge_ref[...] = folded


def unfolded(folded, rows):
    parts = [pltpu.roll(folded, 128 - 18 * k, 1) if k else folded for k in range(rows // 8)]
    return jnp.concatenate(parts, axis=0)


def section(centre, sides, rims, fluids):
    rows, lanes = centre[0][0].shape
    row = iota((rows, lanes), 0)

    def near(f, z):
        tile = centre[f][z]
        below = above = 0.0
        if rims is not None:
            below, above = (rim[2 * f + z : 2 * f + z + 1, :] for rim in rims)
        x_down = jnp.where(row == 0, below, pltpu.roll(tile, 1, 0))
        x_up = jnp.where(row == rows - 1, above, pltpu.roll(tile, rows - 1, 0))
        y_up, y_down = sides[f][z]
        return x_up, x_down, y_up, y_down

    results = []
    for z in range(2):
        velocity = [centre[f][z] for f in range(3)]
        sign = 0.5 if z == 0 else -0.5
        px_up, px_down, py_up, py_down = near(3, z)
        press = (0.5 * (px_up - px_down), 0.5 * (py_up - py_down), sign * centre[3][1 - z])
        new = []
        for f in range(3):
            x_up, x_down, y_up, y_down = near(f, z)
            other = centre[f][1 - z]
            advect = (
                velocity[0] * (0.5 * (x_up - x_down))
                + velocity[1] * (0.5 * (y_up - y_down))
                + velocity[2] * (sign * other)
            )
            lap = other + x_up + x_down + y_up + y_down - 6.0 * velocity[f]
            update = velocity[f] + TIME_STEP * (VISCOSITY * lap - advect - press[f])
            new.append(update * fluids[z])
        results.append(velocity + new + [centre[3][z], fluids[z]])
    return results


def source_kernel(fields_ref, solid_ref, edge_ref, pick_ref, send_ref, rim_ref):
    blocks = send_ref.shape[0]
    rows, lanes = fields_ref.shape[2:]
    lane = iota((rows, lanes), 1)
    end = lane == lanes - 1
    own = lax.axis_index("gx")
    last = lax.axis_index("gy") == lax.axis_size("gy") - 1
    columns = unfolded(edge_ref[...], rows)
    centre, sides = [], []
    for f in range(4):
        centre.append([])
        sides.append([])
        for z in range(2):
            tile = fields_ref[f, z]
            place = 2 * (2 * f + z)
            one = pltpu.roll(columns, lanes - 1 - place, 1)
            two = pltpu.roll(columns, lanes - 2 - place, 1)
            above = jnp.where(lane >= lanes - 2, two, pltpu.roll(tile, lanes - 2, 1))
            above = jnp.where((lane == lanes - 2) & last, 0.0, above)
            centre[f].append(jnp.where(end, one, pltpu.roll(tile, lanes - 1, 1)))
            sides[f].append((above, jnp.where(end & last, 0.0, tile)))
    fluids = []
    for z in range(2):
        fluid = pltpu.roll(1.0 - solid_ref[z].astype(F32), lanes - 1, 1)
        fluids.append(jnp.where(end, pltpu.roll(columns, lanes - 17 - z, 1), fluid))
    results = section(centre, sides, None, fluids)
    for f in range(4):
        for z in range(2):
            for k, row in ((0, 0), (1, rows - 1)):
                rim_ref[k, 2 * f + z : 2 * f + z + 1, :] = fields_ref[f, z, row : row + 1, :]
    rims = [rim_ref[k] for k in range(2)]
    values = [jnp.concatenate([p.astype(BF16) for p in parts], axis=1) for parts in results]
    pad = jnp.zeros((128 - 2 * rows, 8 * lanes), BF16)
    stacked = jnp.concatenate(values + [pad], axis=0)
    lines = dot(pick_ref[...], stacked, NT)
    for b in range(blocks):
        rim = jnp.where(b > own, rims[1], rims[0])
        send_ref[b] = jnp.concatenate([lines[8 * b : 8 * b + 8], rim], axis=0).astype(BF16)


def neighbour_terms(lines, rows):
    cells = lines.shape[1]
    lane = iota((8, cells), 1)
    place = lane & 127
    starts = ((place == 0) | (place == rows)) & (lane >= 128)
    stops = ((place == rows - 1) | (place == 2 * rows - 1)) & (lane < cells - 128)
    hop = 128 - rows + 1
    below = jnp.where(starts, pltpu.roll(lines, hop, 1), 0.0)
    above = jnp.where(stops, pltpu.roll(lines, cells - hop, 1), 0.0)
    slope = 0.5 * (above - below)
    first = jnp.where(iota((8, cells), 0) == 0, slope[6:7, :], 0.0)
    terms = VISCOSITY * (above + below) - lines[0:1, :] * slope - first
    return lines[7:8, :] * (TIME_STEP * terms)


def line_kernel(
    scale_dft, loss_scale, recv_ref, table_ref, turned_ref, small_ref, mix_ref, weight_ref, send_ref,
    back_ref, coef_ref,
):
    blocks = recv_ref.shape[0]
    rows = 48
    lines = jnp.concatenate([recv_ref[b, 0:8, :] for b in range(blocks)], axis=1)
    both = table_ref[...]
    cells_by_modes = turned_ref[...]
    lift, proj = small_ref[0:8, :], small_ref[8:16, :]
    lifted = dot(lift, lines, TN).astype(BF16)
    coeffs = jnp.transpose(dot(lifted, cells_by_modes, NN) * scale_dft)
    coeffs16 = coeffs.astype(BF16)
    wide = jnp.concatenate([coeffs16] * 32, axis=1)
    mode_row = iota(wide.shape, 0) & 31
    mode_col = iota(wide.shape, 1) >> 6
    wide = jnp.where(mode_row == mode_col, wide, jnp.zeros_like(wide))
    product = dot(wide, weight_ref[...], NN)
    swapped = pltpu.roll(product, 64, 1)
    parts = []
    for line in range(2):
        real = slice(64 * line, 64 * line + 32)
        imag = slice(64 * line + 32, 64 * line + 64)
        parts.append(product[real] - swapped[imag])
        parts.append(swapped[real] + product[imag])
    mixed = jnp.concatenate(parts, axis=0)
    mixed_t = jnp.transpose(mixed)[0:64].astype(BF16)
    hidden = dot(mixed_t, both, NN) * (2.0 * scale_dft) + dot(mix_ref[...], lifted, TN)
    square = hidden * hidden
    tanh = jnp.tanh(hidden * (GELU_A + (GELU_A * GELU_B) * square))
    half = 0.5 + 0.5 * tanh
    product = hidden * half
    active = product.astype(BF16)
    rise = 2.0 * GELU_A + (6.0 * GELU_A * GELU_B) * square
    slope = half * (1.0 + (hidden - product) * rise)
    predicted = dot(proj, active, NN)
    wide_lines = lines.astype(F32)
    target = pltpu.roll(wide_lines, 5, 0) + neighbour_terms(wide_lines, rows)
    misfit = (predicted - target) * loss_scale
    misfit = jnp.where(iota(misfit.shape, 0) < 3, misfit, 0.0)
    high = misfit.astype(BF16).astype(F32)
    parts = jnp.concatenate([high, misfit - high], axis=0).astype(BF16)
    twice = jnp.concatenate([proj.astype(F32)] * 2, axis=0).astype(BF16)
    back16 = (slope * dot(twice, parts, TN)).astype(BF16)
    mix_terms = jnp.transpose(dot(back16, lines, NT))
    back_mixed = jnp.transpose(dot(back16, cells_by_modes, NN)) * (2.0 * scale_dft)
    back_ref[...] = jnp.concatenate([back_mixed[0:64], back_mixed[64:128]], axis=1)
    coef_ref[...] = jnp.concatenate([coeffs[0:64], coeffs[64:128]], axis=1)
    mix_high = mix_terms.astype(BF16)
    mix_low = (mix_terms - mix_high.astype(F32)).astype(BF16)
    tail = jnp.concatenate([mix_high, mix_low], axis=1).astype(F32)[0:4]
    lane = iota((4, 128), 1) & 63
    for j in range(8):
        back_j = back_ref[pl.ds(j, 8, stride=8), :]
        coef_j = coef_ref[pl.ds(j, 8, stride=8), :]
        real, imag = coef_j[0:4], coef_j[4:8]
        halves = (
            jnp.where(lane < 32, real, pltpu.roll(imag, 32, 1)),
            jnp.where(lane < 32, pltpu.roll(real, 96, 1), imag),
        )
        for k, half in enumerate(halves):
            chunk = jnp.concatenate([back_j, half, tail], axis=0).astype(BF16)
            send_ref[4 * j + 2 * k] = chunk
            send_ref[4 * j + 2 * k + 1] = chunk


def grad_kernel(recv_ref, last_ref, send_ref, wide_ref, grad_ref):
    side = lax.rem(lax.axis_index("gx"), 2)
    blocks, height = recv_ref.shape[:2]
    for b in range(blocks):
        wide_ref[b * height : (b + 1) * height, :] = recv_ref[b].astype(F32)

    def rows(k):
        return wide_ref[pl.ds(k, blocks, stride=height), :]

    lane = iota((32, 128), 1)
    for g in range(4):
        coef = rows(8 + g).astype(BF16)
        by_real = dot(coef, rows(g).astype(BF16), TN)
        by_imag = dot(coef, rows(4 + g).astype(BF16), TN)
        real = [by_real[k : k + 32] + by_imag[k + 32 : k + 64] for k in (0, 64)]
        imag = [by_imag[k : k + 32] - by_real[k + 32 : k + 64] for k in (0, 64)]
        low = real[0] + pltpu.roll(real[1], 64, 1)
        high = pltpu.roll(imag[0], 64, 1) + imag[1]
        grad_ref[g] = jnp.where(lane < 64, low, high)
    mix = []
    for i in range(3):
        total = jnp.sum(rows(12 + i), axis=0, keepdims=True)
        mix.append(total + pltpu.roll(total, 64, 1))
    for g in range(4):
        own = grad_ref[g, pl.ds(side * 16, 16), :]
        for c in range(4):
            k = 4 * g + c
            send_ref[k, 0:4, :] = own[4 * c : 4 * c + 4]
            for i in range(3):
                send_ref[k, 4 + i : 5 + i, :] = mix[i]
            send_ref[k, 7:8, :] = last_ref[0:1, :]


def final_kernel(
    recv_ref, small_ref, fields_ref, solid_ref, edge_ref, lines_ref, grad_ref, mix_ref, new_ref
):
    rows, lanes = fields_ref.shape[2:]
    lane = iota((rows, lanes), 1)
    last = lines_ref.shape[0] - 1
    own = lax.axis_index("gx")
    rims = []
    for index, inside in ((own - 1, own > 0), (own + 1, own < last)):
        message = lines_ref[jnp.minimum(jnp.maximum(index, 0), last)].astype(F32)
        rims.append(jnp.where(inside, message[8:16], 0.0))
    place, count = lax.axis_index("gy"), lax.axis_size("gy")
    stack = []
    for f in range(4):
        below = recv_ref[f * count + jnp.maximum(place - 1, 0)][7:8, :]
        stack += [below, pltpu.roll(below, 64, 1)]
    lower = jnp.where(place > 0, turned(jnp.concatenate(stack, axis=0))[0:rows], 0.0)
    upper = jnp.where(place < count - 1, unfolded(edge_ref[...], rows), 0.0)
    centre, sides = [], []
    for f in range(4):
        centre.append([fields_ref[f, z] for z in range(2)])
        sides.append([])
        for z in range(2):
            at = 2 * f + z
            tile = centre[f][z]
            edge = pltpu.roll(upper, lanes - 1 - 2 * at, 1)
            y_up = jnp.where(lane == lanes - 1, edge, pltpu.roll(tile, lanes - 1, 1))
            edge = pltpu.roll(lower, lanes - at, 1) if at else lower
            y_down = jnp.where(lane == 0, edge, pltpu.roll(tile, 1, 1))
            sides[f].append((y_up, y_down))
    fluids = [1.0 - solid_ref[z].astype(F32) for z in range(2)]
    results = section(centre, sides, rims, fluids)
    for z in range(2):
        for f in range(3):
            new_ref[f, z] = results[z][3 + f]
    total = recv_ref[0]
    for k in range(1, recv_ref.shape[0]):
        total = total + recv_ref[k]
    grad_ref[...] = total[0:4]
    mix = lax.dot_general(
        small_ref[0:8, :].astype(F32),
        pltpu.roll(total, 4, 0),
        TN,
        precision=lax.Precision.HIGHEST,
        preferred_element_type=F32,
    )
    mix_ref[...] = mix[:, 0:64]


def table_kernel(blocks, mode_ref, tile_ref, table_ref, turned_ref, last_ref, pick_ref):
    rows, lanes = tile_ref.shape[1:]
    ends = [as_row(tile_ref[z, :, lanes - 1 : lanes], (rows, lanes)) for z in range(2)]
    last_ref[...] = jnp.broadcast_to(ends[0] + pltpu.roll(ends[1], 64, 1), last_ref.shape)
    wanted = iota(pick_ref.shape, 0)
    wanted = (wanted & 7) * lanes + (wanted >> 3) + lax.axis_index("grp") * blocks
    pick_ref[...] = jnp.where(iota(pick_ref.shape, 1) == wanted, 1.0, 0.0).astype(BF16)
    modes = mode_ref.shape[1]
    unit = 2.0 * math.pi / (blocks * rows)
    square = (modes, modes)
    index = jnp.where(iota(square, 0) == iota(square, 1), mode_ref[...].astype(F32), 0.0)
    index = jnp.sum(index, axis=1, keepdims=True).astype(jnp.int32)
    lane = iota((modes, 128), 1)
    outer = unit * (((index * lane) & (blocks - 1)) * rows).astype(F32)
    cell = jnp.where(lane >= rows, lane - rows, lane)
    inner = unit * (index * jnp.where(lane < 2 * rows, cell, 0)).astype(F32)
    outer_cos, outer_sin = jnp.cos(outer), jnp.sin(outer)
    inner_cos, inner_sin = jnp.cos(inner), jnp.sin(inner)
    by_cos = jnp.concatenate([outer_cos, -outer_sin] * 2, axis=0)
    by_sin = jnp.concatenate([-outer_sin, -outer_cos] * 2, axis=0)
    low = iota((128, 128), 0) < 2 * modes
    lane = iota((128, 128), 1)
    start = jnp.where(low, 0, rows)
    valid = (lane >= start) & (lane < start + rows)
    inner_cos = jnp.where(valid, jnp.concatenate([inner_cos] * 4, axis=0), 0.0)
    inner_sin = jnp.where(valid, jnp.concatenate([inner_sin] * 4, axis=0), 0.0)
    for b in range(blocks):
        block = by_cos[:, b : b + 1] * inner_cos + by_sin[:, b : b + 1] * inner_sin
        table_ref[:, b * 128 : (b + 1) * 128] = block.astype(BF16)
    by_cos, by_sin = jnp.transpose(by_cos), jnp.transpose(by_sin)
    inner_cos, inner_sin = jnp.transpose(inner_cos), jnp.transpose(inner_sin)
    for b in range(blocks):
        block = by_cos[b : b + 1, :] * inner_cos + by_sin[b : b + 1, :] * inner_sin
        turned_ref[b * 128 : (b + 1) * 128, :] = block.astype(BF16)


def local(slot_field, solid, lift_weight, spectral_weight, mix_weight, project_weight, mode_index):
    tile = slot_field[0]
    planes, rows, lanes = tile.shape
    blocks = lax.axis_size("gx")
    x_length = rows * blocks
    cell_total = x_length * lanes * lax.axis_size("gy") * planes
    loss_scale = 16.0 / math.sqrt(cell_total)
    scale_dft = 1.0 / math.sqrt(x_length)
    none = jnp.zeros((5, lift_weight.shape[1]), BF16)
    small = jnp.concatenate([lift_weight, none, project_weight.T, none], axis=0)

    fields = lax.all_gather(slot_field, "grp", axis=0, tiled=True)
    edge = call(edge_kernel, jax.ShapeDtypeStruct((8, lanes), F32), fields, solid)
    groups, count = lax.axis_size("grp"), lax.axis_size("gy")
    pairs = []
    for g in range(groups):
        pairs += [(g * count + i + 1, g * count + i) for i in range(count - 1)]
        pairs.append(((g + groups // 2) % groups * count, g * count + count - 1))
    edge = lax.ppermute(edge, ("grp", "gy"), pairs)
    table, cells_by_modes, last, pick = call(
        lambda *refs: table_kernel(blocks, *refs),
        [
            jax.ShapeDtypeStruct((128, blocks * 128), BF16),
            jax.ShapeDtypeStruct((blocks * 128, 128), BF16),
            jax.ShapeDtypeStruct((8, lanes), F32),
            jax.ShapeDtypeStruct((blocks * 8, 8 * lanes), BF16),
        ],
        mode_index.reshape(1, -1),
        tile,
    )
    edge, table, cells_by_modes, last, small, pick = lax.optimization_barrier(
        (edge, table, cells_by_modes, last, small, pick)
    )
    send = call(
        source_kernel,
        jax.ShapeDtypeStruct((blocks, 16, 128), BF16),
        fields,
        solid,
        edge,
        pick,
        scratch=[pltpu.VMEM((2, 8, lanes), F32)],
    )
    recv = lines = lax.all_to_all(send, "gx", split_axis=0, concat_axis=0, tiled=True)
    send = call(
        lambda *refs: line_kernel(scale_dft, loss_scale, *refs),
        jax.ShapeDtypeStruct((blocks, 16, 128), BF16),
        recv,
        table,
        cells_by_modes,
        small,
        mix_weight,
        spectral_weight,
        scratch=[pltpu.VMEM((64, 128), F32), pltpu.VMEM((64, 128), F32)],
    )
    recv = lax.all_to_all(send, "gx", split_axis=0, concat_axis=0, tiled=True)
    send = call(
        grad_kernel,
        jax.ShapeDtypeStruct((16, 8, 128), F32),
        recv,
        last,
        scratch=[pltpu.VMEM((blocks * 16, 128), F32), pltpu.VMEM((4, 32, 128), F32)],
    )
    recv = lax.all_to_all(send, ("grp", "gy"), split_axis=0, concat_axis=0, tiled=True)
    spectral_grad, mix_grad, new_velocity = call(
        final_kernel,
        [
            jax.ShapeDtypeStruct((4, 128), F32),
            jax.ShapeDtypeStruct((64, 64), F32),
            jax.ShapeDtypeStruct((3, planes, rows, lanes), F32),
        ],
        recv,
        small,
        fields,
        solid,
        edge,
        lines,
    )
    return new_velocity, spectral_grad, mix_grad


def solution(mesh):
    in_specs = (P("grp", None, "gx", "gy"), P(None, "gx", "gy"), P(), P(), P(), P(), P())
    out_specs = (P(None, None, "gx", "gy"), P(("grp", "gx", "gy"), None), P())
    return jax.shard_map(local, mesh=mesh, in_specs=in_specs, out_specs=out_specs, check_vma=False)
```
